32 devices in a mesh: group: 1, row: 32 (over z, y, x, core).
Axes of the slice: x: 2, y: 2, z: 4, core: 2. Of those that a mesh axis runs over, the one named last changes fastest.
Arguments:
- alignment_tensor: bfloat16 [64, 512, 256], P(('group', 'row')), may hold values from -6 to 6
- pairwise_tensor: bfloat16 [512, 512, 128], P('group', 'row'), may hold values from -6 to 6
- standardize_factor: float32 [256], replicated, may hold values from 0.1 to 1.9
- standardize_shift: float32 [256], replicated, may hold values from -3 to 3
- first_matrix: bfloat16 [256, 32], replicated, may hold values from -0.375 to 0.375
- first_shift: float32 [32], replicated, may hold values from -3 to 3
- second_matrix: bfloat16 [256, 32], replicated, may hold values from -0.375 to 0.375
- second_shift: float32 [32], replicated, may hold values from -3 to 3
- final_matrix: bfloat16 [1024, 128], replicated, may hold values from -3 to 3
- final_shift: float32 [128], replicated, may hold values from -3 to 3
Outputs:
- pair_out: bfloat16 [512, 512, 128], P('group', 'row')
The draws below stay inside these ranges and needn't reach their ends.
All inputs are finite; a program needn't handle non-finite values.
Results may differ from the reference program's by a relative error of at most 0.0061.
Values may be sent and summed in bfloat16 or wider, within the bound.
No kernel may reach another device: no remote copies, remote signals or barrier semaphores. Data moves between devices by JAX's collectives and lax.ppermute only.
A program may use at most 192 MiB of HBM per device.

```python
import jax
import jax.numpy as jnp
from jax import lax

ALIGN_FEATURES = 256
HIDDEN_WIDTH = 32
C_Z = 128
COLS_DEV = 16
BAND = 512
ALIGNED_CHAINS = 64
CHAIN_POSITIONS = 512


def levels(rng, dims, pieces, smallest, largest):
    def one(position, parts):
        steps = jax.random.uniform(jax.random.fold_in(jax.random.fold_in(rng, 6), position), (parts,), jnp.float32, smallest / len(pieces), largest / len(pieces))
        return jnp.repeat(jnp.exp(steps), dims[position] // parts).reshape((-1,) + (1,) * (len(dims) - position - 1))

    level = one(*pieces[0])
    for cut in pieces[1:]:
        level = level * one(*cut)
    return level


def scatter_about(stream_key, shape, scale, most, pieces=(), held_as=jnp.bfloat16):
    values = scale * jax.random.normal(stream_key, shape, jnp.float32)
    if pieces:
        values = values * levels(stream_key, shape, pieces, -0.22, 0.18)
    return jnp.clip(values, -most, most).astype(held_as)


def setup_inputs(seed: int = 0, part: int = 0) -> dict:
    keys = jax.random.split(jax.random.key(seed), 11)
    part_splits = jax.random.split(jax.random.fold_in(keys[10], part), 11)
    alignment_tensor = scatter_about(part_splits[0], (ALIGNED_CHAINS, CHAIN_POSITIONS, ALIGN_FEATURES), 1.0, 6.0, ((0, 32),))
    pairwise_tensor = scatter_about(part_splits[1], (BAND, CHAIN_POSITIONS, C_Z), 1.0, 6.0, ((1, 32),))
    standardize_factor = jnp.clip(1.0 + 0.18 * jax.random.normal(keys[2], (ALIGN_FEATURES,), jnp.float32), 0.1, 1.9)
    standardize_shift = scatter_about(keys[3], (ALIGN_FEATURES,), 0.3, 3.0, (), jnp.float32)
    first_matrix = scatter_about(keys[4], (ALIGN_FEATURES, HIDDEN_WIDTH), ALIGN_FEATURES ** -0.5, 0.375)
    first_shift = scatter_about(keys[5], (HIDDEN_WIDTH,), 0.3, 3.0, (), jnp.float32)
    second_matrix = scatter_about(keys[6], (ALIGN_FEATURES, HIDDEN_WIDTH), ALIGN_FEATURES ** -0.5, 0.375)
    second_shift = scatter_about(keys[7], (HIDDEN_WIDTH,), 0.3, 3.0, (), jnp.float32)
    final_matrix = scatter_about(keys[8], (HIDDEN_WIDTH * HIDDEN_WIDTH, C_Z), 0.5, 3.0)
    final_shift = scatter_about(keys[9], (C_Z,), 0.5, 3.0, (), jnp.float32)
    return {"alignment_tensor": alignment_tensor, "pairwise_tensor": pairwise_tensor, "standardize_factor": standardize_factor, "standardize_shift": standardize_shift, "first_matrix": first_matrix, "first_shift": first_shift, "second_matrix": second_matrix, "second_shift": second_shift, "final_matrix": final_matrix, "final_shift": final_shift}


def standardized_lines(alignment_tensor, standardize_factor, standardize_shift):
    element_amounts = alignment_tensor.astype(jnp.float32)
    center = lax.optimization_barrier(jnp.mean(element_amounts, axis=-1, keepdims=True))
    spread = lax.optimization_barrier(jnp.mean((element_amounts - center) ** 2, axis=-1, keepdims=True))
    return ((element_amounts - center) * lax.rsqrt(spread + 1e-05) * standardize_factor + standardize_shift).astype(jnp.bfloat16)

def mapped_features(standardized_alignment, coefficient_matrix, offset_vector):
    summed_contribution = jnp.einsum('bkq,qy->bky', standardized_alignment.astype(jnp.float32), coefficient_matrix.astype(jnp.float32))
    return (summed_contribution + offset_vector).astype(jnp.bfloat16)

def block_update(left_block, right_block, pair_block, final_matrix, final_shift, count):
    rows = pair_block.shape[0]
    cols = pair_block.shape[1]
    chans = left_block.shape[1] // rows
    product = lax.dot_general(left_block, right_block, (((0,), (0,)), ((), ())), preferred_element_type=jnp.float32)
    outer = (product / count).astype(jnp.bfloat16)
    outer = outer.reshape(rows, chans, cols, chans).transpose(0, 2, 1, 3).reshape(rows * cols, chans * chans)
    update = jnp.dot(outer, final_matrix, preferred_element_type=jnp.float32) + final_shift
    return (pair_block.astype(jnp.float32) + update.reshape(rows, cols, -1)).astype(jnp.bfloat16)

def reference(alignment_tensor, pairwise_tensor, standardize_factor, standardize_shift, first_matrix, first_shift, second_matrix, second_shift, final_matrix, final_shift):
    standardized_alignment = standardized_lines(alignment_tensor, standardize_factor, standardize_shift)
    first_factor = mapped_features(standardized_alignment, first_matrix, first_shift)
    second_factor = mapped_features(standardized_alignment, second_matrix, second_shift)
    seqs = first_factor.shape[0]
    chans = first_factor.shape[2]
    residues = second_factor.shape[1]
    row_block = COLS_DEV
    col_block = COLS_DEV * 8
    row_count = BAND // row_block
    col_count = residues // col_block
    left_blocks = first_factor[:, :BAND].reshape(seqs, row_count, row_block * chans).transpose(1, 0, 2)
    right_blocks = second_factor.reshape(seqs, col_count, col_block * chans).transpose(1, 0, 2)
    pair_blocks = pairwise_tensor.reshape(row_count, row_block, col_count, col_block, -1).transpose(0, 2, 1, 3, 4)
    count = jnp.float32(seqs)

    def row_step(items):
        left_block, pair_row = items

        def col_step(inner):
            right_block, pair_block = inner
            return block_update(left_block, right_block, pair_block, final_matrix, final_shift, count)
        return lax.map(col_step, (right_blocks, pair_row))
    result = lax.map(row_step, (left_blocks, pair_blocks))
    return result.transpose(0, 2, 1, 3, 4).reshape(BAND, residues, -1)
```

```python
import functools

import jax
import jax.numpy as jnp
from jax import lax
from jax.experimental import pallas as pl
from jax.experimental.pallas import tpu as pltpu
from jax.sharding import PartitionSpec as P

LANES = 128


def _stacked(weights, copies):
    q, c = weights.shape
    rows = []
    for k in range(copies):
        left = [jnp.zeros((q, k * c), weights.dtype)] if k else []
        right = [jnp.zeros((q, (copies - 1 - k) * c), weights.dtype)] if k < copies - 1 else []
        rows.append(jnp.concatenate(left + [weights] + right, axis=1))
    return jnp.concatenate(rows, axis=0)


def _project_kernel(x_ref, gain_ref, bias_ref, w1_ref, b1_ref, w2_ref, b2_ref, left_ref, right_ref):
    band_half = left_ref.shape[0]
    n = right_ref.shape[0]
    feats = x_ref.shape[2]
    odd = lax.axis_index("row") % 2
    normed = []
    for s in range(2):
        x = x_ref[s].astype(jnp.float32)
        center = jnp.mean(x, axis=-1, keepdims=True)
        off = x - center
        spread = jnp.mean(off * off, axis=-1, keepdims=True)
        normed.append(off * lax.rsqrt(spread + 1e-05) * gain_ref[...] + bias_ref[...])
    low = [v[:band_half].astype(jnp.bfloat16) for v in normed]
    high = [v[band_half : 2 * band_half].astype(jnp.bfloat16) for v in normed]
    stack1 = _stacked(w1_ref[...], 4)
    shift1 = jnp.concatenate([b1_ref[...]] * 4, axis=1)
    left = jnp.dot(jnp.concatenate(low + high, axis=1), stack1, preferred_element_type=jnp.float32) + shift1
    swapped = pltpu.roll(left, 64, 1)
    left_ref[...] = jnp.where(odd == 1, swapped, left).astype(jnp.bfloat16)

    split = [v.reshape(n, 2, 8, feats) for v in normed]
    parts = [split[s][:, jh].reshape(n * 8, feats).astype(jnp.bfloat16) for jh in range(2) for s in range(2)]
    stack2 = _stacked(w2_ref[...], 4)
    shift2 = jnp.concatenate([b2_ref[...]] * 4, axis=1)
    right = jnp.dot(jnp.concatenate(parts, axis=1), stack2, preferred_element_type=jnp.float32) + shift2
    right_ref[...] = right.reshape(n, 8, LANES).astype(jnp.bfloat16)


def _fold_kernel(right_ref, final_ref, out_ref, scratch):
    d = right_ref.shape[0]
    chans = 32
    block = right_ref[...].astype(jnp.float32).reshape(d * 8, LANES)
    lane = lax.broadcasted_iota(jnp.int32, block.shape, 1) // chans
    lhs = jnp.concatenate([jnp.where(lane == q, block, 0.0) for q in range(4)], axis=0).astype(jnp.bfloat16)
    for c in range(0, chans, 2):
        pair = []
        for k in range(2):
            w = final_ref[pl.ds((c + k) * chans, chans), :]
            pair.append(jnp.concatenate([w] * 4, axis=0))
        rhs = jnp.concatenate(pair, axis=1)
        res = jnp.dot(lhs, rhs, preferred_element_type=jnp.float32)
        for k in range(2):
            scratch[pl.ds(c + k, 4 * d * 8, stride=chans), :] = res[:, k * LANES : (k + 1) * LANES]
    for q in range(4):
        jh, s = q // 2, q % 2
        for dd in range(d):
            for jr in range(8):
                row = ((q * d + dd) * 8 + jr) * chans
                j = jh * 8 + jr
                out_ref[pl.ds((dd * 2 + s) * chans, chans), pl.ds(j * LANES, LANES)] = scratch[
                    pl.ds(row, chans), :
                ].astype(jnp.bfloat16)


def _band_kernel(count, groups, *refs):
    own_refs, other_refs = refs[:groups], refs[groups : 2 * groups]
    t_ref, pair_ref, shift_ref, out_ref, l_ref, acc_ref = refs[2 * groups :]
    step = pl.program_id(0)
    steps = pl.num_programs(0)
    half = own_refs[0].shape[1]
    band, cols = pair_ref.shape[0], pair_ref.shape[1]
    me = lax.axis_index("row")

    @pl.when(step == 0)
    def _():
        lane = lax.broadcasted_iota(jnp.int32, (half, LANES), 1)
        first = (lane // 64) == (me % 2)
        for g in range(groups):
            for zi in range(own_refs[g].shape[0]):
                chip = (zi * groups + g) ^ (me // 2)
                a = own_refs[g][zi].astype(jnp.float32)
                b = other_refs[g][zi].astype(jnp.float32)
                at = pl.ds(pl.multiple_of(chip * LANES, LANES), LANES)
                l_ref[pl.ds(0, half), at] = jnp.where(first, a, b).astype(jnp.bfloat16)
                l_ref[pl.ds(half, half), at] = pltpu.roll(jnp.where(first, b, a), 64, 1).astype(jnp.bfloat16)

    res = jnp.dot(l_ref[...], t_ref[...], preferred_element_type=jnp.float32)
    width = t_ref.shape[1] // LANES
    for k in range(width):
        acc_ref[pl.ds(step * width + k, band, stride=cols), :] = res[:, k * LANES : (k + 1) * LANES]

    @pl.when(step == steps - 1)
    def _():
        shift = shift_ref[...].reshape(1, 1, LANES)
        rows = 32

        def body(r, _):
            at = pl.ds(pl.multiple_of(r * rows, rows), rows)
            flat = pl.ds(pl.multiple_of(r * rows * cols, rows * cols), rows * cols)
            total = acc_ref[flat, :].reshape(rows, cols, LANES) * (1.0 / count) + shift
            out_ref[at] = (pair_ref[at].astype(jnp.float32) + total).astype(jnp.bfloat16)
            return 0

        lax.fori_loop(0, band // rows, body, 0)


def _xor(x, mask, n):
    return lax.ppermute(x, "row", [(i, i ^ mask) for i in range(n)])


def shards(n, alignment, pair, gain, bias, w1, b1, w2, b2, final, shift):
    seqs, residues, feats = alignment.shape
    band, cols, zdim = pair.shape
    chans = w1.shape[1]
    half = band // 2
    count = float(seqs * n)
    vmem = pltpu.CompilerParams(vmem_limit_bytes=48 * 1024 * 1024)

    left, right = pl.pallas_call(
        _project_kernel,
        out_shape=(
            jax.ShapeDtypeStruct((half, LANES), jnp.bfloat16),
            jax.ShapeDtypeStruct((n, 8, LANES), jnp.bfloat16),
        ),
        compiler_params=vmem,
        cost_estimate=pl.CostEstimate(
            flops=4 * seqs * residues * feats * chans, bytes_accessed=2 * seqs * residues * feats, transcendentals=0
        ),
    )(alignment, gain.reshape(1, -1), bias.reshape(1, -1), w1, b1.reshape(1, -1), w2, b2.reshape(1, -1))

    right = lax.all_to_all(right, "row", split_axis=0, concat_axis=0, tiled=True)

    line = [left] + [_xor(left, m, n) for m in range(8, n, 8)]
    line = jnp.stack(line)
    own = [line] + [_xor(line, m, n) for m in (2, 4, 6)]
    other = [_xor(o, 1, n) for o in own]
    groups = 4

    step_d = 4
    folded = pl.pallas_call(
        _fold_kernel,
        grid=(n // step_d,),
        in_specs=[
            pl.BlockSpec((step_d, 8, LANES), lambda i: (i, 0, 0)),
            pl.BlockSpec(final.shape, lambda i: (0, 0)),
        ],
        out_specs=pl.BlockSpec((step_d * 2 * chans, cols * zdim), lambda i: (i, 0)),
        out_shape=jax.ShapeDtypeStruct((n * 2 * chans, cols * zdim), jnp.bfloat16),
        scratch_shapes=[pltpu.VMEM((step_d * 32 * chans, LANES), jnp.float32)],
        compiler_params=vmem,
        cost_estimate=pl.CostEstimate(
            flops=16 * n * 32 * 256 * chans * zdim, bytes_accessed=n * 4 * chans * cols * zdim, transcendentals=0
        ),
    )(right, final)

    k = n * 2 * chans
    tile = 256
    whole = lambda a: pl.BlockSpec(a.shape, lambda i: (0,) * a.ndim)
    return pl.pallas_call(
        functools.partial(_band_kernel, count, groups),
        grid=(cols * zdim // tile,),
        in_specs=[whole(a) for a in own + other]
        + [
            pl.BlockSpec((k, tile), lambda i: (0, i)),
            whole(pair),
            pl.BlockSpec((1, zdim), lambda i: (0, 0)),
        ],
        out_specs=whole(pair),
        out_shape=jax.ShapeDtypeStruct(pair.shape, jnp.bfloat16),
        scratch_shapes=[pltpu.VMEM((band, k), jnp.bfloat16), pltpu.VMEM((band * cols, zdim), jnp.float32)],
        compiler_params=vmem,
        cost_estimate=pl.CostEstimate(
            flops=2 * band * k * cols * zdim, bytes_accessed=2 * k * cols * zdim, transcendentals=0
        ),
    )(*own, *other, folded, pair, shift.reshape(1, -1))


def solution(mesh):
    placed = (P(("group", "row"), None, None), P("group", "row", None)) + (P(),) * 8
    return jax.shard_map(
        functools.partial(shards, mesh.shape["row"]),
        mesh=mesh,
        in_specs=placed,
        out_specs=P("group", "row", None),
        check_vma=False,
    )
```

```python
import functools

import jax
import jax.numpy as jnp
from jax import lax
from jax.experimental import pallas as pl
from jax.experimental.pallas import tpu as pltpu
from jax.sharding import PartitionSpec as P

LANES = 128
CHANS = 32
NT = (((1,), (1,)), ((), ()))


def _stacked(weights, copies):
    c, q = weights.shape
    rows = []
    for k in range(copies):
        left = [jnp.zeros((c, k * q), weights.dtype)] if k else []
        right = [jnp.zeros((c, (copies - 1 - k) * q), weights.dtype)] if k < copies - 1 else []
        rows.append(jnp.concatenate(left + [weights] + right, axis=1))
    return jnp.concatenate(rows, axis=0)


def _project_kernel(*refs):
    sources, (left_ref, right_ref), held = refs[:7], refs[7:9], refs[9:16]
    sems = refs[16]
    copies = [pltpu.make_async_copy(a, b, sems.at[i]) for i, (a, b) in enumerate(zip(sources, held))]
    for copy in copies:
        copy.start()
    for copy in copies:
        copy.wait()
    x_ref, gain_ref, bias_ref, w1_ref, b1_ref, w2_ref, b2_ref = held
    band_half = left_ref.shape[0]
    n = right_ref.shape[0]
    feats = x_ref.shape[2]
    normed = []
    for s in range(2):
        x = x_ref[s].astype(jnp.float32)
        center = jnp.mean(x, axis=-1, keepdims=True)
        off = x - center
        spread = jnp.mean(off * off, axis=-1, keepdims=True)
        normed.append(off * lax.rsqrt(spread + 1e-05) * gain_ref[...] + bias_ref[...])
    low = [v[:band_half].astype(jnp.bfloat16) for v in normed]
    high = [v[band_half : 2 * band_half].astype(jnp.bfloat16) for v in normed]
    shift1 = jnp.concatenate([b1_ref[...]] * 4, axis=1)
    left = lax.dot_general(
        jnp.concatenate(low + high, axis=1), _stacked(w1_ref[...], 4), NT, preferred_element_type=jnp.float32
    )
    left_ref[...] = (left + shift1).astype(jnp.bfloat16)

    split = [v.reshape(n, 2, 8, feats) for v in normed]
    parts = [split[s][:, jh].reshape(n * 8, feats).astype(jnp.bfloat16) for jh in range(2) for s in range(2)]
    shift2 = jnp.concatenate([b2_ref[...]] * 4, axis=1)
    right = lax.dot_general(
        jnp.concatenate(parts, axis=1), _stacked(w2_ref[...], 4), NT, preferred_element_type=jnp.float32
    )
    right_ref[...] = (right + shift2).reshape(n, 8, LANES).astype(jnp.bfloat16)


def _order(me, half):
    row = lax.broadcasted_iota(jnp.int32, (4 * LANES, 8 * CHANS), 0)
    col = lax.broadcasted_iota(jnp.int32, (4 * LANES, 8 * CHANS), 1)
    device = (row // LANES) ^ (me % 4)
    wanted = (row % CHANS) * 8 + ((row // CHANS) % 2) * 4 + device
    hit = (wanted == col) & ((row // (2 * CHANS)) % 2 == half)
    return jnp.where(hit, 1.0, 0.0).astype(jnp.bfloat16)


def _fold_kernel(right_ref, final_ref, out_ref, order_ref):
    me = lax.axis_index("row")
    for h in range(2):
        order_ref[h] = _order(me, h)
    devices = right_ref.shape[0]
    groups = devices // 4
    rows = devices * 8
    block = right_ref[...].astype(jnp.float32).reshape(rows, LANES)
    row = lax.broadcasted_iota(jnp.int32, (2 * rows, 2 * rows), 0)
    col = lax.broadcasted_iota(jnp.int32, (2 * rows, 2 * rows), 1)
    device = (row // 8) % groups * 4 + row % 4
    wanted = ((row // 4) % 2) * rows + device * 8 + row // (8 * groups)
    spread = jnp.where(wanted == col, 1.0, 0.0).astype(jnp.bfloat16)
    lane = lax.broadcasted_iota(jnp.int32, block.shape, 1) // CHANS
    lhs = []
    for jh in range(2):
        both = jnp.concatenate([jnp.where(lane == jh * 2 + s, block, 0.0) for s in range(2)], axis=0)
        moved = jnp.dot(spread, both.astype(jnp.bfloat16), preferred_element_type=jnp.float32)
        lhs.append(moved.astype(jnp.bfloat16))
    lhs = jnp.concatenate(lhs, axis=0)

    def body(pair, _):
        rhs = []
        for k in range(2):
            at = pl.multiple_of(pair * 2 * CHANS + k * CHANS, CHANS)
            rhs.append(jnp.concatenate([final_ref[pl.ds(at, CHANS), :]] * 4, axis=0))
        res = jnp.dot(lhs, jnp.concatenate(rhs, axis=1), preferred_element_type=jnp.float32)
        for j in range(16):
            for g in range(groups):
                r = (j * groups + g) * 8
                tile = jnp.concatenate([res[r : r + 8, :LANES], res[r : r + 8, LANES:]], axis=0)
                at = pl.multiple_of(g * 8 * CHANS + pair * 16, 16)
                out_ref[pl.ds(at, 16), pl.ds(j * LANES, LANES)] = tile.astype(jnp.bfloat16)
        return 0

    lax.fori_loop(0, CHANS // 2, body, 0)


def _band_kernel(count, *refs):
    own_refs, other_refs = refs[:4], refs[4:8]
    t_ref, order_ref, pair_ref, shift_ref, out_ref, l_ref, acc_ref, done_ref, sems = refs[8:17]
    fetched = refs[17:]
    half = own_refs[0].shape[1]
    band, cols = pair_ref.shape[0], pair_ref.shape[1]
    me = lax.axis_index("row")
    wide = 8 * CHANS

    for zi in range(own_refs[0].shape[0]):
        for y in range(2):
            lhs = jnp.concatenate(
                [own_refs[2 * y][zi], other_refs[2 * y][zi], own_refs[2 * y + 1][zi], other_refs[2 * y + 1][zi]],
                axis=1,
            )
            group = (zi * 2 + y) ^ (me // 4)
            at = pl.ds(pl.multiple_of(group * wide, wide), wide)
            for h in range(2):
                moved = jnp.dot(lhs, order_ref[h], preferred_element_type=jnp.float32)
                l_ref[pl.ds(h * half, half), at] = moved.astype(jnp.bfloat16)

    tile = 256
    pitch = cols + 1

    def column(step, _):
        at = pl.ds(pl.multiple_of(step * tile, tile), tile)
        if fetched:
            pltpu.sync_copy(t_ref.at[:, at], fetched[0])
            rhs = fetched[0][...]
        else:
            rhs = t_ref[:, at]
        res = jnp.dot(l_ref[...], rhs, preferred_element_type=jnp.float32)
        for k in range(tile // LANES):
            acc_ref[pl.ds(step * (tile // LANES) + k, band, stride=pitch), :] = res[:, k * LANES : (k + 1) * LANES]
        return 0

    lax.fori_loop(0, cols * LANES // tile, column, 0)

    rows = 32
    shift = shift_ref[...]

    def finish(r, _):
        for k in range(rows):
            i = r * rows + k
            total = acc_ref[pl.ds(i * pitch, cols), :] * (1.0 / count) + shift
            done_ref[i] = (pair_ref[i].astype(jnp.float32) + total).astype(jnp.bfloat16)
        at = pl.ds(pl.multiple_of(r * rows, rows), rows)
        pltpu.make_async_copy(done_ref.at[at], out_ref.at[at], sems.at[r]).start()
        return 0

    lax.fori_loop(0, band // rows, finish, 0)

    def drain(r, _):
        at = pl.ds(pl.multiple_of(r * rows, rows), rows)
        pltpu.make_async_copy(done_ref.at[at], out_ref.at[at], sems.at[r]).wait()
        return 0

    lax.fori_loop(0, band // rows, drain, 0)


def _xor(x, mask, n):
    return lax.ppermute(x, "row", [(i, i ^ mask) for i in range(n)])


def shards(n, alignment, pair, gain, bias, w1, b1, w2, b2, final, shift):
    seqs, residues, feats = alignment.shape
    band, cols, zdim = pair.shape
    half = band // 2
    count = float(seqs * n)
    small = n <= 32
    params = pltpu.CompilerParams(vmem_limit_bytes=(24 if small else 48) * 1024 * 1024)
    anywhere = pl.BlockSpec(memory_space=pl.ANY)
    vmem = pl.BlockSpec(memory_space=pltpu.VMEM)

    sources = [
        alignment, gain.reshape(1, -1), bias.reshape(1, -1), w1.T, b1.reshape(1, -1), w2.T, b2.reshape(1, -1)
    ]
    left, right = pl.pallas_call(
        _project_kernel,
        in_specs=[pl.BlockSpec(memory_space=pltpu.HBM)] * 7,
        out_specs=(vmem, vmem),
        out_shape=(
            jax.ShapeDtypeStruct((half, LANES), jnp.bfloat16),
            jax.ShapeDtypeStruct((n, 8, LANES), jnp.bfloat16),
        ),
        scratch_shapes=[pltpu.VMEM(a.shape, a.dtype) for a in sources] + [pltpu.SemaphoreType.DMA((7,))],
        compiler_params=pltpu.CompilerParams(vmem_limit_bytes=60 * 1024 * 1024),
        cost_estimate=pl.CostEstimate(
            flops=4 * seqs * residues * feats * CHANS, bytes_accessed=2 * seqs * residues * feats, transcendentals=0
        ),
    )(*sources)

    right = lax.all_to_all(right, "row", split_axis=0, concat_axis=0, tiled=True)

    line = [left] + [_xor(left, m, n) for m in range(8, n, 8)]
    line, right = lax.optimization_barrier((jnp.stack(line), right))
    plane = [_xor(line, m, n) for m in (2, 4, 6)]

    k = n * 2 * CHANS
    part = 32
    fold_cost = pl.CostEstimate(
        flops=2 * n * 32 * 256 * CHANS * zdim, bytes_accessed=2 * n * 2 * CHANS * cols * zdim, transcendentals=0
    )
    fold_out = (
        jax.ShapeDtypeStruct((k, cols * zdim), jnp.bfloat16),
        jax.ShapeDtypeStruct((2, 4 * LANES, 8 * CHANS), jnp.bfloat16),
    )
    if small:
        folded, order = pl.pallas_call(
            _fold_kernel,
            in_specs=[vmem, vmem],
            out_specs=(vmem, vmem),
            out_shape=fold_out,
            compiler_params=params,
            cost_estimate=fold_cost,
        )(right, final)
    else:
        folded, order = pl.pallas_call(
            _fold_kernel,
            grid=(n // part,),
            in_specs=[
                pl.BlockSpec((part, 8, LANES), lambda i: (i, 0, 0)),
                pl.BlockSpec(final.shape, lambda i: (0, 0)),
            ],
            out_specs=(
                pl.BlockSpec((part * 2 * CHANS, cols * zdim), lambda i: (i, 0)),
                pl.BlockSpec((2, 4 * LANES, 8 * CHANS), lambda i: (0, 0, 0)),
            ),
            out_shape=fold_out,
            compiler_params=params,
            cost_estimate=fold_cost,
        )(right, final)

    plane, folded = lax.optimization_barrier((plane, folded))
    own = [line] + plane
    other = [_xor(o, 1, n) for o in own]

    return pl.pallas_call(
        functools.partial(_band_kernel, count),
        in_specs=[vmem] * 8 + [vmem if small else anywhere] + [vmem] * 3,
        out_specs=anywhere,
        out_shape=jax.ShapeDtypeStruct(pair.shape, jnp.bfloat16),
        scratch_shapes=[
            pltpu.VMEM((band, k), jnp.bfloat16),
            pltpu.VMEM((band * (cols + 1), zdim), jnp.float32),
            pltpu.VMEM(pair.shape, jnp.bfloat16),
            pltpu.SemaphoreType.DMA((band // 32,)),
        ]
        + ([] if small else [pltpu.VMEM((k, 256), jnp.bfloat16)]),
        compiler_params=params,
        cost_estimate=pl.CostEstimate(
            flops=2 * band * k * cols * zdim, bytes_accessed=2 * k * cols * zdim, transcendentals=0
        ),
    )(*own, *other, folded, order, pair, shift.reshape(1, -1))


def solution(mesh):
    placed = (P(("group", "row"), None, None), P("group", "row", None)) + (P(),) * 8
    return jax.shard_map(
        functools.partial(shards, mesh.shape["row"]),
        mesh=mesh,
        in_specs=placed,
        out_specs=P("group", "row", None),
        check_vma=False,
    )
```

```python
import functools

import jax
import jax.numpy as jnp
from jax import lax
from jax.experimental import pallas as pl
from jax.experimental.pallas import tpu as pltpu
from jax.sharding import PartitionSpec as P

LANES = 128
CHANS = 32
NT = (((1,), (1,)), ((), ()))


def _stacked(weights, copies):
    c, q = weights.shape
    rows = []
    for k in range(copies):
        left = [jnp.zeros((c, k * q), weights.dtype)] if k else []
        right = [jnp.zeros((c, (copies - 1 - k) * q), weights.dtype)] if k < copies - 1 else []
        rows.append(jnp.concatenate(left + [weights] + right, axis=1))
    return jnp.concatenate(rows, axis=0)


def _project_kernel(*refs):
    sources, (left_ref, right_ref), held = refs[:7], refs[7:9], refs[9:16]
    sems = refs[16]
    copies = [pltpu.make_async_copy(a, b, sems.at[i]) for i, (a, b) in enumerate(zip(sources, held))]
    for copy in copies:
        copy.start()
    for copy in copies:
        copy.wait()
    x_ref, gain_ref, bias_ref, w1_ref, b1_ref, w2_ref, b2_ref = held
    band_half = left_ref.shape[0]
    n = right_ref.shape[0]
    feats = x_ref.shape[2]
    normed = []
    for s in range(2):
        x = x_ref[s].astype(jnp.float32)
        center = jnp.mean(x, axis=-1, keepdims=True)
        off = x - center
        spread = jnp.mean(off * off, axis=-1, keepdims=True)
        normed.append(off * lax.rsqrt(spread + 1e-05) * gain_ref[...] + bias_ref[...])
    low = [v[:band_half].astype(jnp.bfloat16) for v in normed]
    high = [v[band_half : 2 * band_half].astype(jnp.bfloat16) for v in normed]
    shift1 = jnp.concatenate([b1_ref[...]] * 4, axis=1)
    left = lax.dot_general(
        jnp.concatenate(low + high, axis=1), _stacked(w1_ref[...], 4), NT, preferred_element_type=jnp.float32
    )
    left_ref[...] = (left + shift1).astype(jnp.bfloat16)

    split = [v.reshape(n, 2, 8, feats) for v in normed]
    parts = [split[s][:, jh].reshape(n * 8, feats).astype(jnp.bfloat16) for jh in range(2) for s in range(2)]
    shift2 = jnp.concatenate([b2_ref[...]] * 4, axis=1)
    right = lax.dot_general(
        jnp.concatenate(parts, axis=1), _stacked(w2_ref[...], 4), NT, preferred_element_type=jnp.float32
    )
    right_ref[...] = (right + shift2).reshape(n, 8, LANES).astype(jnp.bfloat16)


def _order(me, half):
    row = lax.broadcasted_iota(jnp.int32, (4 * LANES, 8 * CHANS), 0)
    col = lax.broadcasted_iota(jnp.int32, (4 * LANES, 8 * CHANS), 1)
    device = (row // LANES) ^ (me % 4)
    wanted = (row % CHANS) * 8 + ((row // CHANS) % 2) * 4 + device
    hit = (wanted == col) & ((row // (2 * CHANS)) % 2 == half)
    return jnp.where(hit, 1.0, 0.0).astype(jnp.bfloat16)


def _fold_kernel(right_ref, final_ref, out_ref, order_ref):
    me = lax.axis_index("row")
    for h in range(2):
        order_ref[h] = _order(me, h)
    devices = right_ref.shape[0]
    groups = devices // 4
    rows = devices * 8
    block = right_ref[...].astype(jnp.float32).reshape(rows, LANES)
    row = lax.broadcasted_iota(jnp.int32, (2 * rows, 2 * rows), 0)
    col = lax.broadcasted_iota(jnp.int32, (2 * rows, 2 * rows), 1)
    device = (row // 8) % groups * 4 + row % 4
    wanted = ((row // 4) % 2) * rows + device * 8 + row // (8 * groups)
    spread = jnp.where(wanted == col, 1.0, 0.0).astype(jnp.bfloat16)
    lane = lax.broadcasted_iota(jnp.int32, block.shape, 1) // CHANS
    lhs = []
    for jh in range(2):
        both = jnp.concatenate([jnp.where(lane == jh * 2 + s, block, 0.0) for s in range(2)], axis=0)
        moved = jnp.dot(spread, both.astype(jnp.bfloat16), preferred_element_type=jnp.float32)
        lhs.append(moved.astype(jnp.bfloat16))
    lhs = jnp.concatenate(lhs, axis=0)

    def body(pair, _):
        rhs = []
        for k in range(2):
            at = pl.multiple_of(pair * 2 * CHANS + k * CHANS, CHANS)
            rhs.append(jnp.concatenate([final_ref[pl.ds(at, CHANS), :]] * 4, axis=0))
        res = jnp.dot(lhs, jnp.concatenate(rhs, axis=1), preferred_element_type=jnp.float32)
        for j in range(16):
            for g in range(groups):
                r = (j * groups + g) * 8
                tile = jnp.concatenate([res[r : r + 8, :LANES], res[r : r + 8, LANES:]], axis=0)
                at = pl.multiple_of(g * 8 * CHANS + pair * 16, 16)
                out_ref[pl.ds(at, 16), pl.ds(j * LANES, LANES)] = tile.astype(jnp.bfloat16)
        return 0

    lax.fori_loop(0, CHANS // 2, body, 0)


def _band_kernel(count, *refs):
    own_refs, other_refs = refs[:4], refs[4:8]
    t_ref, order_ref, pair_ref, shift_ref, out_ref, l_ref, acc_ref, done_ref, sems = refs[8:17]
    fetched = refs[17:]
    half = own_refs[0].shape[1]
    band, cols = pair_ref.shape[0], pair_ref.shape[1]
    me = lax.axis_index("row")
    wide = 8 * CHANS

    for zi in range(own_refs[0].shape[0]):
        for y in range(2):
            lhs = jnp.concatenate(
                [own_refs[2 * y][zi], other_refs[2 * y][zi], own_refs[2 * y + 1][zi], other_refs[2 * y + 1][zi]],
                axis=1,
            )
            group = (zi * 2 + y) ^ (me // 4)
            at = pl.ds(pl.multiple_of(group * wide, wide), wide)
            for h in range(2):
                moved = jnp.dot(lhs, order_ref[h], preferred_element_type=jnp.float32)
                l_ref[pl.ds(h * half, half), at] = moved.astype(jnp.bfloat16)

    tile = 256
    pitch = cols + 1

    def column(step, _):
        at = pl.ds(step * tile if isinstance(step, int) else pl.multiple_of(step * tile, tile), tile)
        if fetched:
            pltpu.sync_copy(t_ref.at[:, at], fetched[0])
            rhs = fetched[0][...]
        else:
            rhs = t_ref[:, at]
        res = jnp.dot(l_ref[...], rhs, preferred_element_type=jnp.float32)
        for k in range(tile // LANES):
            acc_ref[pl.ds(step * (tile // LANES) + k, band, stride=pitch), :] = res[:, k * LANES : (k + 1) * LANES]
        return 0

    if fetched:
        lax.fori_loop(0, cols * LANES // tile, column, 0)
    else:
        for step in range(cols * LANES // tile):
            column(step, 0)

    rows = 32
    shift = shift_ref[...]

    def finish(r, _):
        for k in range(rows):
            i = r * rows + k
            total = acc_ref[pl.ds(i * pitch, cols), :] * (1.0 / count) + shift
            done_ref[i] = (pair_ref[i].astype(jnp.float32) + total).astype(jnp.bfloat16)
        at = pl.ds(pl.multiple_of(r * rows, rows), rows)
        pltpu.make_async_copy(done_ref.at[at], out_ref.at[at], sems.at[r]).start()
        return 0

    lax.fori_loop(0, band // rows, finish, 0)

    def drain(r, _):
        at = pl.ds(pl.multiple_of(r * rows, rows), rows)
        pltpu.make_async_copy(done_ref.at[at], out_ref.at[at], sems.at[r]).wait()
        return 0

    lax.fori_loop(0, band // rows, drain, 0)


def _xor(x, mask, n):
    return lax.ppermute(x, "row", [(i, i ^ mask) for i in range(n)])


def shards(n, alignment, pair, gain, bias, w1, b1, w2, b2, final, shift):
    seqs, residues, feats = alignment.shape
    band, cols, zdim = pair.shape
    half = band // 2
    count = float(seqs * n)
    small = n <= 32
    params = pltpu.CompilerParams(vmem_limit_bytes=(24 if small else 48) * 1024 * 1024)
    anywhere = pl.BlockSpec(memory_space=pl.ANY)
    vmem = pl.BlockSpec(memory_space=pltpu.VMEM)

    sources = [
        alignment, gain.reshape(1, -1), bias.reshape(1, -1), w1.T, b1.reshape(1, -1), w2.T, b2.reshape(1, -1)
    ]
    left, right = pl.pallas_call(
        _project_kernel,
        in_specs=[pl.BlockSpec(memory_space=pltpu.HBM)] * 7,
        out_specs=(vmem, vmem),
        out_shape=(
            jax.ShapeDtypeStruct((half, LANES), jnp.bfloat16),
            jax.ShapeDtypeStruct((n, 8, LANES), jnp.bfloat16),
        ),
        scratch_shapes=[pltpu.VMEM(a.shape, a.dtype) for a in sources] + [pltpu.SemaphoreType.DMA((7,))],
        compiler_params=pltpu.CompilerParams(vmem_limit_bytes=60 * 1024 * 1024),
        cost_estimate=pl.CostEstimate(
            flops=4 * seqs * residues * feats * CHANS, bytes_accessed=2 * seqs * residues * feats, transcendentals=0
        ),
    )(*sources)

    right = lax.all_to_all(right, "row", split_axis=0, concat_axis=0, tiled=True)

    line = [left] + [_xor(left, m, n) for m in range(8, n, 8)]
    line = jnp.stack(line)
    plane = [_xor(line, m, n) for m in (2, 4, 6)]

    k = n * 2 * CHANS
    part = 32
    fold_cost = pl.CostEstimate(
        flops=2 * n * 32 * 256 * CHANS * zdim, bytes_accessed=2 * n * 2 * CHANS * cols * zdim, transcendentals=0
    )
    fold_out = (
        jax.ShapeDtypeStruct((k, cols * zdim), jnp.bfloat16),
        jax.ShapeDtypeStruct((2, 4 * LANES, 8 * CHANS), jnp.bfloat16),
    )
    if small:
        folded, order = pl.pallas_call(
            _fold_kernel,
            in_specs=[vmem, vmem],
            out_specs=(vmem, vmem),
            out_shape=fold_out,
            compiler_params=params,
            cost_estimate=fold_cost,
        )(right, final)
    else:
        folded, order = pl.pallas_call(
            _fold_kernel,
            grid=(n // part,),
            in_specs=[
                pl.BlockSpec((part, 8, LANES), lambda i: (i, 0, 0)),
                pl.BlockSpec(final.shape, lambda i: (0, 0)),
            ],
            out_specs=(
                pl.BlockSpec((part * 2 * CHANS, cols * zdim), lambda i: (i, 0)),
                pl.BlockSpec((2, 4 * LANES, 8 * CHANS), lambda i: (0, 0, 0)),
            ),
            out_shape=fold_out,
            compiler_params=params,
            cost_estimate=fold_cost,
        )(right, final)

    plane, folded = lax.optimization_barrier((plane, folded))
    own = [line] + plane
    other = [_xor(o, 1, n) for o in own]

    return pl.pallas_call(
        functools.partial(_band_kernel, count),
        in_specs=[vmem] * 8 + [vmem if small else anywhere] + [vmem] * 3,
        out_specs=anywhere,
        out_shape=jax.ShapeDtypeStruct(pair.shape, jnp.bfloat16),
        scratch_shapes=[
            pltpu.VMEM((band, k), jnp.bfloat16),
            pltpu.VMEM((band * (cols + 1), zdim), jnp.float32),
            pltpu.VMEM(pair.shape, jnp.bfloat16),
            pltpu.SemaphoreType.DMA((band // 32,)),
        ]
        + ([] if small else [pltpu.VMEM((k, 256), jnp.bfloat16)]),
        compiler_params=params,
        cost_estimate=pl.CostEstimate(
            flops=2 * band * k * cols * zdim, bytes_accessed=2 * k * cols * zdim, transcendentals=0
        ),
    )(*own, *other, folded, order, pair, shift.reshape(1, -1))


def solution(mesh):
    placed = (P(("group", "row"), None, None), P("group", "row", None)) + (P(),) * 8
    return jax.shard_map(
        functools.partial(shards, mesh.shape["row"]),
        mesh=mesh,
        in_specs=placed,
        out_specs=P("group", "row", None),
        check_vma=False,
    )
```

```python
import functools

import jax
import jax.numpy as jnp
from jax import lax
from jax.experimental import pallas as pl
from jax.experimental.pallas import tpu as pltpu
from jax.sharding import PartitionSpec as P

LANES = 128
CHANS = 32
NT = (((1,), (1,)), ((), ()))


def _stacked(weights, copies):
    c, q = weights.shape
    rows = []
    for k in range(copies):
        left = [jnp.zeros((c, k * q), weights.dtype)] if k else []
        right = [jnp.zeros((c, (copies - 1 - k) * q), weights.dtype)] if k < copies - 1 else []
        rows.append(jnp.concatenate(left + [weights] + right, axis=1))
    return jnp.concatenate(rows, axis=0)


def _project_kernel(*refs):
    sources, (left_ref, right_ref), held = refs[:7], refs[7:9], refs[9:16]
    sems = refs[16]
    copies = [pltpu.make_async_copy(a, b, sems.at[i]) for i, (a, b) in enumerate(zip(sources, held))]
    for copy in copies:
        copy.start()
    for copy in copies:
        copy.wait()
    x_ref, gain_ref, bias_ref, w1_ref, b1_ref, w2_ref, b2_ref = held
    band_half = left_ref.shape[0]
    n = right_ref.shape[0]
    feats = x_ref.shape[2]
    normed = []
    for s in range(2):
        x = x_ref[s].astype(jnp.float32)
        center = jnp.mean(x, axis=-1, keepdims=True)
        off = x - center
        spread = jnp.mean(off * off, axis=-1, keepdims=True)
        normed.append(off * lax.rsqrt(spread + 1e-05) * gain_ref[...] + bias_ref[...])
    low = [v[:band_half].astype(jnp.bfloat16) for v in normed]
    high = [v[band_half : 2 * band_half].astype(jnp.bfloat16) for v in normed]
    shift1 = jnp.concatenate([b1_ref[...]] * 4, axis=1)
    left = lax.dot_general(
        jnp.concatenate(low + high, axis=1), _stacked(w1_ref[...], 4), NT, preferred_element_type=jnp.float32
    )
    left_ref[...] = (left + shift1).astype(jnp.bfloat16)

    split = [v.reshape(n, 2, 8, feats) for v in normed]
    parts = [split[s][:, jh].reshape(n * 8, feats).astype(jnp.bfloat16) for jh in range(2) for s in range(2)]
    shift2 = jnp.concatenate([b2_ref[...]] * 4, axis=1)
    right = lax.dot_general(
        jnp.concatenate(parts, axis=1), _stacked(w2_ref[...], 4), NT, preferred_element_type=jnp.float32
    )
    right_ref[...] = (right + shift2).reshape(n, 8, LANES).astype(jnp.bfloat16)


def _order(me, half):
    row = lax.broadcasted_iota(jnp.int32, (4 * LANES, 8 * CHANS), 0)
    col = lax.broadcasted_iota(jnp.int32, (4 * LANES, 8 * CHANS), 1)
    device = (row // LANES) ^ (me // 8 % 4)
    wanted = (row % CHANS) * 8 + ((row // CHANS) % 2) * 4 + device
    hit = (wanted == col) & ((row // (2 * CHANS)) % 2 == half)
    return jnp.where(hit, 1.0, 0.0).astype(jnp.bfloat16)


def _fold_kernel(right_ref, final_ref, out_ref, order_ref):
    me = lax.axis_index("row")
    for h in range(2):
        order_ref[h] = _order(me, h)
    devices = right_ref.shape[0]
    groups = devices // 4
    rows = devices * 8
    block = right_ref[...].astype(jnp.float32).reshape(rows, LANES)
    row = lax.broadcasted_iota(jnp.int32, (2 * rows, 2 * rows), 0)
    col = lax.broadcasted_iota(jnp.int32, (2 * rows, 2 * rows), 1)
    device = (row // 8) % groups + row % 4 * groups
    wanted = ((row // 4) % 2) * rows + device * 8 + row // (8 * groups)
    spread = jnp.where(wanted == col, 1.0, 0.0).astype(jnp.bfloat16)
    lane = lax.broadcasted_iota(jnp.int32, block.shape, 1) // CHANS
    lhs = []
    for jh in range(2):
        both = jnp.concatenate([jnp.where(lane == jh * 2 + s, block, 0.0) for s in range(2)], axis=0)
        moved = jnp.dot(spread, both.astype(jnp.bfloat16), preferred_element_type=jnp.float32)
        lhs.append(moved.astype(jnp.bfloat16))
    lhs = jnp.concatenate(lhs, axis=0)

    for pair in range(CHANS // 2):
        rhs = []
        for k in range(2):
            at = pair * 2 * CHANS + k * CHANS
            rhs.append(jnp.concatenate([final_ref[pl.ds(at, CHANS), :]] * 4, axis=0))
        res = jnp.dot(lhs, jnp.concatenate(rhs, axis=1), preferred_element_type=jnp.float32)
        for j in range(16):
            for g in range(groups):
                r = (j * groups + g) * 8
                tile = jnp.concatenate([res[r : r + 8, :LANES], res[r : r + 8, LANES:]], axis=0)
                out_ref[g, 0, pl.ds(pair * 16, 16), pl.ds(j * LANES, LANES)] = tile.astype(jnp.bfloat16)


def _band_kernel(masks, begins, count, held, *refs):
    refs = list(refs)
    take = lambda k: [refs.pop(0) for _ in range(k)]
    lines = take(len(masks))
    t_ref, order_ref = take(2)
    (sum_ref,) = (None,) if begins else take(1)
    pair_ref, shift_ref = (None, None) if count is None else take(2)
    (out_ref,) = take(1)
    (l_ref,) = take(1)
    me = lax.axis_index("row")
    wide = 8 * CHANS
    places, half, _ = lines[0].shape
    chunks = []
    for line, mask in zip(lines, masks):
        for q in range(places // 4):
            lhs = jnp.concatenate([line[q * 4 + u] for u in range(4)], axis=1)
            at = pl.ds(len(chunks) * wide, wide)
            for h in range(2):
                moved = jnp.dot(lhs, order_ref[h], preferred_element_type=jnp.float32)
                l_ref[pl.ds(h * half, half), at] = moved.astype(jnp.bfloat16)
            chunks.append(((me % 8) ^ mask, q ^ (me // 32)))

    tile = 256
    band = 2 * half
    if count is not None:
        acc_ref, done_ref, sems = take(3)
        cols = pair_ref.shape[1]
        pitch = cols + 1

    def column(step):
        at = pl.ds(step * tile, tile)
        if held:
            rhs = jnp.concatenate([t_ref[g, q, :, at] for g, q in chunks], axis=0)
        else:
            for i, (g, q) in enumerate(chunks):
                pltpu.sync_copy(t_ref.at[g, q, :, at], refs[0].at[pl.ds(i * wide, wide)])
            rhs = refs[0][...]
        res = jnp.dot(l_ref[...], rhs, preferred_element_type=jnp.float32)
        if sum_ref is not None:
            res = res + sum_ref[:, at]
        if count is None:
            out_ref[:, at] = res
        else:
            for k in range(tile // LANES):
                j = step * (tile // LANES) + k
                acc_ref[pl.ds(j, band, stride=pitch), :] = res[:, k * LANES : (k + 1) * LANES]

    for step in range(t_ref.shape[3] // tile):
        column(step)
    if count is None:
        return

    rows = 32
    shift = shift_ref[...]

    def finish(r, _):
        for k in range(rows):
            i = r * rows + k
            total = acc_ref[pl.ds(i * pitch, cols), :] * (1.0 / count) + shift
            done_ref[i] = (pair_ref[i].astype(jnp.float32) + total).astype(jnp.bfloat16)
        at = pl.ds(pl.multiple_of(r * rows, rows), rows)
        pltpu.make_async_copy(done_ref.at[at], out_ref.at[at], sems.at[r]).start()
        return 0

    lax.fori_loop(0, band // rows, finish, 0)

    def drain(r, _):
        at = pl.ds(pl.multiple_of(r * rows, rows), rows)
        pltpu.make_async_copy(done_ref.at[at], out_ref.at[at], sems.at[r]).wait()
        return 0

    lax.fori_loop(0, band // rows, drain, 0)


def _xor(x, mask, n):
    return lax.ppermute(x, "row", [(i, i ^ mask) for i in range(n)])


def shards(n, alignment, pair, gain, bias, w1, b1, w2, b2, final, shift):
    seqs, residues, feats = alignment.shape
    band, cols, zdim = pair.shape
    half = band // 2
    count = float(seqs * n)
    small = n <= 32
    params = pltpu.CompilerParams(vmem_limit_bytes=(24 if small else 48) * 1024 * 1024)
    anywhere = pl.BlockSpec(memory_space=pl.ANY)
    vmem = pl.BlockSpec(memory_space=pltpu.VMEM)

    sources = [
        alignment, gain.reshape(1, -1), bias.reshape(1, -1), w1.T, b1.reshape(1, -1), w2.T, b2.reshape(1, -1)
    ]
    left, right = pl.pallas_call(
        _project_kernel,
        in_specs=[pl.BlockSpec(memory_space=pltpu.HBM)] * 7,
        out_specs=(vmem, vmem),
        out_shape=(
            jax.ShapeDtypeStruct((half, LANES), jnp.bfloat16),
            jax.ShapeDtypeStruct((n, 8, LANES), jnp.bfloat16),
        ),
        scratch_shapes=[pltpu.VMEM(a.shape, a.dtype) for a in sources] + [pltpu.SemaphoreType.DMA((7,))],
        compiler_params=pltpu.CompilerParams(vmem_limit_bytes=60 * 1024 * 1024),
        cost_estimate=pl.CostEstimate(
            flops=4 * seqs * residues * feats * CHANS, bytes_accessed=2 * seqs * residues * feats, transcendentals=0
        ),
    )(*sources)

    right = lax.all_to_all(right, "row", split_axis=0, concat_axis=0, tiled=True)

    line = [left] + [_xor(left, m, n) for m in range(8, n, 8)]
    line = jnp.stack(line)
    plane = [_xor(line, m, n) for m in (2, 4, 6)]

    part = 32
    parts = n // part
    fold_cost = pl.CostEstimate(
        flops=2 * n * 32 * 256 * CHANS * zdim, bytes_accessed=4 * n * CHANS * cols * zdim, transcendentals=0
    )
    fold_out = (
        jax.ShapeDtypeStruct((8, parts, 8 * CHANS, cols * zdim), jnp.bfloat16),
        jax.ShapeDtypeStruct((2, 4 * LANES, 8 * CHANS), jnp.bfloat16),
    )
    if small:
        specs = dict(in_specs=[vmem, vmem], out_specs=(vmem, vmem))
    else:
        specs = dict(
            grid=(parts,),
            in_specs=[
                pl.BlockSpec((part, 8, LANES), lambda i: (i, 0, 0)),
                pl.BlockSpec(final.shape, lambda i: (0, 0)),
            ],
            out_specs=(
                pl.BlockSpec((8, 1, 8 * CHANS, cols * zdim), lambda i: (0, i, 0, 0)),
                pl.BlockSpec((2, 4 * LANES, 8 * CHANS), lambda i: (0, 0, 0)),
            ),
        )
    folded, order = pl.pallas_call(
        _fold_kernel, out_shape=fold_out, compiler_params=params, cost_estimate=fold_cost, **specs
    )(right, final)

    def add(lines, masks, total, last):
        depth = len(masks) * parts * 8 * CHANS
        scratch = [pltpu.VMEM((band, depth), jnp.bfloat16)]
        operands = [*lines, folded, order] + ([] if total is None else [total])
        if last:
            operands += [pair, shift.reshape(1, -1)]
            scratch += [
                pltpu.VMEM((band * (cols + 1), zdim), jnp.float32),
                pltpu.VMEM(pair.shape, jnp.bfloat16),
                pltpu.SemaphoreType.DMA((band // 32,)),
            ]
        if not small:
            scratch.append(pltpu.VMEM((depth, 256), jnp.bfloat16))
        in_specs = [vmem] * len(operands)
        if not small:
            in_specs[len(lines)] = anywhere
        return pl.pallas_call(
            functools.partial(_band_kernel, masks, total is None, count if last else None, small),
            in_specs=in_specs,
            out_specs=anywhere if last else vmem,
            out_shape=jax.ShapeDtypeStruct(pair.shape, jnp.bfloat16)
            if last
            else jax.ShapeDtypeStruct((band, cols * zdim), jnp.float32),
            scratch_shapes=scratch,
            compiler_params=params,
            cost_estimate=pl.CostEstimate(
                flops=2 * band * depth * cols * zdim, bytes_accessed=2 * depth * cols * zdim, transcendentals=0
            ),
        )(*operands)

    total = add([line, _xor(line, 1, n)], (0, 1), None, False)
    plane, total = lax.optimization_barrier((plane, total))
    other = [_xor(o, 1, n) for o in plane]
    total = add(plane, (2, 4, 6), total, False)
    return add(other, (3, 5, 7), total, True)


def solution(mesh):
    placed = (P(("group", "row"), None, None), P("group", "row", None)) + (P(),) * 8
    return jax.shard_map(
        functools.partial(shards, mesh.shape["row"]),
        mesh=mesh,
        in_specs=placed,
        out_specs=P("group", "row", None),
        check_vma=False,
    )
```

```python
import functools

import jax
import jax.numpy as jnp
from jax import lax
from jax.experimental import pallas as pl
from jax.experimental.pallas import tpu as pltpu
from jax.sharding import PartitionSpec as P

LANES = 128
CHANS = 32
NT = (((1,), (1,)), ((), ()))


def _stacked(weights, copies):
    c, q = weights.shape
    rows = []
    for k in range(copies):
        left = [jnp.zeros((c, k * q), weights.dtype)] if k else []
        right = [jnp.zeros((c, (copies - 1 - k) * q), weights.dtype)] if k < copies - 1 else []
        rows.append(jnp.concatenate(left + [weights] + right, axis=1))
    return jnp.concatenate(rows, axis=0)


def _project_kernel(*refs):
    sources, (left_ref, right_ref), held = refs[:7], refs[7:9], refs[9:16]
    sems = refs[16]
    copies = [pltpu.make_async_copy(a, b, sems.at[i]) for i, (a, b) in enumerate(zip(sources, held))]
    for copy in copies:
        copy.start()
    for copy in copies:
        copy.wait()
    x_ref, gain_ref, bias_ref, w1_ref, b1_ref, w2_ref, b2_ref = held
    band_half = left_ref.shape[0]
    n = right_ref.shape[0]
    feats = x_ref.shape[2]
    normed = []
    for s in range(2):
        x = x_ref[s].astype(jnp.float32)
        center = jnp.mean(x, axis=-1, keepdims=True)
        off = x - center
        spread = jnp.mean(off * off, axis=-1, keepdims=True)
        normed.append(off * lax.rsqrt(spread + 1e-05) * gain_ref[...] + bias_ref[...])
    low = [v[:band_half].astype(jnp.bfloat16) for v in normed]
    high = [v[band_half : 2 * band_half].astype(jnp.bfloat16) for v in normed]
    shift1 = jnp.concatenate([b1_ref[...]] * 4, axis=1)
    left = lax.dot_general(
        jnp.concatenate(low + high, axis=1), _stacked(w1_ref[...], 4), NT, preferred_element_type=jnp.float32
    )
    left_ref[...] = (left + shift1).astype(jnp.bfloat16)

    split = [v.reshape(n, 2, 8, feats) for v in normed]
    parts = [split[s][:, jh].reshape(n * 8, feats).astype(jnp.bfloat16) for jh in range(2) for s in range(2)]
    shift2 = jnp.concatenate([b2_ref[...]] * 4, axis=1)
    right = lax.dot_general(
        jnp.concatenate(parts, axis=1), _stacked(w2_ref[...], 4), NT, preferred_element_type=jnp.float32
    )
    right_ref[...] = (right + shift2).reshape(n, 8, LANES).astype(jnp.bfloat16)


def _order(me, half):
    row = lax.broadcasted_iota(jnp.int32, (4 * LANES, 8 * CHANS), 0)
    col = lax.broadcasted_iota(jnp.int32, (4 * LANES, 8 * CHANS), 1)
    device = (row // LANES) ^ (me // 8 % 4)
    wanted = (row % CHANS) * 8 + ((row // CHANS) % 2) * 4 + device
    hit = (wanted == col) & ((row // (2 * CHANS)) % 2 == half)
    return jnp.where(hit, 1.0, 0.0).astype(jnp.bfloat16)


def _fold_kernel(right_ref, final_ref, out_ref, order_ref):
    me = lax.axis_index("row")
    for h in range(2):
        order_ref[h] = _order(me, h)
    devices = right_ref.shape[0]
    groups = devices // 4
    rows = devices * 8
    block = right_ref[...].astype(jnp.float32).reshape(rows, LANES)
    row = lax.broadcasted_iota(jnp.int32, (2 * rows, 2 * rows), 0)
    col = lax.broadcasted_iota(jnp.int32, (2 * rows, 2 * rows), 1)
    device = (row // 8) % groups + row % 4 * groups
    wanted = ((row // 4) % 2) * rows + device * 8 + row // (8 * groups)
    spread = jnp.where(wanted == col, 1.0, 0.0).astype(jnp.bfloat16)
    lane = lax.broadcasted_iota(jnp.int32, block.shape, 1) // CHANS
    lhs = []
    for jh in range(2):
        both = jnp.concatenate([jnp.where(lane == jh * 2 + s, block, 0.0) for s in range(2)], axis=0)
        moved = jnp.dot(spread, both.astype(jnp.bfloat16), preferred_element_type=jnp.float32)
        lhs.append(moved.astype(jnp.bfloat16))
    lhs = jnp.concatenate(lhs, axis=0)

    for pair in range(CHANS // 2):
        rhs = []
        for k in range(2):
            at = pair * 2 * CHANS + k * CHANS
            rhs.append(jnp.concatenate([final_ref[pl.ds(at, CHANS), :]] * 4, axis=0))
        res = jnp.dot(lhs, jnp.concatenate(rhs, axis=1), preferred_element_type=jnp.float32)
        for j in range(16):
            for g in range(groups):
                r = (j * groups + g) * 8
                tile = jnp.concatenate([res[r : r + 8, :LANES], res[r : r + 8, LANES:]], axis=0)
                out_ref[g, 0, pl.ds(pair * 16, 16), pl.ds(j * LANES, LANES)] = tile.astype(jnp.bfloat16)


def _band_kernel(lines, operands, begins, count, held, *refs):
    refs = list(refs)
    take = lambda k: [refs.pop(0) for _ in range(k)]
    blocks = take(operands)
    t_ref, order_ref = take(2)
    (sum_ref,) = (None,) if begins else take(1)
    pair_ref, shift_ref = (None, None) if count is None else take(2)
    (out_ref,) = take(1)
    (l_ref,) = take(1)
    me = lax.axis_index("row")
    wide = 8 * CHANS
    half = blocks[0].shape[-2]
    chunks = []
    for mask, line in lines.items():
        for q in range(len(line) // 4):
            slots = [blocks[i][...] if k is None else blocks[i][k] for i, k in line[q * 4 : q * 4 + 4]]
            lhs = jnp.concatenate(slots, axis=1)
            at = pl.ds(len(chunks) * wide, wide)
            for h in range(2):
                moved = jnp.dot(lhs, order_ref[h], preferred_element_type=jnp.float32)
                l_ref[pl.ds(h * half, half), at] = moved.astype(jnp.bfloat16)
            chunks.append(((me % 8) ^ mask, q ^ (me // 32)))

    tile = 256
    band = 2 * half
    if count is not None:
        acc_ref, done_ref, sems = take(3)
        cols = pair_ref.shape[1]
        pitch = cols + 1

    def column(step):
        at = pl.ds(step * tile, tile)
        if held:
            rhs = jnp.concatenate([t_ref[g, q, :, at] for g, q in chunks], axis=0)
        else:
            for i, (g, q) in enumerate(chunks):
                pltpu.sync_copy(t_ref.at[g, q, :, at], refs[0].at[pl.ds(i * wide, wide)])
            rhs = refs[0][...]
        res = jnp.dot(l_ref[...], rhs, preferred_element_type=jnp.float32)
        if sum_ref is not None:
            res = res + sum_ref[:, at]
        if count is None:
            out_ref[:, at] = res
        else:
            for k in range(tile // LANES):
                j = step * (tile // LANES) + k
                acc_ref[pl.ds(j, band, stride=pitch), :] = res[:, k * LANES : (k + 1) * LANES]

    for step in range(t_ref.shape[3] // tile):
        column(step)
    if count is None:
        return

    rows = 32
    shift = shift_ref[...]

    def finish(r, _):
        for k in range(rows):
            i = r * rows + k
            total = acc_ref[pl.ds(i * pitch, cols), :] * (1.0 / count) + shift
            done_ref[i] = (pair_ref[i].astype(jnp.float32) + total).astype(jnp.bfloat16)
        at = pl.ds(pl.multiple_of(r * rows, rows), rows)
        pltpu.make_async_copy(done_ref.at[at], out_ref.at[at], sems.at[r]).start()
        return 0

    lax.fori_loop(0, band // rows, finish, 0)

    def drain(r, _):
        at = pl.ds(pl.multiple_of(r * rows, rows), rows)
        pltpu.make_async_copy(done_ref.at[at], out_ref.at[at], sems.at[r]).wait()
        return 0

    lax.fori_loop(0, band // rows, drain, 0)


def _xor(x, mask, n):
    return lax.ppermute(x, "row", [(i, i ^ mask) for i in range(n)])


def shards(n, alignment, pair, gain, bias, w1, b1, w2, b2, final, shift):
    seqs, residues, feats = alignment.shape
    band, cols, zdim = pair.shape
    half = band // 2
    count = float(seqs * n)
    small = n <= 32
    params = pltpu.CompilerParams(vmem_limit_bytes=(24 if small else 48) * 1024 * 1024)
    anywhere = pl.BlockSpec(memory_space=pl.ANY)
    vmem = pl.BlockSpec(memory_space=pltpu.VMEM)

    sources = [
        alignment, gain.reshape(1, -1), bias.reshape(1, -1), w1.T, b1.reshape(1, -1), w2.T, b2.reshape(1, -1)
    ]
    left, right = pl.pallas_call(
        _project_kernel,
        in_specs=[pl.BlockSpec(memory_space=pltpu.HBM)] * 7,
        out_specs=(vmem, vmem),
        out_shape=(
            jax.ShapeDtypeStruct((half, LANES), jnp.bfloat16),
            jax.ShapeDtypeStruct((n, 8, LANES), jnp.bfloat16),
        ),
        scratch_shapes=[pltpu.VMEM(a.shape, a.dtype) for a in sources] + [pltpu.SemaphoreType.DMA((7,))],
        compiler_params=pltpu.CompilerParams(vmem_limit_bytes=60 * 1024 * 1024),
        cost_estimate=pl.CostEstimate(
            flops=4 * seqs * residues * feats * CHANS, bytes_accessed=2 * seqs * residues * feats, transcendentals=0
        ),
    )(*sources)

    right = lax.all_to_all(right, "row", split_axis=0, concat_axis=0, tiled=True)

    alone = [_xor(left, m, n) for m in range(8, n, 8)]
    firsts = [_xor(left, m, n) for m in (2, 4, 6)]
    partner = _xor(left, 1, n)
    rest = jnp.stack(alone)
    plane = [_xor(rest, m, n) for m in (2, 4, 6)]
    part = 32
    parts = n // part
    fold_cost = pl.CostEstimate(
        flops=2 * n * 32 * 256 * CHANS * zdim, bytes_accessed=4 * n * CHANS * cols * zdim, transcendentals=0
    )
    fold_out = (
        jax.ShapeDtypeStruct((8, parts, 8 * CHANS, cols * zdim), jnp.bfloat16),
        jax.ShapeDtypeStruct((2, 4 * LANES, 8 * CHANS), jnp.bfloat16),
    )
    if small:
        specs = dict(in_specs=[vmem, vmem], out_specs=(vmem, vmem))
    else:
        specs = dict(
            grid=(parts,),
            in_specs=[
                pl.BlockSpec((part, 8, LANES), lambda i: (i, 0, 0)),
                pl.BlockSpec(final.shape, lambda i: (0, 0)),
            ],
            out_specs=(
                pl.BlockSpec((8, 1, 8 * CHANS, cols * zdim), lambda i: (0, i, 0, 0)),
                pl.BlockSpec((2, 4 * LANES, 8 * CHANS), lambda i: (0, 0, 0)),
            ),
        )
    folded, order = pl.pallas_call(
        _fold_kernel, out_shape=fold_out, compiler_params=params, cost_estimate=fold_cost, **specs
    )(right, final)

    def add(blocks, lines, total, last):
        depth = len(lines) * parts * 8 * CHANS
        scratch = [pltpu.VMEM((band, depth), jnp.bfloat16)]
        operands = [*blocks, folded, order] + ([] if total is None else [total])
        if last:
            operands += [pair, shift.reshape(1, -1)]
            scratch += [
                pltpu.VMEM((band * (cols + 1), zdim), jnp.float32),
                pltpu.VMEM(pair.shape, jnp.bfloat16),
                pltpu.SemaphoreType.DMA((band // 32,)),
            ]
        if not small:
            scratch.append(pltpu.VMEM((depth, 256), jnp.bfloat16))
        in_specs = [vmem] * len(operands)
        if not small:
            in_specs[len(blocks)] = anywhere
        return pl.pallas_call(
            functools.partial(_band_kernel, lines, len(blocks), total is None, count if last else None, small),
            in_specs=in_specs,
            out_specs=anywhere if last else vmem,
            out_shape=jax.ShapeDtypeStruct(pair.shape, jnp.bfloat16)
            if last
            else jax.ShapeDtypeStruct((band, cols * zdim), jnp.float32),
            scratch_shapes=scratch,
            compiler_params=params,
            cost_estimate=pl.CostEstimate(
                flops=2 * band * depth * cols * zdim, bytes_accessed=2 * depth * cols * zdim, transcendentals=0
            ),
        )(*operands)

    more = len(alone)
    whole = lambda first, i: [first] + [(i, k) for k in range(more)]
    alone, firsts, folded = lax.optimization_barrier((alone, firsts, folded))
    across = _xor(jnp.stack(alone + firsts), 1, n)
    total = add([left, rest], {0: whole((0, None), 1)}, None, False)
    plane, total = lax.optimization_barrier((plane, total))
    others = [_xor(o, 1, n) for o in plane]
    lines = {2 * g + 2: whole((g, None), 3 + g) for g in range(3)}
    lines[1] = whole((6, None), 7)
    total = add(firsts + plane + [partner, across], lines, total, False)
    lines = {2 * g + 3: whole((0, more + g), 1 + g) for g in range(3)}
    return add([across] + others, lines, total, True)


def solution(mesh):
    placed = (P(("group", "row"), None, None), P("group", "row", None)) + (P(),) * 8
    return jax.shard_map(
        functools.partial(shards, mesh.shape["row"]),
        mesh=mesh,
        in_specs=placed,
        out_specs=P("group", "row", None),
        check_vma=False,
    )
```

```python
import functools

import jax
import jax.numpy as jnp
from jax import lax
from jax.experimental import pallas as pl
from jax.experimental.pallas import tpu as pltpu
from jax.sharding import PartitionSpec as P

LANES = 128
CHANS = 32
NT = (((1,), (1,)), ((), ()))


def _stacked(weights, copies):
    c, q = weights.shape
    rows = []
    for k in range(copies):
        left = [jnp.zeros((c, k * q), weights.dtype)] if k else []
        right = [jnp.zeros((c, (copies - 1 - k) * q), weights.dtype)] if k < copies - 1 else []
        rows.append(jnp.concatenate(left + [weights] + right, axis=1))
    return jnp.concatenate(rows, axis=0)


def _project_kernel(*refs):
    sources, (left_ref, right_ref), held = refs[:7], refs[7:9], refs[9:16]
    sems = refs[16]
    copies = [pltpu.make_async_copy(a, b, sems.at[i]) for i, (a, b) in enumerate(zip(sources, held))]
    for copy in copies:
        copy.start()
    for copy in copies:
        copy.wait()
    x_ref, gain_ref, bias_ref, w1_ref, b1_ref, w2_ref, b2_ref = held
    band_half = left_ref.shape[1]
    n = right_ref.shape[0]
    feats = x_ref.shape[2]
    normed = []
    for s in range(2):
        x = x_ref[s].astype(jnp.float32)
        center = jnp.mean(x, axis=-1, keepdims=True)
        off = x - center
        spread = jnp.mean(off * off, axis=-1, keepdims=True)
        normed.append(off * lax.rsqrt(spread + 1e-05) * gain_ref[...] + bias_ref[...])
    low = [v[:band_half].astype(jnp.bfloat16) for v in normed]
    high = [v[band_half : 2 * band_half].astype(jnp.bfloat16) for v in normed]
    shift1 = jnp.concatenate([b1_ref[...]] * 4, axis=1)
    left = lax.dot_general(
        jnp.concatenate(low + high, axis=1), _stacked(w1_ref[...], 4), NT, preferred_element_type=jnp.float32
    )
    left = (left + shift1).astype(jnp.bfloat16)
    for k in range(left_ref.shape[0]):
        left_ref[k] = left

    split = [v.reshape(n, 2, 8, feats) for v in normed]
    parts = [split[s][:, jh].reshape(n * 8, feats).astype(jnp.bfloat16) for jh in range(2) for s in range(2)]
    shift2 = jnp.concatenate([b2_ref[...]] * 4, axis=1)
    right = lax.dot_general(
        jnp.concatenate(parts, axis=1), _stacked(w2_ref[...], 4), NT, preferred_element_type=jnp.float32
    )
    right_ref[...] = (right + shift2).reshape(n, 8, LANES).astype(jnp.bfloat16)


def _order(half):
    row = lax.broadcasted_iota(jnp.int32, (4 * LANES, 8 * CHANS), 0)
    col = lax.broadcasted_iota(jnp.int32, (4 * LANES, 8 * CHANS), 1)
    wanted = (row % CHANS) * 8 + ((row // CHANS) % 2) * 4 + row // LANES
    hit = (wanted == col) & ((row // (2 * CHANS)) % 2 == half)
    return jnp.where(hit, 1.0, 0.0).astype(jnp.bfloat16)


def _fold_kernel(right_ref, final_ref, out_ref, order_ref):
    for h in range(2):
        order_ref[h] = _order(h)
    devices = right_ref.shape[0]
    groups = devices // 4
    rows = devices * 8
    block = right_ref[...].astype(jnp.float32).reshape(rows, LANES)
    row = lax.broadcasted_iota(jnp.int32, (2 * rows, 2 * rows), 0)
    col = lax.broadcasted_iota(jnp.int32, (2 * rows, 2 * rows), 1)
    device = (row // 8) % groups + row % 4 * groups
    wanted = ((row // 4) % 2) * rows + device * 8 + row // (8 * groups)
    spread = jnp.where(wanted == col, 1.0, 0.0).astype(jnp.bfloat16)
    lane = lax.broadcasted_iota(jnp.int32, block.shape, 1) // CHANS
    lhs = []
    for jh in range(2):
        both = jnp.concatenate([jnp.where(lane == jh * 2 + s, block, 0.0) for s in range(2)], axis=0)
        moved = jnp.dot(spread, both.astype(jnp.bfloat16), preferred_element_type=jnp.float32)
        lhs.append(moved.astype(jnp.bfloat16))
    lhs = jnp.concatenate(lhs, axis=0)

    for pair in range(CHANS // 2):
        rhs = []
        for k in range(2):
            at = pair * 2 * CHANS + k * CHANS
            rhs.append(jnp.concatenate([final_ref[pl.ds(at, CHANS), :]] * 4, axis=0))
        res = jnp.dot(lhs, jnp.concatenate(rhs, axis=1), preferred_element_type=jnp.float32)
        for j in range(16):
            for g in range(groups):
                r = (j * groups + g) * 8
                tile = jnp.concatenate([res[r : r + 8, :LANES], res[r : r + 8, LANES:]], axis=0)
                out_ref[g, 0, pl.ds(pair * 16, 16), pl.ds(j * LANES, LANES)] = tile.astype(jnp.bfloat16)


def _band_kernel(lines, operands, begins, count, held, *refs):
    refs = list(refs)
    take = lambda k: [refs.pop(0) for _ in range(k)]
    blocks = take(operands)
    t_ref, order_ref = take(2)
    (sum_ref,) = (None,) if begins else take(1)
    pair_ref, shift_ref = (None, None) if count is None else take(2)
    (out_ref,) = take(1)
    (l_ref,) = take(1)
    me = lax.axis_index("row")
    wide = 8 * CHANS
    places, half, _ = blocks[0].shape[-3:]
    chunks = []
    for mask, operand, plane in lines:
        block = blocks[operand].at[(me // 2 % 4) ^ (mask // 2)] if plane else blocks[operand]
        for q in range(places // 4):
            lhs = jnp.concatenate([block[q * 4 + u] for u in range(4)], axis=1)
            at = pl.ds(len(chunks) * wide, wide)
            for h in range(2):
                moved = jnp.dot(lhs, order_ref[h], preferred_element_type=jnp.float32)
                l_ref[pl.ds(h * half, half), at] = moved.astype(jnp.bfloat16)
            chunks.append(((me % 8) ^ mask, q))

    tile = 256
    band = 2 * half
    if count is not None:
        acc_ref, done_ref, sems = take(3)
        cols = pair_ref.shape[1]
        pitch = cols + 1

    def column(step):
        at = pl.ds(step * tile, tile)
        if held:
            rhs = jnp.concatenate([t_ref[g, q, :, at] for g, q in chunks], axis=0)
        else:
            for i, (g, q) in enumerate(chunks):
                pltpu.sync_copy(t_ref.at[g, q, :, at], refs[0].at[pl.ds(i * wide, wide)])
            rhs = refs[0][...]
        res = jnp.dot(l_ref[...], rhs, preferred_element_type=jnp.float32)
        if sum_ref is not None:
            res = res + sum_ref[:, at]
        if count is None:
            out_ref[:, at] = res
        else:
            for k in range(tile // LANES):
                j = step * (tile // LANES) + k
                acc_ref[pl.ds(j, band, stride=pitch), :] = res[:, k * LANES : (k + 1) * LANES]

    for step in range(t_ref.shape[3] // tile):
        column(step)
    if count is None:
        return

    rows = 32
    shift = shift_ref[...]

    def finish(r, _):
        for k in range(rows):
            i = r * rows + k
            total = acc_ref[pl.ds(i * pitch, cols), :] * (1.0 / count) + shift
            done_ref[i] = (pair_ref[i].astype(jnp.float32) + total).astype(jnp.bfloat16)
        at = pl.ds(pl.multiple_of(r * rows, rows), rows)
        pltpu.make_async_copy(done_ref.at[at], out_ref.at[at], sems.at[r]).start()
        return 0

    lax.fori_loop(0, band // rows, finish, 0)

    def drain(r, _):
        at = pl.ds(pl.multiple_of(r * rows, rows), rows)
        pltpu.make_async_copy(done_ref.at[at], out_ref.at[at], sems.at[r]).wait()
        return 0

    lax.fori_loop(0, band // rows, drain, 0)


def _xor(x, mask, n):
    return lax.ppermute(x, "row", [(i, i ^ mask) for i in range(n)])


def shards(n, alignment, pair, gain, bias, w1, b1, w2, b2, final, shift):
    seqs, residues, feats = alignment.shape
    band, cols, zdim = pair.shape
    half = band // 2
    count = float(seqs * n)
    small = n <= 32
    params = pltpu.CompilerParams(vmem_limit_bytes=(24 if small else 48) * 1024 * 1024)
    anywhere = pl.BlockSpec(memory_space=pl.ANY)
    vmem = pl.BlockSpec(memory_space=pltpu.VMEM)

    sources = [
        alignment, gain.reshape(1, -1), bias.reshape(1, -1), w1.T, b1.reshape(1, -1), w2.T, b2.reshape(1, -1)
    ]
    left, right = pl.pallas_call(
        _project_kernel,
        in_specs=[pl.BlockSpec(memory_space=pltpu.HBM)] * 7,
        out_specs=(vmem, vmem),
        out_shape=(
            jax.ShapeDtypeStruct((n // 8, half, LANES), jnp.bfloat16),
            jax.ShapeDtypeStruct((n, 8, LANES), jnp.bfloat16),
        ),
        scratch_shapes=[pltpu.VMEM(a.shape, a.dtype) for a in sources] + [pltpu.SemaphoreType.DMA((7,))],
        compiler_params=pltpu.CompilerParams(vmem_limit_bytes=60 * 1024 * 1024),
        cost_estimate=pl.CostEstimate(
            flops=4 * seqs * residues * feats * CHANS, bytes_accessed=2 * seqs * residues * feats, transcendentals=0
        ),
    )(*sources)

    right = lax.all_to_all(right, "row", split_axis=0, concat_axis=0, tiled=True)

    places = n // 8
    along = [[i * 8 + g for i in range(places)] for g in range(8)]
    across = [[i * 8 + g * 2 + c for g in range(4)] for i in range(places) for c in range(2)]
    line = lax.all_to_all(left, "row", 0, 0, axis_index_groups=along, tiled=True)
    plane = jnp.broadcast_to(line[None], (4,) + line.shape)
    plane = lax.all_to_all(plane, "row", 0, 0, axis_index_groups=across, tiled=True)

    part = 32
    parts = n // part
    fold_cost = pl.CostEstimate(
        flops=2 * n * 32 * 256 * CHANS * zdim, bytes_accessed=4 * n * CHANS * cols * zdim, transcendentals=0
    )
    fold_out = (
        jax.ShapeDtypeStruct((8, parts, 8 * CHANS, cols * zdim), jnp.bfloat16),
        jax.ShapeDtypeStruct((2, 4 * LANES, 8 * CHANS), jnp.bfloat16),
    )
    if small:
        specs = dict(in_specs=[vmem, vmem], out_specs=(vmem, vmem))
    else:
        specs = dict(
            grid=(parts,),
            in_specs=[
                pl.BlockSpec((part, 8, LANES), lambda i: (i, 0, 0)),
                pl.BlockSpec(final.shape, lambda i: (0, 0)),
            ],
            out_specs=(
                pl.BlockSpec((8, 1, 8 * CHANS, cols * zdim), lambda i: (0, i, 0, 0)),
                pl.BlockSpec((2, 4 * LANES, 8 * CHANS), lambda i: (0, 0, 0)),
            ),
        )
    folded, order = pl.pallas_call(
        _fold_kernel, out_shape=fold_out, compiler_params=params, cost_estimate=fold_cost, **specs
    )(right, final)

    def add(blocks, lines, total, last):
        depth = len(lines) * parts * 8 * CHANS
        scratch = [pltpu.VMEM((band, depth), jnp.bfloat16)]
        operands = [*blocks, folded, order] + ([] if total is None else [total])
        if last:
            operands += [pair, shift.reshape(1, -1)]
            scratch += [
                pltpu.VMEM((band * (cols + 1), zdim), jnp.float32),
                pltpu.VMEM(pair.shape, jnp.bfloat16),
                pltpu.SemaphoreType.DMA((band // 32,)),
            ]
        if not small:
            scratch.append(pltpu.VMEM((depth, 256), jnp.bfloat16))
        in_specs = [vmem] * len(operands)
        if not small:
            in_specs[len(blocks)] = anywhere
        return pl.pallas_call(
            functools.partial(_band_kernel, lines, len(blocks), total is None, count if last else None, small),
            in_specs=in_specs,
            out_specs=anywhere if last else vmem,
            out_shape=jax.ShapeDtypeStruct(pair.shape, jnp.bfloat16)
            if last
            else jax.ShapeDtypeStruct((band, cols * zdim), jnp.float32),
            scratch_shapes=scratch,
            compiler_params=params,
            cost_estimate=pl.CostEstimate(
                flops=2 * band * depth * cols * zdim, bytes_accessed=2 * depth * cols * zdim, transcendentals=0
            ),
        )(*operands)

    total = add([line, _xor(line, 1, n)], [(0, 0, False), (1, 1, False)], None, False)
    plane, total = lax.optimization_barrier((plane, total))
    other = _xor(plane, 1, n)
    total = add([plane], [(m, 0, True) for m in (2, 4, 6)], total, False)
    return add([other], [(m, 0, True) for m in (3, 5, 7)], total, True)


def solution(mesh):
    placed = (P(("group", "row"), None, None), P("group", "row", None)) + (P(),) * 8
    return jax.shard_map(
        functools.partial(shards, mesh.shape["row"]),
        mesh=mesh,
        in_specs=placed,
        out_specs=P("group", "row", None),
        check_vma=False,
    )
```

```python
import functools

import jax
import jax.numpy as jnp
from jax import lax
from jax.experimental import pallas as pl
from jax.experimental.pallas import tpu as pltpu
from jax.sharding import PartitionSpec as P

LANES = 128
CHANS = 32
NT = (((1,), (1,)), ((), ()))


def _stacked(weights, copies):
    c, q = weights.shape
    rows = []
    for k in range(copies):
        left = [jnp.zeros((c, k * q), weights.dtype)] if k else []
        right = [jnp.zeros((c, (copies - 1 - k) * q), weights.dtype)] if k < copies - 1 else []
        rows.append(jnp.concatenate(left + [weights] + right, axis=1))
    return jnp.concatenate(rows, axis=0)


def _project_kernel(*refs):
    sources, (left_ref, right_ref), held = refs[:7], refs[7:9], refs[9:16]
    sems = refs[16]
    copies = [pltpu.make_async_copy(a, b, sems.at[i]) for i, (a, b) in enumerate(zip(sources, held))]
    for copy in copies:
        copy.start()
    for copy in copies:
        copy.wait()
    x_ref, gain_ref, bias_ref, w1_ref, b1_ref, w2_ref, b2_ref = held
    band_half = left_ref.shape[0]
    n = right_ref.shape[0]
    feats = x_ref.shape[2]
    normed = []
    for s in range(2):
        x = x_ref[s].astype(jnp.float32)
        center = jnp.mean(x, axis=-1, keepdims=True)
        off = x - center
        spread = jnp.mean(off * off, axis=-1, keepdims=True)
        normed.append(off * lax.rsqrt(spread + 1e-05) * gain_ref[...] + bias_ref[...])
    low = [v[:band_half].astype(jnp.bfloat16) for v in normed]
    high = [v[band_half : 2 * band_half].astype(jnp.bfloat16) for v in normed]
    shift1 = jnp.concatenate([b1_ref[...]] * 4, axis=1)
    left = lax.dot_general(
        jnp.concatenate(low + high, axis=1), _stacked(w1_ref[...], 4), NT, preferred_element_type=jnp.float32
    )
    left_ref[...] = (left + shift1).astype(jnp.bfloat16)

    split = [v.reshape(n, 2, 8, feats) for v in normed]
    parts = [split[s][:, jh].reshape(n * 8, feats).astype(jnp.bfloat16) for jh in range(2) for s in range(2)]
    shift2 = jnp.concatenate([b2_ref[...]] * 4, axis=1)
    right = lax.dot_general(
        jnp.concatenate(parts, axis=1), _stacked(w2_ref[...], 4), NT, preferred_element_type=jnp.float32
    )
    right_ref[...] = (right + shift2).reshape(n, 8, LANES).astype(jnp.bfloat16)


def _order(me, half):
    row = lax.broadcasted_iota(jnp.int32, (4 * LANES, 8 * CHANS), 0)
    col = lax.broadcasted_iota(jnp.int32, (4 * LANES, 8 * CHANS), 1)
    device = (row // LANES) ^ (me // 8 % 4)
    wanted = (row % CHANS) * 8 + ((row // CHANS) % 2) * 4 + device
    hit = (wanted == col) & ((row // (2 * CHANS)) % 2 == half)
    return jnp.where(hit, 1.0, 0.0).astype(jnp.bfloat16)


def _fold_kernel(right_ref, source_ref, out_ref, order_ref, final_ref, sem):
    fetch = pltpu.make_async_copy(source_ref, final_ref, sem)
    fetch.start()
    me = lax.axis_index("row")
    for h in range(2):
        order_ref[h] = _order(me, h)
    devices = right_ref.shape[0]
    groups = devices // 4
    rows = devices * 8
    block = right_ref[...].astype(jnp.float32).reshape(rows, LANES)
    row = lax.broadcasted_iota(jnp.int32, (2 * rows, 2 * rows), 0)
    col = lax.broadcasted_iota(jnp.int32, (2 * rows, 2 * rows), 1)
    device = (row // 8) % groups + row % 4 * groups
    wanted = ((row // 4) % 2) * rows + device * 8 + row // (8 * groups)
    spread = jnp.where(wanted == col, 1.0, 0.0).astype(jnp.bfloat16)
    lane = lax.broadcasted_iota(jnp.int32, block.shape, 1) // CHANS
    lhs = []
    for jh in range(2):
        both = jnp.concatenate([jnp.where(lane == jh * 2 + s, block, 0.0) for s in range(2)], axis=0)
        moved = jnp.dot(spread, both.astype(jnp.bfloat16), preferred_element_type=jnp.float32)
        lhs.append(moved.astype(jnp.bfloat16))
    lhs = jnp.concatenate(lhs, axis=0)

    fetch.wait()
    for pair in range(CHANS // 2):
        rhs = []
        for k in range(2):
            at = pair * 2 * CHANS + k * CHANS
            rhs.append(jnp.concatenate([final_ref[pl.ds(at, CHANS), :]] * 4, axis=0))
        res = jnp.dot(lhs, jnp.concatenate(rhs, axis=1), preferred_element_type=jnp.float32)
        for j in range(16):
            for g in range(groups):
                r = (j * groups + g) * 8
                tile = jnp.concatenate([res[r : r + 8, :LANES], res[r : r + 8, LANES:]], axis=0)
                out_ref[g, 0, pl.ds(pair * 16, 16), pl.ds(j * LANES, LANES)] = tile.astype(jnp.bfloat16)


def _band_kernel(masks, begins, count, held, *refs):
    refs = list(refs)
    take = lambda k: [refs.pop(0) for _ in range(k)]
    lines = take(len(masks))
    t_ref, order_ref = take(2)
    (sum_ref,) = (None,) if begins else take(1)
    pair_ref, shift_ref = (None, None) if count is None else take(2)
    (out_ref,) = take(1)
    (l_ref,) = take(1)
    me = lax.axis_index("row")
    wide = 8 * CHANS
    places, half, _ = lines[0].shape
    chunks = []
    for line, mask in zip(lines, masks):
        for q in range(places // 4):
            lhs = jnp.concatenate([line[q * 4 + u] for u in range(4)], axis=1)
            at = pl.ds(len(chunks) * wide, wide)
            for h in range(2):
                moved = jnp.dot(lhs, order_ref[h], preferred_element_type=jnp.float32)
                l_ref[pl.ds(h * half, half), at] = moved.astype(jnp.bfloat16)
            chunks.append(((me % 8) ^ mask, q ^ (me // 32)))

    tile = 256
    band = 2 * half
    if count is not None:
        acc_ref, done_ref, sems = take(3)
        cols = pair_ref.shape[1]
        pitch = cols + 1

    def column(step):
        at = pl.ds(step * tile, tile)
        if held:
            rhs = jnp.concatenate([t_ref[g, q, :, at] for g, q in chunks], axis=0)
        else:
            for i, (g, q) in enumerate(chunks):
                pltpu.sync_copy(t_ref.at[g, q, :, at], refs[0].at[pl.ds(i * wide, wide)])
            rhs = refs[0][...]
        res = jnp.dot(l_ref[...], rhs, preferred_element_type=jnp.float32)
        if sum_ref is not None:
            res = res + sum_ref[:, at]
        if count is None:
            out_ref[:, at] = res
        else:
            for k in range(tile // LANES):
                j = step * (tile // LANES) + k
                acc_ref[pl.ds(j, band, stride=pitch), :] = res[:, k * LANES : (k + 1) * LANES]

    for step in range(t_ref.shape[3] // tile):
        column(step)
    if count is None:
        return

    rows = 32
    shift = shift_ref[...]

    def finish(r, _):
        for k in range(rows):
            i = r * rows + k
            total = acc_ref[pl.ds(i * pitch, cols), :] * (1.0 / count) + shift
            done_ref[i] = (pair_ref[i].astype(jnp.float32) + total).astype(jnp.bfloat16)
        at = pl.ds(pl.multiple_of(r * rows, rows), rows)
        pltpu.make_async_copy(done_ref.at[at], out_ref.at[at], sems.at[r]).start()
        return 0

    lax.fori_loop(0, band // rows, finish, 0)

    def drain(r, _):
        at = pl.ds(pl.multiple_of(r * rows, rows), rows)
        pltpu.make_async_copy(done_ref.at[at], out_ref.at[at], sems.at[r]).wait()
        return 0

    lax.fori_loop(0, band // rows, drain, 0)


def _xor(x, mask, n):
    return lax.ppermute(x, "row", [(i, i ^ mask) for i in range(n)])


def shards(n, alignment, pair, gain, bias, w1, b1, w2, b2, final, shift):
    seqs, residues, feats = alignment.shape
    band, cols, zdim = pair.shape
    half = band // 2
    count = float(seqs * n)
    small = n <= 32
    params = pltpu.CompilerParams(vmem_limit_bytes=(24 if small else 48) * 1024 * 1024)
    anywhere = pl.BlockSpec(memory_space=pl.ANY)
    vmem = pl.BlockSpec(memory_space=pltpu.VMEM)

    sources = [
        alignment, gain.reshape(1, -1), bias.reshape(1, -1), w1.T, b1.reshape(1, -1), w2.T, b2.reshape(1, -1)
    ]
    sources = [pltpu.with_memory_space_constraint(a, pltpu.HBM) for a in sources]
    left, right = pl.pallas_call(
        _project_kernel,
        in_specs=[pl.BlockSpec(memory_space=pltpu.HBM)] * 7,
        out_specs=(vmem, vmem),
        out_shape=(
            jax.ShapeDtypeStruct((half, LANES), jnp.bfloat16),
            jax.ShapeDtypeStruct((n, 8, LANES), jnp.bfloat16),
        ),
        scratch_shapes=[pltpu.VMEM(a.shape, a.dtype) for a in sources] + [pltpu.SemaphoreType.DMA((7,))],
        compiler_params=params,
        cost_estimate=pl.CostEstimate(
            flops=4 * seqs * residues * feats * CHANS, bytes_accessed=2 * seqs * residues * feats, transcendentals=0
        ),
    )(*sources)

    right = lax.all_to_all(right, "row", split_axis=0, concat_axis=0, tiled=True)

    line = [left] + [_xor(left, m, n) for m in range(8, n, 8)]
    line = jnp.stack(line)
    plane = [_xor(line, m, n) for m in (2, 4, 6)]

    part = 32
    parts = n // part
    fold_cost = pl.CostEstimate(
        flops=2 * n * 32 * 256 * CHANS * zdim, bytes_accessed=4 * n * CHANS * cols * zdim, transcendentals=0
    )
    fold_out = (
        jax.ShapeDtypeStruct((8, parts, 8 * CHANS, cols * zdim), jnp.bfloat16),
        jax.ShapeDtypeStruct((2, 4 * LANES, 8 * CHANS), jnp.bfloat16),
    )
    if small:
        specs = dict(in_specs=[vmem, anywhere], out_specs=(vmem, vmem))
    else:
        specs = dict(
            grid=(parts,),
            in_specs=[
                pl.BlockSpec((part, 8, LANES), lambda i: (i, 0, 0)),
                anywhere,
            ],
            out_specs=(
                pl.BlockSpec((8, 1, 8 * CHANS, cols * zdim), lambda i: (0, i, 0, 0)),
                pl.BlockSpec((2, 4 * LANES, 8 * CHANS), lambda i: (0, 0, 0)),
            ),
        )
    folded, order = pl.pallas_call(
        _fold_kernel,
        out_shape=fold_out,
        scratch_shapes=[pltpu.VMEM(final.shape, final.dtype), pltpu.SemaphoreType.DMA(())],
        compiler_params=params,
        cost_estimate=fold_cost,
        **specs,
    )(right, pltpu.with_memory_space_constraint(final, pltpu.HBM))

    def add(lines, masks, total, last):
        depth = len(masks) * parts * 8 * CHANS
        scratch = [pltpu.VMEM((band, depth), jnp.bfloat16)]
        operands = [*lines, folded, order] + ([] if total is None else [total])
        if last:
            operands += [pair, shift.reshape(1, -1)]
            scratch += [
                pltpu.VMEM((band * (cols + 1), zdim), jnp.float32),
                pltpu.VMEM(pair.shape, jnp.bfloat16),
                pltpu.SemaphoreType.DMA((band // 32,)),
            ]
        if not small:
            scratch.append(pltpu.VMEM((depth, 256), jnp.bfloat16))
        in_specs = [vmem] * len(operands)
        if not small:
            in_specs[len(lines)] = anywhere
        return pl.pallas_call(
            functools.partial(_band_kernel, masks, total is None, count if last else None, small),
            in_specs=in_specs,
            out_specs=anywhere if last else vmem,
            out_shape=jax.ShapeDtypeStruct(pair.shape, jnp.bfloat16)
            if last
            else jax.ShapeDtypeStruct((band, cols * zdim), jnp.float32),
            scratch_shapes=scratch,
            compiler_params=params,
            cost_estimate=pl.CostEstimate(
                flops=2 * band * depth * cols * zdim, bytes_accessed=2 * depth * cols * zdim, transcendentals=0
            ),
        )(*operands)

    sent, _ = lax.optimization_barrier((line, right))
    total = add([line, _xor(sent, 1, n)], (0, 1), None, False)
    diagonal, total = lax.optimization_barrier((plane[2], total))
    crossed = _xor(diagonal, 1, n)
    total = add([diagonal], (6,), total, False)
    x, y, total = lax.optimization_barrier((plane[0], plane[1], total))
    others = [_xor(x, 1, n), _xor(y, 1, n)]
    total = add([x, y, crossed], (2, 4, 7), total, False)
    return add(others, (3, 5), total, True)


def solution(mesh):
    placed = (P(("group", "row"), None, None), P("group", "row", None)) + (P(),) * 8
    return jax.shard_map(
        functools.partial(shards, mesh.shape["row"]),
        mesh=mesh,
        in_specs=placed,
        out_specs=P("group", "row", None),
        check_vma=False,
    )
```

```python
import functools

import jax
import jax.numpy as jnp
from jax import lax
from jax.experimental import pallas as pl
from jax.experimental.pallas import tpu as pltpu
from jax.sharding import PartitionSpec as P

LANES = 128
CHANS = 32
NT = (((1,), (1,)), ((), ()))


def _stacked(weights, copies):
    c, q = weights.shape
    rows = []
    for k in range(copies):
        left = [jnp.zeros((c, k * q), weights.dtype)] if k else []
        right = [jnp.zeros((c, (copies - 1 - k) * q), weights.dtype)] if k < copies - 1 else []
        rows.append(jnp.concatenate(left + [weights] + right, axis=1))
    return jnp.concatenate(rows, axis=0)


def _project_kernel(*refs):
    sources, (left_ref, right_ref), held = refs[:7], refs[7:9], refs[9:16]
    sems = refs[16]
    copies = [pltpu.make_async_copy(a, b, sems.at[i]) for i, (a, b) in enumerate(zip(sources, held))]
    for copy in copies:
        copy.start()
    for copy in copies:
        copy.wait()
    x_ref, gain_ref, bias_ref, w1_ref, b1_ref, w2_ref, b2_ref = held
    band_half = left_ref.shape[0]
    n = right_ref.shape[0]
    feats = x_ref.shape[2]
    normed = []
    for s in range(2):
        x = x_ref[s].astype(jnp.float32)
        center = jnp.mean(x, axis=-1, keepdims=True)
        off = x - center
        spread = jnp.mean(off * off, axis=-1, keepdims=True)
        normed.append(off * lax.rsqrt(spread + 1e-05) * gain_ref[...] + bias_ref[...])
    low = [v[:band_half].astype(jnp.bfloat16) for v in normed]
    high = [v[band_half : 2 * band_half].astype(jnp.bfloat16) for v in normed]
    shift1 = jnp.concatenate([b1_ref[...]] * 4, axis=1)
    left = lax.dot_general(
        jnp.concatenate(low + high, axis=1), _stacked(w1_ref[...], 4), NT, preferred_element_type=jnp.float32
    )
    left_ref[...] = (left + shift1).astype(jnp.bfloat16)

    split = [v.reshape(n, 2, 8, feats) for v in normed]
    parts = [split[s][:, jh].reshape(n * 8, feats).astype(jnp.bfloat16) for jh in range(2) for s in range(2)]
    shift2 = jnp.concatenate([b2_ref[...]] * 4, axis=1)
    right = lax.dot_general(
        jnp.concatenate(parts, axis=1), _stacked(w2_ref[...], 4), NT, preferred_element_type=jnp.float32
    )
    right_ref[...] = (right + shift2).reshape(n, 8, LANES).astype(jnp.bfloat16)


def _order(me, half):
    row = lax.broadcasted_iota(jnp.int32, (4 * LANES, 8 * CHANS), 0)
    col = lax.broadcasted_iota(jnp.int32, (4 * LANES, 8 * CHANS), 1)
    device = (row // LANES) ^ (me // 8 % 4)
    wanted = (row % CHANS) * 8 + ((row // CHANS) % 2) * 4 + device
    hit = (wanted == col) & ((row // (2 * CHANS)) % 2 == half)
    return jnp.where(hit, 1.0, 0.0).astype(jnp.bfloat16)


def _fold_kernel(right_ref, source_ref, out_ref, order_ref, final_ref, sem):
    fetch = pltpu.make_async_copy(source_ref, final_ref, sem)
    fetch.start()
    me = lax.axis_index("row")
    for h in range(2):
        order_ref[h] = _order(me, h)
    devices = right_ref.shape[0]
    groups = devices // 4
    rows = devices * 8
    block = right_ref[...].astype(jnp.float32).reshape(rows, LANES)
    row = lax.broadcasted_iota(jnp.int32, (2 * rows, 2 * rows), 0)
    col = lax.broadcasted_iota(jnp.int32, (2 * rows, 2 * rows), 1)
    device = (row // 8) % groups + row % 4 * groups
    wanted = ((row // 4) % 2) * rows + device * 8 + row // (8 * groups)
    spread = jnp.where(wanted == col, 1.0, 0.0).astype(jnp.bfloat16)
    lane = lax.broadcasted_iota(jnp.int32, block.shape, 1) // CHANS
    lhs = []
    for jh in range(2):
        both = jnp.concatenate([jnp.where(lane == jh * 2 + s, block, 0.0) for s in range(2)], axis=0)
        moved = jnp.dot(spread, both.astype(jnp.bfloat16), preferred_element_type=jnp.float32)
        lhs.append(moved.astype(jnp.bfloat16))
    lhs = jnp.concatenate(lhs, axis=0)

    fetch.wait()
    for pair in range(CHANS // 2):
        rhs = []
        for k in range(2):
            at = pair * 2 * CHANS + k * CHANS
            rhs.append(jnp.concatenate([final_ref[pl.ds(at, CHANS), :]] * 4, axis=0))
        res = jnp.dot(lhs, jnp.concatenate(rhs, axis=1), preferred_element_type=jnp.float32)
        for j in range(16):
            for g in range(groups):
                r = (j * groups + g) * 8
                tile = jnp.concatenate([res[r : r + 8, :LANES], res[r : r + 8, LANES:]], axis=0)
                out_ref[g, 0, pl.ds(pair * 16, 16), pl.ds(j * LANES, LANES)] = tile.astype(jnp.bfloat16)


def _band_kernel(masks, begins, count, held, *refs):
    refs = list(refs)
    take = lambda k: [refs.pop(0) for _ in range(k)]
    lines = take(len(masks))
    t_ref, order_ref = take(2)
    (sum_ref,) = (None,) if begins else take(1)
    pair_ref, shift_ref = (None, None) if count is None else take(2)
    (out_ref,) = take(1)
    (l_ref,) = take(1)
    me = lax.axis_index("row")
    wide = 8 * CHANS
    places, half, _ = lines[0].shape
    chunks = []
    for line, mask in zip(lines, masks):
        for q in range(places // 4):
            lhs = jnp.concatenate([line[q * 4 + u] for u in range(4)], axis=1)
            at = pl.ds(len(chunks) * wide, wide)
            for h in range(2):
                moved = jnp.dot(lhs, order_ref[h], preferred_element_type=jnp.float32)
                l_ref[pl.ds(h * half, half), at] = moved.astype(jnp.bfloat16)
            chunks.append(((me % 8) ^ mask, q ^ (me // 32)))

    tile = 256
    band = 2 * half
    if count is not None:
        acc_ref, done_ref, sems = take(3)
        cols = pair_ref.shape[1]
        pitch = cols + 1

    def column(step):
        at = pl.ds(step * tile, tile)
        if held:
            rhs = jnp.concatenate([t_ref[g, q, :, at] for g, q in chunks], axis=0)
        else:
            for i, (g, q) in enumerate(chunks):
                pltpu.sync_copy(t_ref.at[g, q, :, at], refs[0].at[pl.ds(i * wide, wide)])
            rhs = refs[0][...]
        res = jnp.dot(l_ref[...], rhs, preferred_element_type=jnp.float32)
        if sum_ref is not None:
            res = res + sum_ref[:, at]
        if count is None:
            out_ref[:, at] = res
        else:
            for k in range(tile // LANES):
                j = step * (tile // LANES) + k
                acc_ref[pl.ds(j, band, stride=pitch), :] = res[:, k * LANES : (k + 1) * LANES]

    for step in range(t_ref.shape[3] // tile):
        column(step)
    if count is None:
        return

    rows = 32
    shift = shift_ref[...]

    def finish(r, _):
        for k in range(rows):
            i = r * rows + k
            total = acc_ref[pl.ds(i * pitch, cols), :] * (1.0 / count) + shift
            done_ref[i] = (pair_ref[i].astype(jnp.float32) + total).astype(jnp.bfloat16)
        at = pl.ds(pl.multiple_of(r * rows, rows), rows)
        pltpu.make_async_copy(done_ref.at[at], out_ref.at[at], sems.at[r]).start()
        return 0

    lax.fori_loop(0, band // rows, finish, 0)

    def drain(r, _):
        at = pl.ds(pl.multiple_of(r * rows, rows), rows)
        pltpu.make_async_copy(done_ref.at[at], out_ref.at[at], sems.at[r]).wait()
        return 0

    lax.fori_loop(0, band // rows, drain, 0)


def _xor(x, mask, n):
    return lax.ppermute(x, "row", [(i, i ^ mask) for i in range(n)])


def shards(n, alignment, pair, gain, bias, w1, b1, w2, b2, final, shift):
    seqs, residues, feats = alignment.shape
    band, cols, zdim = pair.shape
    half = band // 2
    count = float(seqs * n)
    small = n <= 32
    params = pltpu.CompilerParams(vmem_limit_bytes=(24 if small else 48) * 1024 * 1024)
    anywhere = pl.BlockSpec(memory_space=pl.ANY)
    vmem = pl.BlockSpec(memory_space=pltpu.VMEM)

    sources = [
        alignment, gain.reshape(1, -1), bias.reshape(1, -1), w1.T, b1.reshape(1, -1), w2.T, b2.reshape(1, -1)
    ]
    sources = [pltpu.with_memory_space_constraint(a, pltpu.HBM) for a in sources]
    left, right = pl.pallas_call(
        _project_kernel,
        in_specs=[pl.BlockSpec(memory_space=pltpu.HBM)] * 7,
        out_specs=(vmem, vmem),
        out_shape=(
            jax.ShapeDtypeStruct((half, LANES), jnp.bfloat16),
            jax.ShapeDtypeStruct((n, 8, LANES), jnp.bfloat16),
        ),
        scratch_shapes=[pltpu.VMEM(a.shape, a.dtype) for a in sources] + [pltpu.SemaphoreType.DMA((7,))],
        compiler_params=params,
        cost_estimate=pl.CostEstimate(
            flops=4 * seqs * residues * feats * CHANS, bytes_accessed=2 * seqs * residues * feats, transcendentals=0
        ),
    )(*sources)

    right = lax.all_to_all(right, "row", split_axis=0, concat_axis=0, tiled=True)

    line = [left] + [_xor(left, m, n) for m in range(8, n, 8)]
    line = jnp.stack(line)
    plane = [_xor(line, m, n) for m in (2, 4, 6)]

    part = 32
    parts = n // part
    fold_cost = pl.CostEstimate(
        flops=2 * n * 32 * 256 * CHANS * zdim, bytes_accessed=4 * n * CHANS * cols * zdim, transcendentals=0
    )
    fold_out = (
        jax.ShapeDtypeStruct((8, parts, 8 * CHANS, cols * zdim), jnp.bfloat16),
        jax.ShapeDtypeStruct((2, 4 * LANES, 8 * CHANS), jnp.bfloat16),
    )
    if small:
        specs = dict(in_specs=[vmem, anywhere], out_specs=(vmem, vmem))
    else:
        specs = dict(
            grid=(parts,),
            in_specs=[
                pl.BlockSpec((part, 8, LANES), lambda i: (i, 0, 0)),
                anywhere,
            ],
            out_specs=(
                pl.BlockSpec((8, 1, 8 * CHANS, cols * zdim), lambda i: (0, i, 0, 0)),
                pl.BlockSpec((2, 4 * LANES, 8 * CHANS), lambda i: (0, 0, 0)),
            ),
        )
    folded, order = pl.pallas_call(
        _fold_kernel,
        out_shape=fold_out,
        scratch_shapes=[pltpu.VMEM(final.shape, final.dtype), pltpu.SemaphoreType.DMA(())],
        compiler_params=params,
        cost_estimate=fold_cost,
        **specs,
    )(right, pltpu.with_memory_space_constraint(final, pltpu.HBM))

    def add(lines, masks, total, last):
        depth = len(masks) * parts * 8 * CHANS
        scratch = [pltpu.VMEM((band, depth), jnp.bfloat16)]
        operands = [*lines, folded, order] + ([] if total is None else [total])
        if last:
            operands += [pair, shift.reshape(1, -1)]
            scratch += [
                pltpu.VMEM((band * (cols + 1), zdim), jnp.float32),
                pltpu.VMEM(pair.shape, jnp.bfloat16),
                pltpu.SemaphoreType.DMA((band // 32,)),
            ]
        if not small:
            scratch.append(pltpu.VMEM((depth, 256), jnp.bfloat16))
        in_specs = [vmem] * len(operands)
        if not small:
            in_specs[len(lines)] = anywhere
        return pl.pallas_call(
            functools.partial(_band_kernel, masks, total is None, count if last else None, small),
            in_specs=in_specs,
            out_specs=anywhere if last else vmem,
            out_shape=jax.ShapeDtypeStruct(pair.shape, jnp.bfloat16)
            if last
            else jax.ShapeDtypeStruct((band, cols * zdim), jnp.float32),
            scratch_shapes=scratch,
            compiler_params=params,
            cost_estimate=pl.CostEstimate(
                flops=2 * band * depth * cols * zdim, bytes_accessed=2 * depth * cols * zdim, transcendentals=0
            ),
        )(*operands)

    total = add([line, _xor(line, 1, n)], (0, 1), None, False)
    diagonal, total = lax.optimization_barrier((plane[2], total))
    crossed = _xor(diagonal, 1, n)
    total = add([diagonal], (6,), total, False)
    x, y, total = lax.optimization_barrier((plane[0], plane[1], total))
    others = [_xor(x, 1, n), _xor(y, 1, n)]
    total = add([x, y, crossed], (2, 4, 7), total, False)
    return add(others, (3, 5), total, True)


def solution(mesh):
    placed = (P(("group", "row"), None, None), P("group", "row", None)) + (P(),) * 8
    return jax.shard_map(
        functools.partial(shards, mesh.shape["row"]),
        mesh=mesh,
        in_specs=placed,
        out_specs=P("group", "row", None),
        check_vma=False,
    )
```

```python
import functools

import jax
import jax.numpy as jnp
from jax import lax
from jax.experimental import pallas as pl
from jax.experimental.pallas import tpu as pltpu
from jax.sharding import PartitionSpec as P

LANES = 128
CHANS = 32
NT = (((1,), (1,)), ((), ()))


def _stacked(weights, copies):
    c, q = weights.shape
    rows = []
    for k in range(copies):
        left = [jnp.zeros((c, k * q), weights.dtype)] if k else []
        right = [jnp.zeros((c, (copies - 1 - k) * q), weights.dtype)] if k < copies - 1 else []
        rows.append(jnp.concatenate(left + [weights] + right, axis=1))
    return jnp.concatenate(rows, axis=0)


def _order(me, half):
    row = lax.broadcasted_iota(jnp.int32, (4 * LANES, 8 * CHANS), 0)
    col = lax.broadcasted_iota(jnp.int32, (4 * LANES, 8 * CHANS), 1)
    device = (row // LANES) ^ (me // 8 % 4)
    wanted = (row % CHANS) * 8 + ((row // CHANS) % 2) * 4 + device
    hit = (wanted == col) & ((row // (2 * CHANS)) % 2 == half)
    return jnp.where(hit, 1.0, 0.0).astype(jnp.bfloat16)


def _project_kernel(*refs):
    sources, final_source, outs, held = refs[:7], refs[7], refs[8:12], refs[12:19]
    left_ref, right_ref, final_ref, order_ref = outs
    sems = refs[19]
    copies = [pltpu.make_async_copy(a, b, sems.at[i]) for i, (a, b) in enumerate(zip(sources, held))]
    copies.append(pltpu.make_async_copy(final_source, final_ref, sems.at[7]))
    for copy in copies:
        copy.start()
    me = lax.axis_index("row")
    for h in range(2):
        order_ref[h] = _order(me, h)
    for copy in copies:
        copy.wait()
    x_ref, gain_ref, bias_ref, w1_ref, b1_ref, w2_ref, b2_ref = held
    band_half = left_ref.shape[0]
    n = right_ref.shape[0]
    feats = x_ref.shape[2]
    normed = []
    for s in range(2):
        x = x_ref[s].astype(jnp.float32)
        center = jnp.mean(x, axis=-1, keepdims=True)
        off = x - center
        spread = jnp.mean(off * off, axis=-1, keepdims=True)
        normed.append(off * lax.rsqrt(spread + 1e-05) * gain_ref[...] + bias_ref[...])
    low = [v[:band_half].astype(jnp.bfloat16) for v in normed]
    high = [v[band_half : 2 * band_half].astype(jnp.bfloat16) for v in normed]
    shift1 = jnp.concatenate([b1_ref[...]] * 4, axis=1)
    left = lax.dot_general(
        jnp.concatenate(low + high, axis=1), _stacked(w1_ref[...], 4), NT, preferred_element_type=jnp.float32
    )
    left_ref[...] = (left + shift1).astype(jnp.bfloat16)

    split = [v.reshape(n, 2, 8, feats) for v in normed]
    parts = [split[s][:, jh].reshape(n * 8, feats).astype(jnp.bfloat16) for jh in range(2) for s in range(2)]
    shift2 = jnp.concatenate([b2_ref[...]] * 4, axis=1)
    right = lax.dot_general(
        jnp.concatenate(parts, axis=1), _stacked(w2_ref[...], 4), NT, preferred_element_type=jnp.float32
    )
    right_ref[...] = (right + shift2).reshape(n, 8, LANES).astype(jnp.bfloat16)


def _line_kernel(*refs):
    pieces, order_ref, out_ref = refs[:-2], refs[-2], refs[-1]
    half = pieces[0].shape[0]
    wide = order_ref.shape[2]
    for q in range(len(pieces) // 4):
        lhs = jnp.concatenate([piece[...] for piece in pieces[q * 4 : q * 4 + 4]], axis=1)
        for h in range(2):
            moved = jnp.dot(lhs, order_ref[h], preferred_element_type=jnp.float32)
            out_ref[pl.ds(h * half, half), pl.ds(q * wide, wide)] = moved.astype(jnp.bfloat16)


def _fold_kernel(right_ref, final_ref, out_ref, block_ref, pairs_ref):
    devices = right_ref.shape[0]
    groups = devices // 4
    block_ref[...] = right_ref[...].astype(jnp.float32).reshape(devices * 8, LANES)
    for jr in range(8):
        for g in range(groups):
            four = block_ref[pl.ds(g * 8 + jr, 4, stride=groups * 8), :]
            for s in range(2):
                pairs_ref[pl.ds((jr * groups + g) * 8 + s * 4, 4), :] = four
    block = pairs_ref[...]
    lane = lax.broadcasted_iota(jnp.int32, block.shape, 1) // CHANS
    s = lax.broadcasted_iota(jnp.int32, block.shape, 0) // 4 % 2
    lhs = [jnp.where(lane == jh * 2 + s, block, 0.0).astype(jnp.bfloat16) for jh in range(2)]
    lhs = jnp.concatenate(lhs, axis=0)

    for pair in range(CHANS // 2):
        rhs = []
        for k in range(2):
            at = pair * 2 * CHANS + k * CHANS
            rhs.append(jnp.concatenate([final_ref[pl.ds(at, CHANS), :]] * 4, axis=0))
        res = jnp.dot(lhs, jnp.concatenate(rhs, axis=1), preferred_element_type=jnp.float32)
        for j in range(16):
            for g in range(groups):
                r = (j * groups + g) * 8
                tile = jnp.concatenate([res[r : r + 8, :LANES], res[r : r + 8, LANES:]], axis=0)
                out_ref[g, 0, pl.ds(pair * 16, 16), pl.ds(j * LANES, LANES)] = tile.astype(jnp.bfloat16)


def _band_kernel(masks, begins, count, held, *refs):
    refs = list(refs)
    take = lambda k: [refs.pop(0) for _ in range(k)]
    lines = []
    for mask in masks:
        parts = take(2 if mask == 6 else 1)
        lines.append(parts)
    (t_ref,) = take(1)
    (sum_ref,) = (None,) if begins else take(1)
    pair_ref, shift_ref = (None, None) if count is None else take(2)
    (out_ref,) = take(1)
    me = lax.axis_index("row")
    wide = t_ref.shape[2]
    chunks = [((me % 8) ^ mask, q ^ (me // 32)) for mask in masks for q in range(t_ref.shape[1])]

    tile = 256
    band = sum(part.shape[0] for part in lines[0])
    if count is not None:
        acc_ref, done_ref, sems = take(3)
        cols = pair_ref.shape[1]
        pitch = cols + 1

    def column(step):
        at = pl.ds(step * tile, tile)
        lhs = jnp.concatenate([jnp.concatenate([part[...] for part in line], axis=0) for line in lines], axis=1)
        if held:
            rhs = jnp.concatenate([t_ref[g, q, :, at] for g, q in chunks], axis=0)
        else:
            for i, (g, q) in enumerate(chunks):
                pltpu.sync_copy(t_ref.at[g, q, :, at], refs[0].at[pl.ds(i * wide, wide)])
            rhs = refs[0][...]
        res = jnp.dot(lhs, rhs, preferred_element_type=jnp.float32)
        if sum_ref is not None:
            res = res + sum_ref[:, at]
        if count is None:
            out_ref[:, at] = res
        else:
            for k in range(tile // LANES):
                j = step * (tile // LANES) + k
                acc_ref[pl.ds(j, band, stride=pitch), :] = res[:, k * LANES : (k + 1) * LANES]

    for step in range(t_ref.shape[3] // tile):
        column(step)
    if count is None:
        return

    rows = 32
    shift = shift_ref[...]

    def finish(r, _):
        for k in range(rows):
            i = r * rows + k
            total = acc_ref[pl.ds(i * pitch, cols), :] * (1.0 / count) + shift
            done_ref[i] = (pair_ref[i].astype(jnp.float32) + total).astype(jnp.bfloat16)
        at = pl.ds(pl.multiple_of(r * rows, rows), rows)
        pltpu.make_async_copy(done_ref.at[at], out_ref.at[at], sems.at[r]).start()
        return 0

    lax.fori_loop(0, band // rows, finish, 0)

    def drain(r, _):
        at = pl.ds(pl.multiple_of(r * rows, rows), rows)
        pltpu.make_async_copy(done_ref.at[at], out_ref.at[at], sems.at[r]).wait()
        return 0

    lax.fori_loop(0, band // rows, drain, 0)


def _xor(x, mask, n):
    return lax.ppermute(x, "row", [(i, i ^ mask) for i in range(n)])


def shards(n, alignment, pair, gain, bias, w1, b1, w2, b2, final, shift):
    seqs, residues, feats = alignment.shape
    band, cols, zdim = pair.shape
    half = band // 2
    count = float(seqs * n)
    small = n <= 32
    params = pltpu.CompilerParams(vmem_limit_bytes=(24 if small else 48) * 1024 * 1024)
    anywhere = pl.BlockSpec(memory_space=pl.ANY)
    vmem = pl.BlockSpec(memory_space=pltpu.VMEM)

    sources = [
        alignment, gain.reshape(1, -1), bias.reshape(1, -1), w1.T, b1.reshape(1, -1), w2.T, b2.reshape(1, -1)
    ]
    sources = [pltpu.with_memory_space_constraint(a, pltpu.HBM) for a in sources]
    left, right, final, order = pl.pallas_call(
        _project_kernel,
        in_specs=[anywhere] * 8,
        out_specs=(vmem,) * 4,
        out_shape=(
            jax.ShapeDtypeStruct((half, LANES), jnp.bfloat16),
            jax.ShapeDtypeStruct((n, 8, LANES), jnp.bfloat16),
            jax.ShapeDtypeStruct(final.shape, final.dtype),
            jax.ShapeDtypeStruct((2, 4 * LANES, 8 * CHANS), jnp.bfloat16),
        ),
        scratch_shapes=[pltpu.VMEM(a.shape, a.dtype) for a in sources] + [pltpu.SemaphoreType.DMA((8,))],
        compiler_params=params,
        cost_estimate=pl.CostEstimate(
            flops=4 * seqs * residues * feats * CHANS, bytes_accessed=2 * seqs * residues * feats, transcendentals=0
        ),
    )(*sources, pltpu.with_memory_space_constraint(final, pltpu.HBM))

    right = lax.all_to_all(right, "row", split_axis=0, concat_axis=0, tiled=True)

    part = 32
    parts = n // part
    pieces = [left] + [_xor(left, m, n) for m in range(8, n, 8)]
    line = pl.pallas_call(
        _line_kernel,
        in_specs=[vmem] * (len(pieces) + 1),
        out_specs=vmem,
        out_shape=jax.ShapeDtypeStruct((band, parts * 8 * CHANS), jnp.bfloat16),
        compiler_params=params,
        cost_estimate=pl.CostEstimate(flops=2**27, bytes_accessed=2**20, transcendentals=0),
    )(*pieces, order)
    x, y = _xor(line, 2, n), _xor(line, 4, n)

    fold_cost = pl.CostEstimate(
        flops=2 * n * 32 * 256 * CHANS * zdim, bytes_accessed=4 * n * CHANS * cols * zdim, transcendentals=0
    )
    fold_out = jax.ShapeDtypeStruct((8, parts, 8 * CHANS, cols * zdim), jnp.bfloat16)
    if small:
        specs = dict(in_specs=[vmem, vmem], out_specs=vmem)
    else:
        specs = dict(
            grid=(parts,),
            in_specs=[
                pl.BlockSpec((part, 8, LANES), lambda i: (i, 0, 0)),
                pl.BlockSpec(final.shape, lambda i: (0, 0)),
            ],
            out_specs=pl.BlockSpec((8, 1, 8 * CHANS, cols * zdim), lambda i: (0, i, 0, 0)),
        )
    folded = pl.pallas_call(
        _fold_kernel,
        out_shape=fold_out,
        scratch_shapes=[pltpu.VMEM((part * 8, LANES), jnp.float32), pltpu.VMEM((part * 16, LANES), jnp.float32)],
        compiler_params=params,
        cost_estimate=fold_cost,
        **specs,
    )(right, final)

    def add(lines, masks, total, last):
        depth = len(masks) * parts * 8 * CHANS
        scratch = []
        operands = [*lines, folded] + ([] if total is None else [total])
        if last:
            operands += [pair, shift.reshape(1, -1)]
            scratch += [
                pltpu.VMEM((band * (cols + 1), zdim), jnp.float32),
                pltpu.VMEM(pair.shape, jnp.bfloat16),
                pltpu.SemaphoreType.DMA((band // 32,)),
            ]
        if not small:
            scratch.append(pltpu.VMEM((depth, 256), jnp.bfloat16))
        in_specs = [vmem] * len(operands)
        if not small:
            in_specs[len(lines)] = anywhere
        return pl.pallas_call(
            functools.partial(_band_kernel, masks, total is None, count if last else None, small),
            in_specs=in_specs,
            out_specs=anywhere if last else vmem,
            out_shape=jax.ShapeDtypeStruct(pair.shape, jnp.bfloat16)
            if last
            else jax.ShapeDtypeStruct((band, cols * zdim), jnp.float32),
            scratch_shapes=scratch,
            compiler_params=params,
            cost_estimate=pl.CostEstimate(
                flops=2 * band * depth * cols * zdim, bytes_accessed=2 * depth * cols * zdim, transcendentals=0
            ),
        )(*operands)

    total = add([line, _xor(line, 1, n)], (0, 1), None, False)
    x, y, total = lax.optimization_barrier((x, y, total))
    upper, lower = _xor(x[:half], 4, n), _xor(y[half:], 2, n)
    total = add([x, y], (2, 4), total, False)
    x, y, total = lax.optimization_barrier((x, y, total))
    across = [_xor(x, 1, n), _xor(y, 1, n)]
    total = add(across, (3, 5), total, False)
    upper, lower, total = lax.optimization_barrier((upper, lower, total))
    last = _xor(jnp.concatenate([upper, lower], axis=0), 1, n)
    total = add([upper, lower], (6,), total, False)
    return add([last], (7,), total, True)


def solution(mesh):
    placed = (P(("group", "row"), None, None), P("group", "row", None)) + (P(),) * 8
    return jax.shard_map(
        functools.partial(shards, mesh.shape["row"]),
        mesh=mesh,
        in_specs=placed,
        out_specs=P("group", "row", None),
        check_vma=False,
    )
```

```python
import functools

import jax
import jax.numpy as jnp
from jax import lax
from jax.experimental import pallas as pl
from jax.experimental.pallas import tpu as pltpu
from jax.sharding import PartitionSpec as P

LANES = 128
CHANS = 32
NT = (((1,), (1,)), ((), ()))


def _stacked(weights, copies):
    c, q = weights.shape
    rows = []
    for k in range(copies):
        left = [jnp.zeros((c, k * q), weights.dtype)] if k else []
        right = [jnp.zeros((c, (copies - 1 - k) * q), weights.dtype)] if k < copies - 1 else []
        rows.append(jnp.concatenate(left + [weights] + right, axis=1))
    return jnp.concatenate(rows, axis=0)


def _order(me, half):
    row = lax.broadcasted_iota(jnp.int32, (4 * LANES, 8 * CHANS), 0)
    col = lax.broadcasted_iota(jnp.int32, (4 * LANES, 8 * CHANS), 1)
    device = (row // LANES) ^ (me // 8 % 4)
    wanted = (row % CHANS) * 8 + ((row // CHANS) % 2) * 4 + device
    hit = (wanted == col) & ((row // (2 * CHANS)) % 2 == half)
    return jnp.where(hit, 1.0, 0.0).astype(jnp.bfloat16)


def _project_kernel(*refs):
    sources, final_source, outs, held = refs[:7], refs[7], refs[8:12], refs[12:19]
    left_ref, right_ref, final_ref, order_ref = outs
    sems = refs[19]
    copies = [pltpu.make_async_copy(a, b, sems.at[i]) for i, (a, b) in enumerate(zip(sources, held))]
    copies.append(pltpu.make_async_copy(final_source, final_ref, sems.at[7]))
    for copy in copies:
        copy.start()
    me = lax.axis_index("row")
    for h in range(2):
        order_ref[h] = _order(me, h)
    for copy in copies:
        copy.wait()
    x_ref, gain_ref, bias_ref, w1_ref, b1_ref, w2_ref, b2_ref = held
    band_half = left_ref.shape[0]
    n = right_ref.shape[0]
    feats = x_ref.shape[2]
    normed = []
    for s in range(2):
        x = x_ref[s].astype(jnp.float32)
        center = jnp.mean(x, axis=-1, keepdims=True)
        off = x - center
        spread = jnp.mean(off * off, axis=-1, keepdims=True)
        normed.append(off * lax.rsqrt(spread + 1e-05) * gain_ref[...] + bias_ref[...])
    low = [v[:band_half].astype(jnp.bfloat16) for v in normed]
    high = [v[band_half : 2 * band_half].astype(jnp.bfloat16) for v in normed]
    shift1 = jnp.concatenate([b1_ref[...]] * 4, axis=1)
    left = lax.dot_general(
        jnp.concatenate(low + high, axis=1), _stacked(w1_ref[...], 4), NT, preferred_element_type=jnp.float32
    )
    left_ref[...] = (left + shift1).astype(jnp.bfloat16)

    split = [v.reshape(n, 2, 8, feats) for v in normed]
    parts = [split[s][:, jh].reshape(n * 8, feats).astype(jnp.bfloat16) for jh in range(2) for s in range(2)]
    shift2 = jnp.concatenate([b2_ref[...]] * 4, axis=1)
    right = lax.dot_general(
        jnp.concatenate(parts, axis=1), _stacked(w2_ref[...], 4), NT, preferred_element_type=jnp.float32
    )
    right_ref[...] = (right + shift2).reshape(n, 8, LANES).astype(jnp.bfloat16)


def _line_kernel(*refs):
    pieces, order_ref, out_ref = refs[:-2], refs[-2], refs[-1]
    half = pieces[0].shape[0]
    wide = order_ref.shape[2]
    for q in range(len(pieces) // 4):
        lhs = jnp.concatenate([piece[...] for piece in pieces[q * 4 : q * 4 + 4]], axis=1)
        for h in range(2):
            moved = jnp.dot(lhs, order_ref[h], preferred_element_type=jnp.float32)
            out_ref[pl.ds(h * half, half), pl.ds(q * wide, wide)] = moved.astype(jnp.bfloat16)


def _fold_kernel(right_ref, final_ref, out_ref, block_ref, pairs_ref):
    devices = right_ref.shape[0]
    groups = devices // 4
    block_ref[...] = right_ref[...].astype(jnp.float32).reshape(devices * 8, LANES)
    for jr in range(8):
        for g in range(groups):
            four = block_ref[pl.ds(g * 8 + jr, 4, stride=groups * 8), :]
            for s in range(2):
                pairs_ref[pl.ds((jr * groups + g) * 8 + s * 4, 4), :] = four
    block = pairs_ref[...]
    lane = lax.broadcasted_iota(jnp.int32, block.shape, 1) // CHANS
    s = lax.broadcasted_iota(jnp.int32, block.shape, 0) // 4 % 2
    lhs = [jnp.where(lane == jh * 2 + s, block, 0.0).astype(jnp.bfloat16) for jh in range(2)]
    lhs = jnp.concatenate(lhs, axis=0)

    for pair in range(CHANS // 2):
        rhs = []
        for k in range(2):
            at = pair * 2 * CHANS + k * CHANS
            rhs.append(jnp.concatenate([final_ref[pl.ds(at, CHANS), :]] * 4, axis=0))
        res = jnp.dot(lhs, jnp.concatenate(rhs, axis=1), preferred_element_type=jnp.float32)
        for j in range(16):
            for g in range(groups):
                r = (j * groups + g) * 8
                tile = jnp.concatenate([res[r : r + 8, :LANES], res[r : r + 8, LANES:]], axis=0)
                out_ref[g, 0, pl.ds(pair * 16, 16), pl.ds(j * LANES, LANES)] = tile.astype(jnp.bfloat16)


def _band_kernel(masks, begins, count, held, *refs):
    refs = list(refs)
    take = lambda k: [refs.pop(0) for _ in range(k)]
    if masks == (1, 3, 5):
        (block,) = take(1)
        lines = [[block.at[k]] for k in range(3)]
    else:
        lines = [take(2 if mask == 6 else 1) for mask in masks]
    (t_ref,) = take(1)
    (sum_ref,) = (None,) if begins else take(1)
    pair_ref, shift_ref = (None, None) if count is None else take(2)
    (out_ref,) = take(1)
    me = lax.axis_index("row")
    wide = t_ref.shape[2]
    chunks = [((me % 8) ^ mask, q ^ (me // 32)) for mask in masks for q in range(t_ref.shape[1])]

    tile = 256
    band = sum(part.shape[0] for part in lines[0])
    if count is not None:
        acc_ref, done_ref, sems = take(3)
        cols = pair_ref.shape[1]
        pitch = cols + 1

    def column(step):
        at = pl.ds(step * tile, tile)
        lhs = jnp.concatenate([jnp.concatenate([part[...] for part in line], axis=0) for line in lines], axis=1)
        if held:
            rhs = jnp.concatenate([t_ref[g, q, :, at] for g, q in chunks], axis=0)
        else:
            for i, (g, q) in enumerate(chunks):
                pltpu.sync_copy(t_ref.at[g, q, :, at], refs[0].at[pl.ds(i * wide, wide)])
            rhs = refs[0][...]
        res = jnp.dot(lhs, rhs, preferred_element_type=jnp.float32)
        if sum_ref is not None:
            res = res + sum_ref[:, at]
        if count is None:
            out_ref[:, at] = res
        else:
            for k in range(tile // LANES):
                j = step * (tile // LANES) + k
                acc_ref[pl.ds(j, band, stride=pitch), :] = res[:, k * LANES : (k + 1) * LANES]

    for step in range(t_ref.shape[3] // tile):
        column(step)
    if count is None:
        return

    rows = 32
    shift = shift_ref[...]

    def finish(r, _):
        for k in range(rows):
            i = r * rows + k
            total = acc_ref[pl.ds(i * pitch, cols), :] * (1.0 / count) + shift
            done_ref[i] = (pair_ref[i].astype(jnp.float32) + total).astype(jnp.bfloat16)
        at = pl.ds(pl.multiple_of(r * rows, rows), rows)
        pltpu.make_async_copy(done_ref.at[at], out_ref.at[at], sems.at[r]).start()
        return 0

    lax.fori_loop(0, band // rows, finish, 0)

    def drain(r, _):
        at = pl.ds(pl.multiple_of(r * rows, rows), rows)
        pltpu.make_async_copy(done_ref.at[at], out_ref.at[at], sems.at[r]).wait()
        return 0

    lax.fori_loop(0, band // rows, drain, 0)


def _xor(x, mask, n):
    return lax.ppermute(x, "row", [(i, i ^ mask) for i in range(n)])


def shards(n, alignment, pair, gain, bias, w1, b1, w2, b2, final, shift):
    seqs, residues, feats = alignment.shape
    band, cols, zdim = pair.shape
    half = band // 2
    count = float(seqs * n)
    small = n <= 32
    params = pltpu.CompilerParams(vmem_limit_bytes=(24 if small else 48) * 1024 * 1024)
    anywhere = pl.BlockSpec(memory_space=pl.ANY)
    vmem = pl.BlockSpec(memory_space=pltpu.VMEM)

    sources = [
        alignment, gain.reshape(1, -1), bias.reshape(1, -1), w1.T, b1.reshape(1, -1), w2.T, b2.reshape(1, -1)
    ]
    sources = [pltpu.with_memory_space_constraint(a, pltpu.HBM) for a in sources]
    left, right, final, order = pl.pallas_call(
        _project_kernel,
        in_specs=[anywhere] * 8,
        out_specs=(vmem,) * 4,
        out_shape=(
            jax.ShapeDtypeStruct((half, LANES), jnp.bfloat16),
            jax.ShapeDtypeStruct((n, 8, LANES), jnp.bfloat16),
            jax.ShapeDtypeStruct(final.shape, final.dtype),
            jax.ShapeDtypeStruct((2, 4 * LANES, 8 * CHANS), jnp.bfloat16),
        ),
        scratch_shapes=[pltpu.VMEM(a.shape, a.dtype) for a in sources] + [pltpu.SemaphoreType.DMA((8,))],
        compiler_params=params,
        cost_estimate=pl.CostEstimate(
            flops=4 * seqs * residues * feats * CHANS, bytes_accessed=2 * seqs * residues * feats, transcendentals=0
        ),
    )(*sources, pltpu.with_memory_space_constraint(final, pltpu.HBM))

    right = lax.all_to_all(right, "row", split_axis=0, concat_axis=0, tiled=True)

    part = 32
    parts = n // part
    pieces = [left] + [_xor(left, m, n) for m in range(8, n, 8)]
    line = pl.pallas_call(
        _line_kernel,
        in_specs=[vmem] * (len(pieces) + 1),
        out_specs=vmem,
        out_shape=jax.ShapeDtypeStruct((band, parts * 8 * CHANS), jnp.bfloat16),
        compiler_params=params,
        cost_estimate=pl.CostEstimate(flops=2**27, bytes_accessed=2**20, transcendentals=0),
    )(*pieces, order)
    x, y = _xor(line, 2, n), _xor(line, 4, n)

    fold_cost = pl.CostEstimate(
        flops=2 * n * 32 * 256 * CHANS * zdim, bytes_accessed=4 * n * CHANS * cols * zdim, transcendentals=0
    )
    fold_out = jax.ShapeDtypeStruct((8, parts, 8 * CHANS, cols * zdim), jnp.bfloat16)
    if small:
        specs = dict(in_specs=[vmem, vmem], out_specs=vmem)
    else:
        specs = dict(
            grid=(parts,),
            in_specs=[
                pl.BlockSpec((part, 8, LANES), lambda i: (i, 0, 0)),
                pl.BlockSpec(final.shape, lambda i: (0, 0)),
            ],
            out_specs=pl.BlockSpec((8, 1, 8 * CHANS, cols * zdim), lambda i: (0, i, 0, 0)),
        )
    folded = pl.pallas_call(
        _fold_kernel,
        out_shape=fold_out,
        scratch_shapes=[pltpu.VMEM((part * 8, LANES), jnp.float32), pltpu.VMEM((part * 16, LANES), jnp.float32)],
        compiler_params=params,
        cost_estimate=fold_cost,
        **specs,
    )(right, final)

    def add(lines, masks, total, last):
        depth = len(masks) * parts * 8 * CHANS
        scratch = []
        operands = [*lines, folded] + ([] if total is None else [total])
        if last:
            operands += [pair, shift.reshape(1, -1)]
            scratch += [
                pltpu.VMEM((band * (cols + 1), zdim), jnp.float32),
                pltpu.VMEM(pair.shape, jnp.bfloat16),
                pltpu.SemaphoreType.DMA((band // 32,)),
            ]
        if not small:
            scratch.append(pltpu.VMEM((depth, 256), jnp.bfloat16))
        in_specs = [vmem] * len(operands)
        if not small:
            in_specs[len(lines)] = anywhere
        return pl.pallas_call(
            functools.partial(_band_kernel, masks, total is None, count if last else None, small),
            in_specs=in_specs,
            out_specs=anywhere if last else vmem,
            out_shape=jax.ShapeDtypeStruct(pair.shape, jnp.bfloat16)
            if last
            else jax.ShapeDtypeStruct((band, cols * zdim), jnp.float32),
            scratch_shapes=scratch,
            compiler_params=params,
            cost_estimate=pl.CostEstimate(
                flops=band * cols * zdim, bytes_accessed=band * cols, transcendentals=0
            ),
        )(*operands)

    x, y, folded = lax.optimization_barrier((x, y, folded))
    upper, lower = _xor(x[:half], 4, n), _xor(y[half:], 2, n)
    across = _xor(jnp.stack([line, x, y]), 1, n)
    total = add([line, x, y], (0, 2, 4), None, False)
    total = add([across], (1, 3, 5), total, False)
    upper, lower, total = lax.optimization_barrier((upper, lower, total))
    last = _xor(jnp.concatenate([upper, lower], axis=0), 1, n)
    total = add([upper, lower], (6,), total, False)
    return add([last], (7,), total, True)


def solution(mesh):
    placed = (P(("group", "row"), None, None), P("group", "row", None)) + (P(),) * 8
    return jax.shard_map(
        functools.partial(shards, mesh.shape["row"]),
        mesh=mesh,
        in_specs=placed,
        out_specs=P("group", "row", None),
        check_vma=False,
    )
```

```python
import functools

import jax
import jax.numpy as jnp
from jax import lax
from jax.experimental import pallas as pl
from jax.experimental.pallas import tpu as pltpu
from jax.sharding import PartitionSpec as P

LANES = 128
CHANS = 32
NT = (((1,), (1,)), ((), ()))


def _stacked(weights, copies):
    c, q = weights.shape
    rows = []
    for k in range(copies):
        left = [jnp.zeros((c, k * q), weights.dtype)] if k else []
        right = [jnp.zeros((c, (copies - 1 - k) * q), weights.dtype)] if k < copies - 1 else []
        rows.append(jnp.concatenate(left + [weights] + right, axis=1))
    return jnp.concatenate(rows, axis=0)


def _order(me, half):
    row = lax.broadcasted_iota(jnp.int32, (4 * LANES, 8 * CHANS), 0)
    col = lax.broadcasted_iota(jnp.int32, (4 * LANES, 8 * CHANS), 1)
    device = (row // LANES) ^ (me // 8 % 4)
    wanted = (row % CHANS) * 8 + ((row // CHANS) % 2) * 4 + device
    hit = (wanted == col) & ((row // (2 * CHANS)) % 2 == half)
    return jnp.where(hit, 1.0, 0.0).astype(jnp.bfloat16)


def _project_kernel(*refs):
    sources, final_source, outs, held = refs[:7], refs[7], refs[8:12], refs[12:19]
    left_ref, right_ref, final_ref, order_ref = outs
    sems = refs[19]
    copies = [pltpu.make_async_copy(a, b, sems.at[i]) for i, (a, b) in enumerate(zip(sources, held))]
    copies.append(pltpu.make_async_copy(final_source, final_ref, sems.at[7]))
    for copy in copies:
        copy.start()
    me = lax.axis_index("row")
    for h in range(2):
        order_ref[h] = _order(me, h)
    for copy in copies:
        copy.wait()
    x_ref, gain_ref, bias_ref, w1_ref, b1_ref, w2_ref, b2_ref = held
    band_half = left_ref.shape[0]
    n = right_ref.shape[0] * 2
    feats = x_ref.shape[2]
    normed = []
    for s in range(2):
        x = x_ref[s].astype(jnp.float32)
        center = jnp.mean(x, axis=-1, keepdims=True)
        off = x - center
        spread = jnp.mean(off * off, axis=-1, keepdims=True)
        normed.append(off * lax.rsqrt(spread + 1e-05) * gain_ref[...] + bias_ref[...])
    low = [v[:band_half].astype(jnp.bfloat16) for v in normed]
    high = [v[band_half : 2 * band_half].astype(jnp.bfloat16) for v in normed]
    shift1 = jnp.concatenate([b1_ref[...]] * 4, axis=1)
    left = lax.dot_general(
        jnp.concatenate(low + high, axis=1), _stacked(w1_ref[...], 4), NT, preferred_element_type=jnp.float32
    )
    left_ref[...] = (left + shift1).astype(jnp.bfloat16)

    split = [v.reshape(n, 2, 8, feats) for v in normed]
    parts = [split[s][:, jh].reshape(n * 8, feats).astype(jnp.bfloat16) for jh in range(2) for s in range(2)]
    shift2 = jnp.concatenate([b2_ref[...]] * 4, axis=1)
    right = lax.dot_general(
        jnp.concatenate(parts, axis=1), _stacked(w2_ref[...], 4), NT, preferred_element_type=jnp.float32
    )
    right_ref[...] = (right + shift2).reshape(n // 2, 16, LANES).astype(jnp.bfloat16)


def _line_kernel(*refs):
    pieces, order_ref, out_ref = refs[:-2], refs[-2], refs[-1]
    half = pieces[0].shape[0]
    wide = order_ref.shape[2]
    for q in range(len(pieces) // 4):
        lhs = jnp.concatenate([piece[...] for piece in pieces[q * 4 : q * 4 + 4]], axis=1)
        for h in range(2):
            moved = jnp.dot(lhs, order_ref[h], preferred_element_type=jnp.float32)
            out_ref[pl.ds(h * half, half), pl.ds(q * wide, wide)] = moved.astype(jnp.bfloat16)


def _fold_kernel(own_ref, other_ref, final_ref, out_ref, block_ref, pairs_ref):
    chips = own_ref.shape[0]
    devices = chips * 2
    groups = devices // 4
    core = lax.axis_index("row") % 2
    own, other = (ref[...].astype(jnp.float32).reshape(chips, 2, 8, LANES) for ref in (own_ref, other_ref))
    own, other = (jnp.where(core == 0, block[:, 0], block[:, 1]) for block in (own, other))
    by_core = jnp.where(core == 0, own, other), jnp.where(core == 0, other, own)
    for p in range(chips):
        for c in range(2):
            block_ref[pl.ds((p * 2 + c) * 8, 8), :] = by_core[c][p]
    for jr in range(8):
        for g in range(groups):
            four = block_ref[pl.ds(g * 8 + jr, 4, stride=groups * 8), :]
            for s in range(2):
                pairs_ref[pl.ds((jr * groups + g) * 8 + s * 4, 4), :] = four
    block = pairs_ref[...]
    lane = lax.broadcasted_iota(jnp.int32, block.shape, 1) // CHANS
    s = lax.broadcasted_iota(jnp.int32, block.shape, 0) // 4 % 2
    lhs = [jnp.where(lane == jh * 2 + s, block, 0.0).astype(jnp.bfloat16) for jh in range(2)]
    lhs = jnp.concatenate(lhs, axis=0)

    for pair in range(CHANS // 2):
        rhs = []
        for k in range(2):
            at = pair * 2 * CHANS + k * CHANS
            rhs.append(jnp.concatenate([final_ref[pl.ds(at, CHANS), :]] * 4, axis=0))
        res = jnp.dot(lhs, jnp.concatenate(rhs, axis=1), preferred_element_type=jnp.float32)
        for j in range(16):
            for g in range(groups):
                r = (j * groups + g) * 8
                tile = jnp.concatenate([res[r : r + 8, :LANES], res[r : r + 8, LANES:]], axis=0)
                out_ref[g, 0, pl.ds(pair * 16, 16), pl.ds(j * LANES, LANES)] = tile.astype(jnp.bfloat16)


def _band_kernel(masks, begins, count, held, *refs):
    refs = list(refs)
    take = lambda k: [refs.pop(0) for _ in range(k)]
    if masks == (1, 3, 5):
        (block,) = take(1)
        lines = [[block.at[k]] for k in range(3)]
    else:
        lines = [take(2 if mask == 6 else 1) for mask in masks]
    (t_ref,) = take(1)
    (sum_ref,) = (None,) if begins else take(1)
    pair_ref, shift_ref = (None, None) if count is None else take(2)
    (out_ref,) = take(1)
    me = lax.axis_index("row")
    wide = t_ref.shape[2]
    chunks = [((me % 8) ^ mask, q ^ (me // 32)) for mask in masks for q in range(t_ref.shape[1])]

    tile = 256
    band = sum(part.shape[0] for part in lines[0])
    if count is not None:
        acc_ref, done_ref, sems = take(3)
        cols = pair_ref.shape[1]
        pitch = cols + 1

    def column(step):
        at = pl.ds(step * tile, tile)
        lhs = jnp.concatenate([jnp.concatenate([part[...] for part in line], axis=0) for line in lines], axis=1)
        if held:
            rhs = jnp.concatenate([t_ref[g, q, :, at] for g, q in chunks], axis=0)
        else:
            for i, (g, q) in enumerate(chunks):
                pltpu.sync_copy(t_ref.at[g, q, :, at], refs[0].at[pl.ds(i * wide, wide)])
            rhs = refs[0][...]
        res = jnp.dot(lhs, rhs, preferred_element_type=jnp.float32)
        if sum_ref is not None:
            res = res + sum_ref[:, at]
        if count is None:
            out_ref[:, at] = res
        else:
            for k in range(tile // LANES):
                j = step * (tile // LANES) + k
                acc_ref[pl.ds(j, band, stride=pitch), :] = res[:, k * LANES : (k + 1) * LANES]

    for step in range(t_ref.shape[3] // tile):
        column(step)
    if count is None:
        return

    rows = 32
    shift = shift_ref[...]

    def finish(r, _):
        for k in range(rows):
            i = r * rows + k
            total = acc_ref[pl.ds(i * pitch, cols), :] * (1.0 / count) + shift
            done_ref[i] = (pair_ref[i].astype(jnp.float32) + total).astype(jnp.bfloat16)
        at = pl.ds(pl.multiple_of(r * rows, rows), rows)
        pltpu.make_async_copy(done_ref.at[at], out_ref.at[at], sems.at[r]).start()
        return 0

    lax.fori_loop(0, band // rows, finish, 0)

    def drain(r, _):
        at = pl.ds(pl.multiple_of(r * rows, rows), rows)
        pltpu.make_async_copy(done_ref.at[at], out_ref.at[at], sems.at[r]).wait()
        return 0

    lax.fori_loop(0, band // rows, drain, 0)


def _xor(x, mask, n):
    return lax.ppermute(x, "row", [(i, i ^ mask) for i in range(n)])


def shards(n, alignment, pair, gain, bias, w1, b1, w2, b2, final, shift):
    seqs, residues, feats = alignment.shape
    band, cols, zdim = pair.shape
    half = band // 2
    count = float(seqs * n)
    small = n <= 32
    params = pltpu.CompilerParams(vmem_limit_bytes=(24 if small else 48) * 1024 * 1024)
    anywhere = pl.BlockSpec(memory_space=pl.ANY)
    vmem = pl.BlockSpec(memory_space=pltpu.VMEM)

    sources = [
        alignment, gain.reshape(1, -1), bias.reshape(1, -1), w1.T, b1.reshape(1, -1), w2.T, b2.reshape(1, -1)
    ]
    sources = [pltpu.with_memory_space_constraint(a, pltpu.HBM) for a in sources]
    left, right, final, order = pl.pallas_call(
        _project_kernel,
        in_specs=[anywhere] * 8,
        out_specs=(vmem,) * 4,
        out_shape=(
            jax.ShapeDtypeStruct((half, LANES), jnp.bfloat16),
            jax.ShapeDtypeStruct((n // 2, 16, LANES), jnp.bfloat16),
            jax.ShapeDtypeStruct(final.shape, final.dtype),
            jax.ShapeDtypeStruct((2, 4 * LANES, 8 * CHANS), jnp.bfloat16),
        ),
        scratch_shapes=[pltpu.VMEM(a.shape, a.dtype) for a in sources] + [pltpu.SemaphoreType.DMA((8,))],
        compiler_params=params,
        cost_estimate=pl.CostEstimate(
            flops=4 * seqs * residues * feats * CHANS, bytes_accessed=2 * seqs * residues * feats, transcendentals=0
        ),
    )(*sources, pltpu.with_memory_space_constraint(final, pltpu.HBM))

    cores = [[chip * 2 + core for chip in range(n // 2)] for core in range(2)]
    right = lax.all_to_all(right, "row", split_axis=0, concat_axis=0, axis_index_groups=cores, tiled=True)
    right_other = _xor(right, 1, n)

    part = 32
    parts = n // part
    pieces = [left] + [_xor(left, m, n) for m in range(8, n, 8)]
    line = pl.pallas_call(
        _line_kernel,
        in_specs=[vmem] * (len(pieces) + 1),
        out_specs=vmem,
        out_shape=jax.ShapeDtypeStruct((band, parts * 8 * CHANS), jnp.bfloat16),
        compiler_params=params,
        cost_estimate=pl.CostEstimate(flops=2**27, bytes_accessed=2**20, transcendentals=0),
    )(*pieces, order)
    x, y = _xor(line, 2, n), _xor(line, 4, n)

    fold_cost = pl.CostEstimate(
        flops=2 * n * 32 * 256 * CHANS * zdim, bytes_accessed=4 * n * CHANS * cols * zdim, transcendentals=0
    )
    fold_out = jax.ShapeDtypeStruct((8, parts, 8 * CHANS, cols * zdim), jnp.bfloat16)
    if small:
        specs = dict(in_specs=[vmem] * 3, out_specs=vmem)
    else:
        specs = dict(
            grid=(parts,),
            in_specs=[
                pl.BlockSpec((part // 2, 16, LANES), lambda i: (i, 0, 0)),
                pl.BlockSpec((part // 2, 16, LANES), lambda i: (i, 0, 0)),
                pl.BlockSpec(final.shape, lambda i: (0, 0)),
            ],
            out_specs=pl.BlockSpec((8, 1, 8 * CHANS, cols * zdim), lambda i: (0, i, 0, 0)),
        )
    folded = pl.pallas_call(
        _fold_kernel,
        out_shape=fold_out,
        scratch_shapes=[pltpu.VMEM((part * 8, LANES), jnp.float32), pltpu.VMEM((part * 16, LANES), jnp.float32)],
        compiler_params=params,
        cost_estimate=fold_cost,
        **specs,
    )(right, right_other, final)

    def add(lines, masks, total, last):
        depth = len(masks) * parts * 8 * CHANS
        scratch = []
        operands = [*lines, folded] + ([] if total is None else [total])
        if last:
            operands += [pair, shift.reshape(1, -1)]
            scratch += [
                pltpu.VMEM((band * (cols + 1), zdim), jnp.float32),
                pltpu.VMEM(pair.shape, jnp.bfloat16),
                pltpu.SemaphoreType.DMA((band // 32,)),
            ]
        if not small:
            scratch.append(pltpu.VMEM((depth, 256), jnp.bfloat16))
        in_specs = [vmem] * len(operands)
        if not small:
            in_specs[len(lines)] = anywhere
        return pl.pallas_call(
            functools.partial(_band_kernel, masks, total is None, count if last else None, small),
            in_specs=in_specs,
            out_specs=anywhere if last else vmem,
            out_shape=jax.ShapeDtypeStruct(pair.shape, jnp.bfloat16)
            if last
            else jax.ShapeDtypeStruct((band, cols * zdim), jnp.float32),
            scratch_shapes=scratch,
            compiler_params=params,
            cost_estimate=pl.CostEstimate(
                flops=band * cols * zdim, bytes_accessed=band * cols, transcendentals=0
            ),
        )(*operands)

    x, y, folded = lax.optimization_barrier((x, y, folded))
    upper, lower = _xor(x[:half], 4, n), _xor(y[half:], 2, n)
    across = _xor(jnp.stack([line, x, y]), 1, n)
    total = add([line, x, y], (0, 2, 4), None, False)
    total = add([across], (1, 3, 5), total, False)
    upper, lower, total = lax.optimization_barrier((upper, lower, total))
    last = _xor(jnp.concatenate([upper, lower], axis=0), 1, n)
    total = add([upper, lower], (6,), total, False)
    return add([last], (7,), total, True)


def solution(mesh):
    placed = (P(("group", "row"), None, None), P("group", "row", None)) + (P(),) * 8
    return jax.shard_map(
        functools.partial(shards, mesh.shape["row"]),
        mesh=mesh,
        in_specs=placed,
        out_specs=P("group", "row", None),
        check_vma=False,
    )
```

```python
import functools

import jax
import jax.numpy as jnp
from jax import lax
from jax.experimental import pallas as pl
from jax.experimental.pallas import tpu as pltpu
from jax.sharding import PartitionSpec as P

LANES = 128
CHANS = 32
NT = (((1,), (1,)), ((), ()))


def _stacked(weights, copies):
    c, q = weights.shape
    rows = []
    for k in range(copies):
        left = [jnp.zeros((c, k * q), weights.dtype)] if k else []
        right = [jnp.zeros((c, (copies - 1 - k) * q), weights.dtype)] if k < copies - 1 else []
        rows.append(jnp.concatenate(left + [weights] + right, axis=1))
    return jnp.concatenate(rows, axis=0)


def _order(me, half):
    row = lax.broadcasted_iota(jnp.int32, (4 * LANES, 8 * CHANS), 0)
    col = lax.broadcasted_iota(jnp.int32, (4 * LANES, 8 * CHANS), 1)
    device = (row // LANES) ^ (me // 8 % 4)
    wanted = (row % CHANS) * 8 + ((row // CHANS) % 2) * 4 + device
    hit = (wanted == col) & ((row // (2 * CHANS)) % 2 == half)
    return jnp.where(hit, 1.0, 0.0).astype(jnp.bfloat16)


def _project_kernel(*refs):
    sources, final_source, outs, held = refs[:7], refs[7], refs[8:12], refs[12:19]
    left_ref, right_ref, final_ref, order_ref = outs
    sems = refs[19]
    pairs = [(sources[0].at[s], held[0].at[s]) for s in range(2)]
    pairs += list(zip(sources[1:], held[1:])) + [(final_source, final_ref)]
    copies = [pltpu.make_async_copy(a, b, sems.at[i]) for i, (a, b) in enumerate(pairs)]
    for copy in copies:
        copy.start()
    me = lax.axis_index("row")
    for h in range(2):
        order_ref[h] = _order(me, h)
    for copy in copies[:1] + copies[2:8]:
        copy.wait()
    x_ref, gain_ref, bias_ref, w1_ref, b1_ref, w2_ref, b2_ref = held
    half = left_ref.shape[0]
    n = right_ref.shape[0]
    feats = x_ref.shape[2]
    split = []
    for s in range(2):
        if s:
            copies[1].wait()
        x = x_ref[s].astype(jnp.float32)
        center = jnp.mean(x, axis=-1, keepdims=True)
        off = x - center
        spread = jnp.mean(off * off, axis=-1, keepdims=True)
        normed = off * lax.rsqrt(spread + 1e-05) * gain_ref[...] + bias_ref[...]
        split.append(normed.reshape(n, 2, 8, feats))
    parts = [split[s][:, jh].reshape(n * 8, feats).astype(jnp.bfloat16) for jh in range(2) for s in range(2)]
    weights = jnp.concatenate([_stacked(w1_ref[...], 4), _stacked(w2_ref[...], 4)], axis=0)
    shifts = jnp.concatenate([b1_ref[...]] * 4 + [b2_ref[...]] * 4, axis=1)
    both = lax.dot_general(jnp.concatenate(parts, axis=1), weights, NT, preferred_element_type=jnp.float32) + shifts
    left_ref[...] = both[:half, :LANES].astype(jnp.bfloat16)
    right_ref[...] = both[:, LANES:].reshape(n, 8, LANES).astype(jnp.bfloat16)
    copies[8].wait()


def _line_kernel(*refs):
    pieces, order_ref, out_ref = refs[:-2], refs[-2], refs[-1]
    half = pieces[0].shape[0]
    wide = order_ref.shape[2]
    for q in range(len(pieces) // 4):
        lhs = jnp.concatenate([pieces[q * 4 + k][...] for k in (0, 1, 3, 2)], axis=1)
        for h in range(2):
            moved = jnp.dot(lhs, order_ref[h], preferred_element_type=jnp.float32)
            out_ref[pl.ds(h * half, half), pl.ds(q * wide, wide)] = moved.astype(jnp.bfloat16)


def _fold_kernel(right_ref, final_ref, out_ref, block_ref, pairs_ref):
    devices = right_ref.shape[0]
    groups = devices // 4
    block_ref[...] = right_ref[...].astype(jnp.float32).reshape(devices * 8, LANES)
    for jr in range(8):
        for g in range(groups):
            four = block_ref[pl.ds(g * 8 + jr, 4, stride=groups * 8), :]
            for s in range(2):
                pairs_ref[pl.ds((jr * groups + g) * 8 + s * 4, 4), :] = four
    block = pairs_ref[...]
    lane = lax.broadcasted_iota(jnp.int32, block.shape, 1) // CHANS
    s = lax.broadcasted_iota(jnp.int32, block.shape, 0) // 4 % 2
    lhs = [jnp.where(lane == jh * 2 + s, block, 0.0).astype(jnp.bfloat16) for jh in range(2)]
    lhs = jnp.concatenate(lhs, axis=0)

    for pair in range(CHANS // 2):
        rhs = []
        for k in range(2):
            at = pair * 2 * CHANS + k * CHANS
            rhs.append(jnp.concatenate([final_ref[pl.ds(at, CHANS), :]] * 4, axis=0))
        res = jnp.dot(lhs, jnp.concatenate(rhs, axis=1), preferred_element_type=jnp.float32)
        for j in range(16):
            for g in range(groups):
                r = (j * groups + g) * 8
                tile = jnp.concatenate([res[r : r + 8, :LANES], res[r : r + 8, LANES:]], axis=0)
                out_ref[g, 0, pl.ds(pair * 16, 16), pl.ds(j * LANES, LANES)] = tile.astype(jnp.bfloat16)


def _band_kernel(masks, begins, count, held, *refs):
    refs = list(refs)
    take = lambda k: [refs.pop(0) for _ in range(k)]
    if masks == (1, 3, 5):
        (block,) = take(1)
        lines = [[block.at[k]] for k in range(3)]
    else:
        lines = [take(2 if mask in (6, 7) else 1) for mask in masks]
    (t_ref,) = take(1)
    (sum_ref,) = (None,) if begins else take(1)
    pair_ref, shift_ref = (None, None) if count is None else take(2)
    (out_ref,) = take(1)
    me = lax.axis_index("row")
    wide = t_ref.shape[2]
    chunks = [((me % 8) ^ mask, q ^ (me // 32)) for mask in masks for q in range(t_ref.shape[1])]

    tile = 256
    band = sum(part.shape[0] for part in lines[0])

    def column(step, rows):
        at = pl.ds(step * tile, tile)
        if held:
            rhs = jnp.concatenate([t_ref[g, q, :, at] for g, q in chunks], axis=0)
        else:
            for i, (g, q) in enumerate(chunks):
                pltpu.sync_copy(t_ref.at[g, q, :, at], refs[0].at[pl.ds(i * wide, wide)])
            rhs = refs[0][...]
        lhs = []
        for line in lines:
            ends = [sum(part.shape[0] for part in line[: k + 1]) for k in range(len(line))]
            pieces = []
            for first, size in rows:
                k = next(k for k, end in enumerate(ends) if first < end)
                begin = first - (ends[k] - line[k].shape[0])
                pieces.append(line[k][pl.ds(begin, size), :])
            lhs.append(jnp.concatenate(pieces, axis=0))
        res = jnp.dot(jnp.concatenate(lhs, axis=1), rhs, preferred_element_type=jnp.float32)
        if sum_ref is not None:
            res = res + jnp.concatenate([sum_ref[pl.ds(first, size), at] for first, size in rows], axis=0)
        return res

    halves = [(0, band // 2), (band // 2, band // 2)]
    steps = t_ref.shape[3] // tile
    if count is None:
        for step in range(steps):
            out_ref[:, pl.ds(step * tile, tile)] = column(step, halves)
        return

    acc_ref, done_ref, sems = take(3)
    cols = pair_ref.shape[1]
    pitch = cols + 1
    shift = shift_ref[...]
    chunk = band // 2 // steps

    def finish(r):
        for k in range(chunk):
            i = r * chunk + k
            row = (i // 8) % 2 * (band // 2) + i // 16 * 8 + i % 8
            total = acc_ref[pl.ds(row * pitch, cols), :] * (1.0 / count) + shift
            done_ref[i] = (pair_ref[i].astype(jnp.float32) + total).astype(jnp.bfloat16)
        at = pl.ds(r * chunk, chunk)
        pltpu.make_async_copy(done_ref.at[at], out_ref.at[at], sems.at[r]).start()

    for part in range(2):
        rows = [(first + part * size // 2, size // 2) for first, size in halves]
        for step in range(steps):
            res = column(step, rows)
            for k in range(tile // LANES):
                j = step * (tile // LANES) + k
                for piece, (first, size) in enumerate(rows):
                    acc_ref[pl.ds(first * pitch + j, size, stride=pitch), :] = res[
                        piece * size : (piece + 1) * size, k * LANES : (k + 1) * LANES
                    ]
            if part:
                finish(step)
    for step in range(steps):
        finish(steps + step)
    for r in range(2 * steps):
        at = pl.ds(r * chunk, chunk)
        pltpu.make_async_copy(done_ref.at[at], out_ref.at[at], sems.at[r]).wait()


def _xor(x, mask, n):
    return lax.ppermute(x, "row", [(i, i ^ mask) for i in range(n)])


def shards(n, alignment, pair, gain, bias, w1, b1, w2, b2, final, shift):
    seqs, residues, feats = alignment.shape
    band, cols, zdim = pair.shape
    half = band // 2
    count = float(seqs * n)
    small = n <= 32
    params = pltpu.CompilerParams(vmem_limit_bytes=(24 if small else 48) * 1024 * 1024)
    anywhere = pl.BlockSpec(memory_space=pl.ANY)
    vmem = pl.BlockSpec(memory_space=pltpu.VMEM)

    sources = [
        alignment, gain.reshape(1, -1), bias.reshape(1, -1), w1.T, b1.reshape(1, -1), w2.T, b2.reshape(1, -1)
    ]
    sources = [pltpu.with_memory_space_constraint(a, pltpu.HBM) for a in sources]
    left, right, final, order = pl.pallas_call(
        _project_kernel,
        in_specs=[anywhere] * 8,
        out_specs=(vmem,) * 4,
        out_shape=(
            jax.ShapeDtypeStruct((half, LANES), jnp.bfloat16),
            jax.ShapeDtypeStruct((n, 8, LANES), jnp.bfloat16),
            jax.ShapeDtypeStruct(final.shape, final.dtype),
            jax.ShapeDtypeStruct((2, 4 * LANES, 8 * CHANS), jnp.bfloat16),
        ),
        scratch_shapes=[pltpu.VMEM(a.shape, a.dtype) for a in sources] + [pltpu.SemaphoreType.DMA((9,))],
        compiler_params=params,
        cost_estimate=pl.CostEstimate(
            flops=4 * seqs * residues * feats * CHANS, bytes_accessed=2 * seqs * residues * feats, transcendentals=0
        ),
    )(*sources, pltpu.with_memory_space_constraint(final, pltpu.HBM))

    right = lax.all_to_all(right, "row", split_axis=0, concat_axis=0, tiled=True)

    part = 32
    parts = n // part
    pieces = [left] + [_xor(left, m, n) for m in range(8, n, 8)]
    pieces = [pieces[k ^ (k // 2 % 2)] for k in range(len(pieces))]
    line = pl.pallas_call(
        _line_kernel,
        in_specs=[vmem] * (len(pieces) + 1),
        out_specs=vmem,
        out_shape=jax.ShapeDtypeStruct((band, parts * 8 * CHANS), jnp.bfloat16),
        compiler_params=params,
        cost_estimate=pl.CostEstimate(flops=2**27, bytes_accessed=2**20, transcendentals=0),
    )(*pieces, order)
    x, y = _xor(line, 2, n), _xor(line, 4, n)

    fold_cost = pl.CostEstimate(
        flops=2 * n * 32 * 256 * CHANS * zdim, bytes_accessed=4 * n * CHANS * cols * zdim, transcendentals=0
    )
    fold_out = jax.ShapeDtypeStruct((8, parts, 8 * CHANS, cols * zdim), jnp.bfloat16)
    if small:
        specs = dict(in_specs=[vmem, vmem], out_specs=vmem)
    else:
        specs = dict(
            grid=(parts,),
            in_specs=[
                pl.BlockSpec((part, 8, LANES), lambda i: (i, 0, 0)),
                pl.BlockSpec(final.shape, lambda i: (0, 0)),
            ],
            out_specs=pl.BlockSpec((8, 1, 8 * CHANS, cols * zdim), lambda i: (0, i, 0, 0)),
        )
    folded = pl.pallas_call(
        _fold_kernel,
        out_shape=fold_out,
        scratch_shapes=[pltpu.VMEM((part * 8, LANES), jnp.float32), pltpu.VMEM((part * 16, LANES), jnp.float32)],
        compiler_params=params,
        cost_estimate=fold_cost,
        **specs,
    )(right, final)

    def add(lines, masks, total, last):
        depth = len(masks) * parts * 8 * CHANS
        scratch = []
        operands = [*lines, folded] + ([] if total is None else [total])
        if last:
            operands += [pair, shift.reshape(1, -1)]
            scratch += [
                pltpu.VMEM((band * (cols + 1), zdim), jnp.float32),
                pltpu.VMEM(pair.shape, jnp.bfloat16),
                pltpu.SemaphoreType.DMA((cols * zdim // 128,)),
            ]
        if not small:
            scratch.append(pltpu.VMEM((depth, 256), jnp.bfloat16))
        in_specs = [vmem] * len(operands)
        if not small:
            in_specs[len(lines)] = anywhere
        return pl.pallas_call(
            functools.partial(_band_kernel, masks, total is None, count if last else None, small),
            in_specs=in_specs,
            out_specs=anywhere if last else vmem,
            out_shape=jax.ShapeDtypeStruct(pair.shape, jnp.bfloat16)
            if last
            else jax.ShapeDtypeStruct((band, cols * zdim), jnp.float32),
            scratch_shapes=scratch,
            compiler_params=params,
            cost_estimate=pl.CostEstimate(
                flops=band * cols * zdim, bytes_accessed=band * cols, transcendentals=0
            ),
        )(*operands)

    x, y, folded = lax.optimization_barrier((x, y, folded))
    upper, lower = _xor(x[:half], 4, n), _xor(y[half:], 2, n)
    across = _xor(jnp.stack([line, x, y]), 1, n)
    total = add([line, x, y], (0, 2, 4), None, False)
    total = add([across], (1, 3, 5), total, False)
    upper, total = lax.optimization_barrier((upper, total))
    last = [_xor(upper, 1, n)]
    lower, total = lax.optimization_barrier((lower, total))
    last.append(_xor(lower, 1, n))
    total = add([upper, lower], (6,), total, False)
    return add(last, (7,), total, True)


def solution(mesh):
    placed = (P(("group", "row"), None, None), P("group", "row", None)) + (P(),) * 8
    return jax.shard_map(
        functools.partial(shards, mesh.shape["row"]),
        mesh=mesh,
        in_specs=placed,
        out_specs=P("group", "row", None),
        check_vma=False,
    )
```

```python
import functools

import jax
import jax.numpy as jnp
from jax import lax
from jax.experimental import pallas as pl
from jax.experimental.pallas import tpu as pltpu
from jax.sharding import PartitionSpec as P

LANES = 128
CHANS = 32
NT = (((1,), (1,)), ((), ()))


def _stacked(weights, copies):
    c, q = weights.shape
    rows = []
    for k in range(copies):
        left = [jnp.zeros((c, k * q), weights.dtype)] if k else []
        right = [jnp.zeros((c, (copies - 1 - k) * q), weights.dtype)] if k < copies - 1 else []
        rows.append(jnp.concatenate(left + [weights] + right, axis=1))
    return jnp.concatenate(rows, axis=0)


def _order(me, half):
    row = lax.broadcasted_iota(jnp.int32, (4 * LANES, 8 * CHANS), 0)
    col = lax.broadcasted_iota(jnp.int32, (4 * LANES, 8 * CHANS), 1)
    device = (row // LANES) ^ (me // 8 % 4)
    wanted = (row % CHANS) * 8 + ((row // CHANS) % 2) * 4 + device
    hit = (wanted == col) & ((row // (2 * CHANS)) % 2 == half)
    return jnp.where(hit, 1.0, 0.0).astype(jnp.bfloat16)


def _project_kernel(*refs):
    sources, final_source, outs, held = refs[:7], refs[7], refs[8:12], refs[12:19]
    left_ref, right_ref, final_ref, order_ref = outs
    sems = refs[19]
    pairs = [(sources[0].at[s], held[0].at[s]) for s in range(2)]
    pairs += list(zip(sources[1:], held[1:])) + [(final_source, final_ref)]
    copies = [pltpu.make_async_copy(a, b, sems.at[i]) for i, (a, b) in enumerate(pairs)]
    for copy in copies:
        copy.start()
    me = lax.axis_index("row")
    for h in range(2):
        order_ref[h] = _order(me, h)
    for copy in copies[:1] + copies[2:8]:
        copy.wait()
    x_ref, gain_ref, bias_ref, w1_ref, b1_ref, w2_ref, b2_ref = held
    half = left_ref.shape[0]
    n = right_ref.shape[0]
    feats = x_ref.shape[2]
    split = []
    for s in range(2):
        if s:
            copies[1].wait()
        x = x_ref[s].astype(jnp.float32)
        center = jnp.mean(x, axis=-1, keepdims=True)
        off = x - center
        spread = jnp.mean(off * off, axis=-1, keepdims=True)
        normed = off * lax.rsqrt(spread + 1e-05) * gain_ref[...] + bias_ref[...]
        split.append(normed.reshape(n, 2, 8, feats))
    parts = [split[s][:, jh].reshape(n * 8, feats).astype(jnp.bfloat16) for jh in range(2) for s in range(2)]
    weights = jnp.concatenate([_stacked(w1_ref[...], 4), _stacked(w2_ref[...], 4)], axis=0)
    shifts = jnp.concatenate([b1_ref[...]] * 4 + [b2_ref[...]] * 4, axis=1)
    both = lax.dot_general(jnp.concatenate(parts, axis=1), weights, NT, preferred_element_type=jnp.float32) + shifts
    left_ref[...] = both[:half, :LANES].astype(jnp.bfloat16)
    right_ref[...] = both[:, LANES:].reshape(n, 8, LANES).astype(jnp.bfloat16)
    copies[8].wait()


def _line_kernel(*refs):
    pieces, order_ref, out_ref = refs[:-2], refs[-2], refs[-1]
    half = pieces[0].shape[0]
    wide = order_ref.shape[2]
    for q in range(len(pieces) // 4):
        lhs = jnp.concatenate([pieces[q * 4 + k][...] for k in (0, 1, 3, 2)], axis=1)
        for h in range(2):
            moved = jnp.dot(lhs, order_ref[h], preferred_element_type=jnp.float32)
            out_ref[pl.ds(h * half, half), pl.ds(q * wide, wide)] = moved.astype(jnp.bfloat16)


def _fold_kernel(right_ref, final_ref, out_ref, block_ref, pairs_ref):
    devices = right_ref.shape[0]
    groups = devices // 4
    block_ref[...] = right_ref[...].astype(jnp.float32).reshape(devices * 8, LANES)
    for jr in range(8):
        for g in range(groups):
            four = block_ref[pl.ds(g * 8 + jr, 4, stride=groups * 8), :]
            for s in range(2):
                pairs_ref[pl.ds((jr * groups + g) * 8 + s * 4, 4), :] = four
    block = pairs_ref[...]
    lane = lax.broadcasted_iota(jnp.int32, block.shape, 1) // CHANS
    s = lax.broadcasted_iota(jnp.int32, block.shape, 0) // 4 % 2
    lhs = [jnp.where(lane == jh * 2 + s, block, 0.0).astype(jnp.bfloat16) for jh in range(2)]
    lhs = jnp.concatenate(lhs, axis=0)

    for pair in range(CHANS // 2):
        rhs = []
        for k in range(2):
            at = pair * 2 * CHANS + k * CHANS
            rhs.append(jnp.concatenate([final_ref[pl.ds(at, CHANS), :]] * 4, axis=0))
        res = jnp.dot(lhs, jnp.concatenate(rhs, axis=1), preferred_element_type=jnp.float32)
        for j in range(16):
            for g in range(groups):
                r = (j * groups + g) * 8
                tile = jnp.concatenate([res[r : r + 8, :LANES], res[r : r + 8, LANES:]], axis=0)
                out_ref[g, 0, pl.ds(pair * 16, 16), pl.ds(j * LANES, LANES)] = tile.astype(jnp.bfloat16)


def _band_kernel(masks, begins, count, held, *refs):
    refs = list(refs)
    take = lambda k: [refs.pop(0) for _ in range(k)]
    lines = []
    for mask in masks:
        if mask in (1, 3, 5):
            block = take(1)[0] if mask == 1 else block
            lines.append([block.at[mask // 2]])
        else:
            lines.append(take(2 if mask > 5 else 1))
    (t_ref,) = take(1)
    (sum_ref,) = (None,) if begins else take(1)
    pair_ref, shift_ref = (None, None) if count is None else take(2)
    (out_ref,) = take(1)
    me = lax.axis_index("row")
    wide = t_ref.shape[2]
    chunks = [((me % 8) ^ mask, q ^ (me // 32)) for mask in masks for q in range(t_ref.shape[1])]

    tile = 256
    band = sum(part.shape[0] for part in lines[0])

    def column(step):
        at = pl.ds(step * tile, tile)
        if held:
            rhs = jnp.concatenate([t_ref[g, q, :, at] for g, q in chunks], axis=0)
        else:
            for i, (g, q) in enumerate(chunks):
                pltpu.sync_copy(t_ref.at[g, q, :, at], refs[0].at[pl.ds(i * wide, wide)])
            rhs = refs[0][...]
        lhs = jnp.concatenate([jnp.concatenate([part[...] for part in line], axis=0) for line in lines], axis=1)
        res = jnp.dot(lhs, rhs, preferred_element_type=jnp.float32)
        return res if sum_ref is None else res + sum_ref[:, at]

    steps = t_ref.shape[3] // tile
    if count is None:
        for step in range(steps):
            out_ref[:, pl.ds(step * tile, tile)] = column(step)
        return

    acc_ref, done_ref, sems = take(3)
    cols = pair_ref.shape[1]
    pitch = cols + 1
    shift = shift_ref[...]
    chunk = band // 2 // steps

    def finish(r):
        for k in range(chunk):
            i = r * chunk + k
            row = (i // 8) % 2 * (band // 2) + i // 16 * 8 + i % 8
            total = acc_ref[pl.ds(row * pitch, cols), :] * (1.0 / count) + shift
            done_ref[i] = (pair_ref[i].astype(jnp.float32) + total).astype(jnp.bfloat16)
        at = pl.ds(r * chunk, chunk)
        pltpu.make_async_copy(done_ref.at[at], out_ref.at[at], sems.at[r]).start()

    for step in range(steps):
        res = column(step)
        for k in range(tile // LANES):
            j = step * (tile // LANES) + k
            acc_ref[pl.ds(j, band, stride=pitch), :] = res[:, k * LANES : (k + 1) * LANES]
    for r in range(2 * steps):
        finish(r)
    for r in range(2 * steps):
        at = pl.ds(r * chunk, chunk)
        pltpu.make_async_copy(done_ref.at[at], out_ref.at[at], sems.at[r]).wait()


def _xor(x, mask, n):
    return lax.ppermute(x, "row", [(i, i ^ mask) for i in range(n)])


def shards(n, alignment, pair, gain, bias, w1, b1, w2, b2, final, shift):
    seqs, residues, feats = alignment.shape
    band, cols, zdim = pair.shape
    half = band // 2
    count = float(seqs * n)
    small = n <= 32
    params = pltpu.CompilerParams(vmem_limit_bytes=(24 if small else 48) * 1024 * 1024)
    anywhere = pl.BlockSpec(memory_space=pl.ANY)
    vmem = pl.BlockSpec(memory_space=pltpu.VMEM)

    sources = [
        alignment, gain.reshape(1, -1), bias.reshape(1, -1), w1.T, b1.reshape(1, -1), w2.T, b2.reshape(1, -1)
    ]
    sources = [pltpu.with_memory_space_constraint(a, pltpu.HBM) for a in sources]
    left, right, final, order = pl.pallas_call(
        _project_kernel,
        in_specs=[anywhere] * 8,
        out_specs=(vmem,) * 4,
        out_shape=(
            jax.ShapeDtypeStruct((half, LANES), jnp.bfloat16),
            jax.ShapeDtypeStruct((n, 8, LANES), jnp.bfloat16),
            jax.ShapeDtypeStruct(final.shape, final.dtype),
            jax.ShapeDtypeStruct((2, 4 * LANES, 8 * CHANS), jnp.bfloat16),
        ),
        scratch_shapes=[pltpu.VMEM(a.shape, a.dtype) for a in sources] + [pltpu.SemaphoreType.DMA((9,))],
        compiler_params=params,
        cost_estimate=pl.CostEstimate(
            flops=4 * seqs * residues * feats * CHANS, bytes_accessed=2 * seqs * residues * feats, transcendentals=0
        ),
    )(*sources, pltpu.with_memory_space_constraint(final, pltpu.HBM))

    part = 32
    parts = n // part
    pieces = [left] + [_xor(left, m, n) for m in range(8, n, 8)]
    pieces, right = lax.optimization_barrier((pieces, right))
    pieces = [pieces[k ^ (k // 2 % 2)] for k in range(len(pieces))]
    line = pl.pallas_call(
        _line_kernel,
        in_specs=[vmem] * (len(pieces) + 1),
        out_specs=vmem,
        out_shape=jax.ShapeDtypeStruct((band, parts * 8 * CHANS), jnp.bfloat16),
        compiler_params=params,
        cost_estimate=pl.CostEstimate(flops=2**27, bytes_accessed=2**20, transcendentals=0),
    )(*pieces, order)
    x, y = _xor(line, 2, n), _xor(line, 4, n)
    right = lax.all_to_all(right, "row", split_axis=0, concat_axis=0, tiled=True)

    fold_cost = pl.CostEstimate(
        flops=2 * n * 32 * 256 * CHANS * zdim, bytes_accessed=4 * n * CHANS * cols * zdim, transcendentals=0
    )
    fold_out = jax.ShapeDtypeStruct((8, parts, 8 * CHANS, cols * zdim), jnp.bfloat16)
    if small:
        specs = dict(in_specs=[vmem, vmem], out_specs=vmem)
    else:
        specs = dict(
            grid=(parts,),
            in_specs=[
                pl.BlockSpec((part, 8, LANES), lambda i: (i, 0, 0)),
                pl.BlockSpec(final.shape, lambda i: (0, 0)),
            ],
            out_specs=pl.BlockSpec((8, 1, 8 * CHANS, cols * zdim), lambda i: (0, i, 0, 0)),
        )
    folded = pl.pallas_call(
        _fold_kernel,
        out_shape=fold_out,
        scratch_shapes=[pltpu.VMEM((part * 8, LANES), jnp.float32), pltpu.VMEM((part * 16, LANES), jnp.float32)],
        compiler_params=params,
        cost_estimate=fold_cost,
        **specs,
    )(right, final)

    def add(lines, masks, total, last):
        depth = len(masks) * parts * 8 * CHANS
        scratch = []
        operands = [*lines, folded] + ([] if total is None else [total])
        if last:
            operands += [pair, shift.reshape(1, -1)]
            scratch += [
                pltpu.VMEM((band * (cols + 1), zdim), jnp.float32),
                pltpu.VMEM(pair.shape, jnp.bfloat16),
                pltpu.SemaphoreType.DMA((cols * zdim // 128,)),
            ]
        if not small:
            scratch.append(pltpu.VMEM((depth, 256), jnp.bfloat16))
        in_specs = [vmem] * len(operands)
        if not small:
            in_specs[len(lines)] = anywhere
        return pl.pallas_call(
            functools.partial(_band_kernel, masks, total is None, count if last else None, small),
            in_specs=in_specs,
            out_specs=anywhere if last else vmem,
            out_shape=jax.ShapeDtypeStruct(pair.shape, jnp.bfloat16)
            if last
            else jax.ShapeDtypeStruct((band, cols * zdim), jnp.float32),
            scratch_shapes=scratch,
            compiler_params=params,
            cost_estimate=pl.CostEstimate(
                flops=band * cols * zdim, bytes_accessed=band * cols, transcendentals=0
            ),
        )(*operands)

    upper, lower = _xor(x[:half], 4, n), _xor(y[half:], 2, n)
    across = _xor(jnp.stack([line, x, y]), 1, n)
    total = add([line, x, y, across], (0, 2, 4, 1, 3, 5), None, False)
    last = [_xor(upper, 1, n), _xor(lower, 1, n)]
    return add([upper, lower, *last], (6, 7), total, True)


def solution(mesh):
    placed = (P(("group", "row"), None, None), P("group", "row", None)) + (P(),) * 8
    return jax.shard_map(
        functools.partial(shards, mesh.shape["row"]),
        mesh=mesh,
        in_specs=placed,
        out_specs=P("group", "row", None),
        check_vma=False,
    )
```

```python
import functools

import jax
import jax.numpy as jnp
from jax import lax
from jax.experimental import pallas as pl
from jax.experimental.pallas import tpu as pltpu
from jax.sharding import PartitionSpec as P

LANES = 128
CHANS = 32
NT = (((1,), (1,)), ((), ()))


def _stacked(weights, copies):
    c, q = weights.shape
    rows = []
    for k in range(copies):
        left = [jnp.zeros((c, k * q), weights.dtype)] if k else []
        right = [jnp.zeros((c, (copies - 1 - k) * q), weights.dtype)] if k < copies - 1 else []
        rows.append(jnp.concatenate(left + [weights] + right, axis=1))
    return jnp.concatenate(rows, axis=0)


def _order(me, half):
    row = lax.broadcasted_iota(jnp.int32, (4 * LANES, 8 * CHANS), 0)
    col = lax.broadcasted_iota(jnp.int32, (4 * LANES, 8 * CHANS), 1)
    device = (row // LANES) ^ (me // 8 % 4)
    wanted = (row % CHANS) * 8 + ((row // CHANS) % 2) * 4 + device
    hit = (wanted == col) & ((row // (2 * CHANS)) % 2 == half)
    return jnp.where(hit, 1.0, 0.0).astype(jnp.bfloat16)


def _project_kernel(*refs):
    sources, final_source, outs, held = refs[:7], refs[7], refs[8:12], refs[12:19]
    left_ref, right_ref, final_ref, order_ref = outs
    sems = refs[19]
    pairs = [(sources[0].at[s], held[0].at[s]) for s in range(2)]
    pairs += list(zip(sources[1:], held[1:])) + [(final_source, final_ref)]
    copies = [pltpu.make_async_copy(a, b, sems.at[i]) for i, (a, b) in enumerate(pairs)]
    for copy in copies:
        copy.start()
    me = lax.axis_index("row")
    for h in range(2):
        order_ref[h] = _order(me, h)
    for copy in copies[:1] + copies[2:8]:
        copy.wait()
    x_ref, gain_ref, bias_ref, w1_ref, b1_ref, w2_ref, b2_ref = held
    half = left_ref.shape[0]
    n = right_ref.shape[0]
    feats = x_ref.shape[2]
    split = []
    for s in range(2):
        if s:
            copies[1].wait()
        x = x_ref[s].astype(jnp.float32)
        center = jnp.mean(x, axis=-1, keepdims=True)
        off = x - center
        spread = jnp.mean(off * off, axis=-1, keepdims=True)
        normed = off * lax.rsqrt(spread + 1e-05) * gain_ref[...] + bias_ref[...]
        split.append(normed.reshape(n, 2, 8, feats))
    parts = [split[s][:, jh].reshape(n * 8, feats).astype(jnp.bfloat16) for jh in range(2) for s in range(2)]
    weights = jnp.concatenate([_stacked(w1_ref[...], 4), _stacked(w2_ref[...], 4)], axis=0)
    shifts = jnp.concatenate([b1_ref[...]] * 4 + [b2_ref[...]] * 4, axis=1)
    both = lax.dot_general(jnp.concatenate(parts, axis=1), weights, NT, preferred_element_type=jnp.float32) + shifts
    left_ref[...] = both[:half, :LANES].astype(jnp.bfloat16)
    right_ref[...] = both[:, LANES:].reshape(n, 8, LANES).astype(jnp.bfloat16)
    copies[8].wait()


def _line_kernel(*refs):
    pieces, order_ref, out_ref = refs[:-2], refs[-2], refs[-1]
    half = pieces[0].shape[0]
    wide = order_ref.shape[2]
    for q in range(len(pieces) // 4):
        lhs = jnp.concatenate([pieces[q * 4 + k][...] for k in (0, 1, 3, 2)], axis=1)
        for h in range(2):
            moved = jnp.dot(lhs, order_ref[h], preferred_element_type=jnp.float32)
            out_ref[pl.ds(h * half, half), pl.ds(q * wide, wide)] = moved.astype(jnp.bfloat16)


def _fold_kernel(right_ref, final_ref, out_ref, block_ref, pairs_ref):
    devices = right_ref.shape[0]
    groups = devices // 4
    block_ref[...] = right_ref[...].astype(jnp.float32).reshape(devices * 8, LANES)
    for jr in range(8):
        for g in range(groups):
            four = block_ref[pl.ds(g * 8 + jr, 4, stride=groups * 8), :]
            for s in range(2):
                pairs_ref[pl.ds((jr * groups + g) * 8 + s * 4, 4), :] = four
    block = pairs_ref[...]
    lane = lax.broadcasted_iota(jnp.int32, block.shape, 1) // CHANS
    s = lax.broadcasted_iota(jnp.int32, block.shape, 0) // 4 % 2
    lhs = [jnp.where(lane == jh * 2 + s, block, 0.0).astype(jnp.bfloat16) for jh in range(2)]
    lhs = jnp.concatenate(lhs, axis=0)

    for pair in range(CHANS // 2):
        rhs = []
        for k in range(2):
            at = pair * 2 * CHANS + k * CHANS
            rhs.append(jnp.concatenate([final_ref[pl.ds(at, CHANS), :]] * 4, axis=0))
        res = jnp.dot(lhs, jnp.concatenate(rhs, axis=1), preferred_element_type=jnp.float32)
        for j in range(16):
            for g in range(groups):
                r = (j * groups + g) * 8
                tile = jnp.concatenate([res[r : r + 8, :LANES], res[r : r + 8, LANES:]], axis=0)
                out_ref[g, 0, pl.ds(pair * 16, 16), pl.ds(j * LANES, LANES)] = tile.astype(jnp.bfloat16)


def _band_kernel(masks, begins, count, held, *refs):
    refs = list(refs)
    take = lambda k: [refs.pop(0) for _ in range(k)]
    if masks == (3, 5):
        (block,) = take(1)
        lines = [block.at[k] for k in range(2)]
    else:
        lines = take(len(masks))
    (t_ref,) = take(1)
    (sum_ref,) = (None,) if begins else take(1)
    pair_ref, shift_ref = (None, None) if count is None else take(2)
    (out_ref,) = take(1)
    me = lax.axis_index("row")
    wide = t_ref.shape[2]
    chunks = [((me % 8) ^ mask, q ^ (me // 32)) for mask in masks for q in range(t_ref.shape[1])]

    tile = 256
    band = lines[0].shape[0]

    def column(step):
        at = pl.ds(step * tile, tile)
        if held:
            rhs = jnp.concatenate([t_ref[g, q, :, at] for g, q in chunks], axis=0)
        else:
            for i, (g, q) in enumerate(chunks):
                pltpu.sync_copy(t_ref.at[g, q, :, at], refs[0].at[pl.ds(i * wide, wide)])
            rhs = refs[0][...]
        lhs = jnp.concatenate([line[...] for line in lines], axis=1)
        res = jnp.dot(lhs, rhs, preferred_element_type=jnp.float32)
        return res if sum_ref is None else res + sum_ref[:, at]

    steps = t_ref.shape[3] // tile
    if count is None:
        for step in range(steps):
            out_ref[:, pl.ds(step * tile, tile)] = column(step)
        return

    acc_ref, done_ref, sems = take(3)
    cols = pair_ref.shape[1]
    pitch = cols + 1
    shift = shift_ref[...]
    chunk = band // 2 // steps

    def finish(r):
        for k in range(chunk):
            i = r * chunk + k
            row = (i // 8) % 2 * (band // 2) + i // 16 * 8 + i % 8
            total = acc_ref[pl.ds(row * pitch, cols), :] * (1.0 / count) + shift
            done_ref[i] = (pair_ref[i].astype(jnp.float32) + total).astype(jnp.bfloat16)
        at = pl.ds(r * chunk, chunk)
        pltpu.make_async_copy(done_ref.at[at], out_ref.at[at], sems.at[r]).start()

    for step in range(steps):
        res = column(step)
        for k in range(tile // LANES):
            j = step * (tile // LANES) + k
            acc_ref[pl.ds(j, band, stride=pitch), :] = res[:, k * LANES : (k + 1) * LANES]
    for r in range(2 * steps):
        finish(r)
    for r in range(2 * steps):
        at = pl.ds(r * chunk, chunk)
        pltpu.make_async_copy(done_ref.at[at], out_ref.at[at], sems.at[r]).wait()


def _xor(x, mask, n):
    return lax.ppermute(x, "row", [(i, i ^ mask) for i in range(n)])


def shards(n, alignment, pair, gain, bias, w1, b1, w2, b2, final, shift):
    seqs, residues, feats = alignment.shape
    band, cols, zdim = pair.shape
    half = band // 2
    count = float(seqs * n)
    small = n <= 32
    params = pltpu.CompilerParams(vmem_limit_bytes=(24 if small else 48) * 1024 * 1024)
    anywhere = pl.BlockSpec(memory_space=pl.ANY)
    vmem = pl.BlockSpec(memory_space=pltpu.VMEM)

    sources = [
        alignment, gain.reshape(1, -1), bias.reshape(1, -1), w1.T, b1.reshape(1, -1), w2.T, b2.reshape(1, -1)
    ]
    sources = [pltpu.with_memory_space_constraint(a, pltpu.HBM) for a in sources]
    left, right, final, order = pl.pallas_call(
        _project_kernel,
        in_specs=[anywhere] * 8,
        out_specs=(vmem,) * 4,
        out_shape=(
            jax.ShapeDtypeStruct((half, LANES), jnp.bfloat16),
            jax.ShapeDtypeStruct((n, 8, LANES), jnp.bfloat16),
            jax.ShapeDtypeStruct(final.shape, final.dtype),
            jax.ShapeDtypeStruct((2, 4 * LANES, 8 * CHANS), jnp.bfloat16),
        ),
        scratch_shapes=[pltpu.VMEM(a.shape, a.dtype) for a in sources] + [pltpu.SemaphoreType.DMA((9,))],
        compiler_params=params,
        cost_estimate=pl.CostEstimate(
            flops=4 * seqs * residues * feats * CHANS, bytes_accessed=2 * seqs * residues * feats, transcendentals=0
        ),
    )(*sources, pltpu.with_memory_space_constraint(final, pltpu.HBM))

    right = lax.all_to_all(right, "row", split_axis=0, concat_axis=0, tiled=True)

    part = 32
    parts = n // part
    pieces = [left] + [_xor(left, m, n) for m in range(8, n, 8)]
    pieces = [pieces[k ^ (k // 2 % 2)] for k in range(len(pieces))]
    line = pl.pallas_call(
        _line_kernel,
        in_specs=[vmem] * (len(pieces) + 1),
        out_specs=vmem,
        out_shape=jax.ShapeDtypeStruct((band, parts * 8 * CHANS), jnp.bfloat16),
        compiler_params=params,
        cost_estimate=pl.CostEstimate(flops=2**27, bytes_accessed=2**20, transcendentals=0),
    )(*pieces, order)
    x, y, diagonal = (_xor(line, m, n) for m in (2, 4, 6))

    fold_cost = pl.CostEstimate(
        flops=2 * n * 32 * 256 * CHANS * zdim, bytes_accessed=4 * n * CHANS * cols * zdim, transcendentals=0
    )
    fold_out = jax.ShapeDtypeStruct((8, parts, 8 * CHANS, cols * zdim), jnp.bfloat16)
    if small:
        specs = dict(in_specs=[vmem, vmem], out_specs=vmem)
    else:
        specs = dict(
            grid=(parts,),
            in_specs=[
                pl.BlockSpec((part, 8, LANES), lambda i: (i, 0, 0)),
                pl.BlockSpec(final.shape, lambda i: (0, 0)),
            ],
            out_specs=pl.BlockSpec((8, 1, 8 * CHANS, cols * zdim), lambda i: (0, i, 0, 0)),
        )
    folded = pl.pallas_call(
        _fold_kernel,
        out_shape=fold_out,
        scratch_shapes=[pltpu.VMEM((part * 8, LANES), jnp.float32), pltpu.VMEM((part * 16, LANES), jnp.float32)],
        compiler_params=params,
        cost_estimate=fold_cost,
        **specs,
    )(right, final)

    def add(lines, masks, total, last):
        depth = len(masks) * parts * 8 * CHANS
        scratch = []
        operands = [*lines, folded] + ([] if total is None else [total])
        if last:
            operands += [pair, shift.reshape(1, -1)]
            scratch += [
                pltpu.VMEM((band * (cols + 1), zdim), jnp.float32),
                pltpu.VMEM(pair.shape, jnp.bfloat16),
                pltpu.SemaphoreType.DMA((cols * zdim // 128,)),
            ]
        if not small:
            scratch.append(pltpu.VMEM((depth, 256), jnp.bfloat16))
        in_specs = [vmem] * len(operands)
        if not small:
            in_specs[len(lines)] = anywhere
        return pl.pallas_call(
            functools.partial(_band_kernel, masks, total is None, count if last else None, small),
            in_specs=in_specs,
            out_specs=anywhere if last else vmem,
            out_shape=jax.ShapeDtypeStruct(pair.shape, jnp.bfloat16)
            if last
            else jax.ShapeDtypeStruct((band, cols * zdim), jnp.float32),
            scratch_shapes=scratch,
            compiler_params=params,
            cost_estimate=pl.CostEstimate(
                flops=band * cols * zdim, bytes_accessed=band * cols, transcendentals=0
            ),
        )(*operands)

    total = add([line, _xor(line, 1, n)], (0, 1), None, False)
    x, y, total = lax.optimization_barrier((x, y, total))
    across = _xor(jnp.stack([x, y]), 1, n)
    total = add([x, y], (2, 4), total, False)
    total = add([across], (3, 5), total, False)
    diagonal, total = lax.optimization_barrier((diagonal, total))
    last = _xor(diagonal, 1, n)
    total = add([diagonal], (6,), total, False)
    return add([last], (7,), total, True)


def solution(mesh):
    placed = (P(("group", "row"), None, None), P("group", "row", None)) + (P(),) * 8
    return jax.shard_map(
        functools.partial(shards, mesh.shape["row"]),
        mesh=mesh,
        in_specs=placed,
        out_specs=P("group", "row", None),
        check_vma=False,
    )
```

```python
import functools

import jax
import jax.numpy as jnp
from jax import lax
from jax.experimental import pallas as pl
from jax.experimental.pallas import tpu as pltpu
from jax.sharding import PartitionSpec as P

LANES = 128
CHANS = 32
NT = (((1,), (1,)), ((), ()))


def _stacked(weights, copies):
    c, q = weights.shape
    rows = []
    for k in range(copies):
        left = [jnp.zeros((c, k * q), weights.dtype)] if k else []
        right = [jnp.zeros((c, (copies - 1 - k) * q), weights.dtype)] if k < copies - 1 else []
        rows.append(jnp.concatenate(left + [weights] + right, axis=1))
    return jnp.concatenate(rows, axis=0)


def _order(me, half):
    row = lax.broadcasted_iota(jnp.int32, (4 * LANES, 8 * CHANS), 0)
    col = lax.broadcasted_iota(jnp.int32, (4 * LANES, 8 * CHANS), 1)
    device = (row // LANES) ^ (me // 8 % 4)
    wanted = (row % CHANS) * 8 + ((row // CHANS) % 2) * 4 + device
    hit = (wanted == col) & ((row // (2 * CHANS)) % 2 == half)
    return jnp.where(hit, 1.0, 0.0).astype(jnp.bfloat16)


def _project_kernel(*refs):
    sources, final_source, outs, held = refs[:7], refs[7], refs[8:12], refs[12:19]
    left_ref, right_ref, final_ref, order_ref = outs
    sems = refs[19]
    pairs = [(sources[0].at[s], held[0].at[s]) for s in range(2)]
    pairs += list(zip(sources[1:], held[1:])) + [(final_source, final_ref)]
    copies = [pltpu.make_async_copy(a, b, sems.at[i]) for i, (a, b) in enumerate(pairs)]
    for copy in copies:
        copy.start()
    me = lax.axis_index("row")
    for h in range(2):
        order_ref[h] = _order(me, h)
    for copy in copies[:1] + copies[2:8]:
        copy.wait()
    x_ref, gain_ref, bias_ref, w1_ref, b1_ref, w2_ref, b2_ref = held
    half = left_ref.shape[0]
    n = right_ref.shape[0]
    feats = x_ref.shape[2]
    split = []
    for s in range(2):
        if s:
            copies[1].wait()
        x = x_ref[s].astype(jnp.float32)
        center = jnp.mean(x, axis=-1, keepdims=True)
        off = x - center
        spread = jnp.mean(off * off, axis=-1, keepdims=True)
        normed = off * lax.rsqrt(spread + 1e-05) * gain_ref[...] + bias_ref[...]
        split.append(normed.reshape(n, 2, 8, feats))
    parts = [split[s][:, jh].reshape(n * 8, feats).astype(jnp.bfloat16) for jh in range(2) for s in range(2)]
    weights = jnp.concatenate([_stacked(w1_ref[...], 4), _stacked(w2_ref[...], 4)], axis=0)
    shifts = jnp.concatenate([b1_ref[...]] * 4 + [b2_ref[...]] * 4, axis=1)
    both = lax.dot_general(jnp.concatenate(parts, axis=1), weights, NT, preferred_element_type=jnp.float32) + shifts
    left_ref[...] = both[:half, :LANES].astype(jnp.bfloat16)
    right_ref[...] = both[:, LANES:].reshape(n, 8, LANES).astype(jnp.bfloat16)
    copies[8].wait()


def _line_kernel(*refs):
    pieces, order_ref, out_ref = refs[:-2], refs[-2], refs[-1]
    half = pieces[0].shape[0]
    wide = order_ref.shape[2]
    for q in range(len(pieces) // 4):
        lhs = jnp.concatenate([pieces[q * 4 + k][...] for k in (0, 1, 3, 2)], axis=1)
        for h in range(2):
            moved = jnp.dot(lhs, order_ref[h], preferred_element_type=jnp.float32)
            out_ref[pl.ds(h * half, half), pl.ds(q * wide, wide)] = moved.astype(jnp.bfloat16)


def _fold_kernel(right_ref, final_ref, out_ref, block_ref, pairs_ref):
    devices = right_ref.shape[0]
    groups = devices // 4
    block_ref[...] = right_ref[...].astype(jnp.float32).reshape(devices * 8, LANES)
    for jr in range(8):
        for g in range(groups):
            four = block_ref[pl.ds(g * 8 + jr, 4, stride=groups * 8), :]
            for s in range(2):
                pairs_ref[pl.ds((jr * groups + g) * 8 + s * 4, 4), :] = four
    block = pairs_ref[...]
    lane = lax.broadcasted_iota(jnp.int32, block.shape, 1) // CHANS
    s = lax.broadcasted_iota(jnp.int32, block.shape, 0) // 4 % 2
    lhs = [jnp.where(lane == jh * 2 + s, block, 0.0).astype(jnp.bfloat16) for jh in range(2)]
    lhs = jnp.concatenate(lhs, axis=0)

    for pair in range(CHANS // 2):
        rhs = []
        for k in range(2):
            at = pair * 2 * CHANS + k * CHANS
            rhs.append(jnp.concatenate([final_ref[pl.ds(at, CHANS), :]] * 4, axis=0))
        res = jnp.dot(lhs, jnp.concatenate(rhs, axis=1), preferred_element_type=jnp.float32)
        for j in range(16):
            for g in range(groups):
                r = (j * groups + g) * 8
                tile = jnp.concatenate([res[r : r + 8, :LANES], res[r : r + 8, LANES:]], axis=0)
                out_ref[g, 0, pl.ds(pair * 16, 16), pl.ds(j * LANES, LANES)] = tile.astype(jnp.bfloat16)


def _band_kernel(masks, begins, count, held, *refs):
    refs = list(refs)
    take = lambda k: [refs.pop(0) for _ in range(k)]
    if masks == (1, 3, 5):
        (block,) = take(1)
        lines = [[block.at[k]] for k in range(3)]
    else:
        lines = [take(2 if mask in (6, 7) else 1) for mask in masks]
    (t_ref,) = take(1)
    (sum_ref,) = (None,) if begins else take(1)
    pair_ref, shift_ref = (None, None) if count is None else take(2)
    (out_ref,) = take(1)
    me = lax.axis_index("row")
    wide = t_ref.shape[2]
    chunks = [((me % 8) ^ mask, q ^ (me // 32)) for mask in masks for q in range(t_ref.shape[1])]

    tile = 256
    band = sum(part.shape[0] for part in lines[0])

    def column(step):
        at = pl.ds(step * tile, tile)
        if held:
            rhs = jnp.concatenate([t_ref[g, q, :, at] for g, q in chunks], axis=0)
        else:
            for i, (g, q) in enumerate(chunks):
                pltpu.sync_copy(t_ref.at[g, q, :, at], refs[0].at[pl.ds(i * wide, wide)])
            rhs = refs[0][...]
        lhs = jnp.concatenate([jnp.concatenate([part[...] for part in line], axis=0) for line in lines], axis=1)
        res = jnp.dot(lhs, rhs, preferred_element_type=jnp.float32)
        return res if sum_ref is None else res + sum_ref[:, at]

    steps = t_ref.shape[3] // tile
    if count is None:
        for step in range(steps):
            out_ref[:, pl.ds(step * tile, tile)] = column(step)
        return

    acc_ref, done_ref, sems = take(3)
    cols = pair_ref.shape[1]
    pitch = cols + 1
    shift = shift_ref[...]
    for step in range(steps):
        res = column(step)
        for k in range(tile // LANES):
            j = step * (tile // LANES) + k
            acc_ref[pl.ds(j, band, stride=pitch), :] = res[:, k * LANES : (k + 1) * LANES]

    chunk = 32

    def finish(r, _):
        for k in range(chunk):
            i = r * chunk + k
            row = k // 8 % 2 * (band // 2) + (r * (chunk // 16) + k // 16) * 8 + k % 8
            total = acc_ref[pl.ds(row * pitch, cols), :] * (1.0 / count) + shift
            done_ref[i] = (pair_ref[i].astype(jnp.float32) + total).astype(jnp.bfloat16)
        at = pl.ds(pl.multiple_of(r * chunk, chunk), chunk)
        pltpu.make_async_copy(done_ref.at[at], out_ref.at[at], sems.at[r]).start()
        return 0

    lax.fori_loop(0, band // chunk, finish, 0)

    def drain(r, _):
        at = pl.ds(pl.multiple_of(r * chunk, chunk), chunk)
        pltpu.make_async_copy(done_ref.at[at], out_ref.at[at], sems.at[r]).wait()
        return 0

    lax.fori_loop(0, band // chunk, drain, 0)


def _xor(x, mask, n):
    return lax.ppermute(x, "row", [(i, i ^ mask) for i in range(n)])


def shards(n, alignment, pair, gain, bias, w1, b1, w2, b2, final, shift):
    seqs, residues, feats = alignment.shape
    band, cols, zdim = pair.shape
    half = band // 2
    count = float(seqs * n)
    small = n <= 32
    params = pltpu.CompilerParams(vmem_limit_bytes=(24 if small else 48) * 1024 * 1024)
    anywhere = pl.BlockSpec(memory_space=pl.ANY)
    vmem = pl.BlockSpec(memory_space=pltpu.VMEM)

    sources = [
        alignment, gain.reshape(1, -1), bias.reshape(1, -1), w1.T, b1.reshape(1, -1), w2.T, b2.reshape(1, -1)
    ]
    sources = [pltpu.with_memory_space_constraint(a, pltpu.HBM) for a in sources]
    left, right, final, order = pl.pallas_call(
        _project_kernel,
        in_specs=[anywhere] * 8,
        out_specs=(vmem,) * 4,
        out_shape=(
            jax.ShapeDtypeStruct((half, LANES), jnp.bfloat16),
            jax.ShapeDtypeStruct((n, 8, LANES), jnp.bfloat16),
            jax.ShapeDtypeStruct(final.shape, final.dtype),
            jax.ShapeDtypeStruct((2, 4 * LANES, 8 * CHANS), jnp.bfloat16),
        ),
        scratch_shapes=[pltpu.VMEM(a.shape, a.dtype) for a in sources] + [pltpu.SemaphoreType.DMA((9,))],
        compiler_params=params,
        cost_estimate=pl.CostEstimate(
            flops=4 * seqs * residues * feats * CHANS, bytes_accessed=2 * seqs * residues * feats, transcendentals=0
        ),
    )(*sources, pltpu.with_memory_space_constraint(final, pltpu.HBM))

    right = lax.all_to_all(right, "row", split_axis=0, concat_axis=0, tiled=True)

    part = 32
    parts = n // part
    pieces = [left] + [_xor(left, m, n) for m in range(8, n, 8)]
    pieces = [pieces[k ^ (k // 2 % 2)] for k in range(len(pieces))]
    line = pl.pallas_call(
        _line_kernel,
        in_specs=[vmem] * (len(pieces) + 1),
        out_specs=vmem,
        out_shape=jax.ShapeDtypeStruct((band, parts * 8 * CHANS), jnp.bfloat16),
        compiler_params=params,
        cost_estimate=pl.CostEstimate(flops=2**27, bytes_accessed=2**20, transcendentals=0),
    )(*pieces, order)
    x, y = _xor(line, 2, n), _xor(line, 4, n)

    fold_cost = pl.CostEstimate(
        flops=2 * n * 32 * 256 * CHANS * zdim, bytes_accessed=4 * n * CHANS * cols * zdim, transcendentals=0
    )
    fold_out = jax.ShapeDtypeStruct((8, parts, 8 * CHANS, cols * zdim), jnp.bfloat16)
    if small:
        specs = dict(in_specs=[vmem, vmem], out_specs=vmem)
    else:
        specs = dict(
            grid=(parts,),
            in_specs=[
                pl.BlockSpec((part, 8, LANES), lambda i: (i, 0, 0)),
                pl.BlockSpec(final.shape, lambda i: (0, 0)),
            ],
            out_specs=pl.BlockSpec((8, 1, 8 * CHANS, cols * zdim), lambda i: (0, i, 0, 0)),
        )
    folded = pl.pallas_call(
        _fold_kernel,
        out_shape=fold_out,
        scratch_shapes=[pltpu.VMEM((part * 8, LANES), jnp.float32), pltpu.VMEM((part * 16, LANES), jnp.float32)],
        compiler_params=params,
        cost_estimate=fold_cost,
        **specs,
    )(right, final)

    def add(lines, masks, total, last):
        depth = len(masks) * parts * 8 * CHANS
        scratch = []
        operands = [*lines, folded] + ([] if total is None else [total])
        if last:
            operands += [pair, shift.reshape(1, -1)]
            scratch += [
                pltpu.VMEM((band * (cols + 1), zdim), jnp.float32),
                pltpu.VMEM(pair.shape, jnp.bfloat16),
                pltpu.SemaphoreType.DMA((band // 32,)),
            ]
        if not small:
            scratch.append(pltpu.VMEM((depth, 256), jnp.bfloat16))
        in_specs = [vmem] * len(operands)
        if not small:
            in_specs[len(lines)] = anywhere
        return pl.pallas_call(
            functools.partial(_band_kernel, masks, total is None, count if last else None, small),
            in_specs=in_specs,
            out_specs=anywhere if last else vmem,
            out_shape=jax.ShapeDtypeStruct(pair.shape, jnp.bfloat16)
            if last
            else jax.ShapeDtypeStruct((band, cols * zdim), jnp.float32),
            scratch_shapes=scratch,
            compiler_params=params,
            cost_estimate=pl.CostEstimate(
                flops=band * cols * zdim, bytes_accessed=band * cols, transcendentals=0
            ),
        )(*operands)

    x, y, folded = lax.optimization_barrier((x, y, folded))
    cut = band * 9 // 16
    upper, lower = _xor(x[:cut], 4, n), _xor(y[cut:], 2, n)
    across = _xor(jnp.stack([line, x, y]), 1, n)
    total = add([line, x, y], (0, 2, 4), None, False)
    total = add([across], (1, 3, 5), total, False)
    upper, total = lax.optimization_barrier((upper, total))
    last = [_xor(upper, 1, n)]
    lower, total = lax.optimization_barrier((lower, total))
    last.append(_xor(lower, 1, n))
    total = add([upper, lower], (6,), total, False)
    return add(last, (7,), total, True)


def solution(mesh):
    placed = (P(("group", "row"), None, None), P("group", "row", None)) + (P(),) * 8
    return jax.shard_map(
        functools.partial(shards, mesh.shape["row"]),
        mesh=mesh,
        in_specs=placed,
        out_specs=P("group", "row", None),
        check_vma=False,
    )
```

```python
import functools

import jax
import jax.numpy as jnp
from jax import lax
from jax.experimental import pallas as pl
from jax.experimental.pallas import tpu as pltpu
from jax.sharding import PartitionSpec as P

LANES = 128
CHANS = 32
NT = (((1,), (1,)), ((), ()))


def _stacked(weights, copies):
    c, q = weights.shape
    rows = []
    for k in range(copies):
        left = [jnp.zeros((c, k * q), weights.dtype)] if k else []
        right = [jnp.zeros((c, (copies - 1 - k) * q), weights.dtype)] if k < copies - 1 else []
        rows.append(jnp.concatenate(left + [weights] + right, axis=1))
    return jnp.concatenate(rows, axis=0)


def _order(me, half):
    row = lax.broadcasted_iota(jnp.int32, (4 * LANES, 8 * CHANS), 0)
    col = lax.broadcasted_iota(jnp.int32, (4 * LANES, 8 * CHANS), 1)
    device = (row // LANES) ^ (me // 8 % 4)
    wanted = (row % CHANS) * 8 + ((row // CHANS) % 2) * 4 + device
    hit = (wanted == col) & ((row // (2 * CHANS)) % 2 == half)
    return jnp.where(hit, 1.0, 0.0).astype(jnp.bfloat16)


def _project_kernel(*refs):
    sources, final_source, outs, held = refs[:7], refs[7], refs[8:12], refs[12:19]
    left_ref, right_ref, final_ref, order_ref = outs
    sems = refs[19]
    pairs = [(sources[0].at[s], held[0].at[s]) for s in range(2)]
    pairs += list(zip(sources[1:], held[1:])) + [(final_source, final_ref)]
    copies = [pltpu.make_async_copy(a, b, sems.at[i]) for i, (a, b) in enumerate(pairs)]
    for copy in copies:
        copy.start()
    me = lax.axis_index("row")
    for h in range(2):
        order_ref[h] = _order(me, h)
    for copy in copies[:1] + copies[2:8]:
        copy.wait()
    x_ref, gain_ref, bias_ref, w1_ref, b1_ref, w2_ref, b2_ref = held
    half = left_ref.shape[0]
    n = right_ref.shape[0]
    feats = x_ref.shape[2]
    split = []
    for s in range(2):
        if s:
            copies[1].wait()
        x = x_ref[s].astype(jnp.float32)
        center = jnp.mean(x, axis=-1, keepdims=True)
        off = x - center
        spread = jnp.mean(off * off, axis=-1, keepdims=True)
        normed = off * lax.rsqrt(spread + 1e-05) * gain_ref[...] + bias_ref[...]
        split.append(normed.reshape(n, 2, 8, feats))
    parts = [split[s][:, jh].reshape(n * 8, feats).astype(jnp.bfloat16) for jh in range(2) for s in range(2)]
    weights = jnp.concatenate([_stacked(w1_ref[...], 4), _stacked(w2_ref[...], 4)], axis=0)
    shifts = jnp.concatenate([b1_ref[...]] * 4 + [b2_ref[...]] * 4, axis=1)
    both = lax.dot_general(jnp.concatenate(parts, axis=1), weights, NT, preferred_element_type=jnp.float32) + shifts
    left_ref[...] = both[:half, :LANES].astype(jnp.bfloat16)
    right_ref[...] = both[:, LANES:].reshape(n, 8, LANES).astype(jnp.bfloat16)
    copies[8].wait()


def _line_kernel(*refs):
    pieces, order_ref, out_ref = refs[:-2], refs[-2], refs[-1]
    half = pieces[0].shape[0]
    wide = order_ref.shape[2]
    for q in range(len(pieces) // 4):
        lhs = jnp.concatenate([pieces[q * 4 + k][...] for k in (0, 1, 3, 2)], axis=1)
        for h in range(2):
            moved = jnp.dot(lhs, order_ref[h], preferred_element_type=jnp.float32)
            out_ref[pl.ds(h * half, half), pl.ds(q * wide, wide)] = moved.astype(jnp.bfloat16)


def _fold_kernel(right_ref, final_ref, out_ref, block_ref, pairs_ref):
    devices = right_ref.shape[0]
    groups = devices // 4
    block_ref[...] = right_ref[...].astype(jnp.float32).reshape(devices * 8, LANES)
    for jr in range(8):
        for g in range(groups):
            four = block_ref[pl.ds(g * 8 + jr, 4, stride=groups * 8), :]
            for s in range(2):
                pairs_ref[pl.ds((jr * groups + g) * 8 + s * 4, 4), :] = four
    block = pairs_ref[...]
    lane = lax.broadcasted_iota(jnp.int32, block.shape, 1) // CHANS
    s = lax.broadcasted_iota(jnp.int32, block.shape, 0) // 4 % 2
    lhs = [jnp.where(lane == jh * 2 + s, block, 0.0).astype(jnp.bfloat16) for jh in range(2)]
    lhs = jnp.concatenate(lhs, axis=0)

    def columns(r, _):
        for u in range(4):
            column(r * 4 + u)
        return 0

    def column(pair):
        rhs = []
        for k in range(2):
            at = pl.multiple_of(pair * 2 * CHANS + k * CHANS, CHANS)
            rhs.append(jnp.concatenate([final_ref[pl.ds(at, CHANS), :]] * 4, axis=0))
        res = jnp.dot(lhs, jnp.concatenate(rhs, axis=1), preferred_element_type=jnp.float32)
        for j in range(16):
            for g in range(groups):
                r = (j * groups + g) * 8
                tile = jnp.concatenate([res[r : r + 8, :LANES], res[r : r + 8, LANES:]], axis=0)
                out_ref[g, 0, pl.ds(pl.multiple_of(pair * 16, 16), 16), pl.ds(j * LANES, LANES)] = tile.astype(
                    jnp.bfloat16
                )

    lax.fori_loop(0, CHANS // 8, columns, 0)


def _band_kernel(masks, begins, scale, last, held, *refs):
    refs = list(refs)
    take = lambda k: [refs.pop(0) for _ in range(k)]
    if masks == (1, 3, 5):
        (block,) = take(1)
        lines = [[block.at[k]] for k in range(3)]
    else:
        lines = [take(2 if mask in (6, 7) else 1) for mask in masks]
    (t_ref,) = take(1)
    (sum_ref,) = (None,) if begins else take(1)
    shift_ref = None if scale is None or last else take(1)[0]
    pair_ref = take(1)[0] if last else None
    (out_ref,) = take(1)
    me = lax.axis_index("row")
    wide = t_ref.shape[2]
    chunks = [((me % 8) ^ mask, q ^ (me // 32)) for mask in masks for q in range(t_ref.shape[1])]

    tile = 256
    band = sum(part.shape[0] for part in lines[0])

    def column(begin):
        at = pl.ds(pl.multiple_of(begin, tile), tile)
        if held:
            rhs = jnp.concatenate([t_ref[g, q, :, at] for g, q in chunks], axis=0)
        else:
            for i, (g, q) in enumerate(chunks):
                pltpu.sync_copy(t_ref.at[g, q, :, at], refs[0].at[pl.ds(i * wide, wide)])
            rhs = refs[0][...]
        lhs = jnp.concatenate([jnp.concatenate([part[...] for part in line], axis=0) for line in lines], axis=1)
        res = jnp.dot(lhs, rhs, preferred_element_type=jnp.float32)
        if last:
            return res * scale + sum_ref[:, at]
        if sum_ref is not None:
            res = res + sum_ref[:, at]
        if shift_ref is not None:
            res = res * scale + jnp.concatenate([shift_ref[...]] * (tile // LANES), axis=1)
        return res

    if last:
        acc_ref, done_ref, sems = take(3)
        cols = pair_ref.shape[1]
        pitch = cols + 1
    unrolled = 4

    def columns(r, _):
        for u in range(unrolled):
            step = r * unrolled + u
            res = column(step * tile)
            if not last:
                out_ref[:, pl.ds(pl.multiple_of(step * tile, tile), tile)] = res
                continue
            for k in range(tile // LANES):
                j = step * (tile // LANES) + k
                acc_ref[pl.ds(j, band, stride=pitch), :] = res[:, k * LANES : (k + 1) * LANES]
        return 0

    lax.fori_loop(0, t_ref.shape[3] // tile // unrolled, columns, 0)
    if not last:
        return

    chunk = 32

    def finish(r, _):
        for k in range(chunk):
            i = r * chunk + k
            row = k // 8 % 2 * (band // 2) + (r * (chunk // 16) + k // 16) * 8 + k % 8
            total = acc_ref[pl.ds(row * pitch, cols), :]
            done_ref[i] = (pair_ref[i].astype(jnp.float32) + total).astype(jnp.bfloat16)
        at = pl.ds(pl.multiple_of(r * chunk, chunk), chunk)
        pltpu.make_async_copy(done_ref.at[at], out_ref.at[at], sems.at[r]).start()
        return 0

    lax.fori_loop(0, band // chunk, finish, 0)

    def drain(r, _):
        at = pl.ds(pl.multiple_of(r * chunk, chunk), chunk)
        pltpu.make_async_copy(done_ref.at[at], out_ref.at[at], sems.at[r]).wait()
        return 0

    lax.fori_loop(0, band // chunk, drain, 0)


def _xor(x, mask, n):
    return lax.ppermute(x, "row", [(i, i ^ mask) for i in range(n)])


def shards(n, alignment, pair, gain, bias, w1, b1, w2, b2, final, shift):
    seqs, residues, feats = alignment.shape
    band, cols, zdim = pair.shape
    half = band // 2
    count = float(seqs * n)
    small = n <= 32
    params = pltpu.CompilerParams(vmem_limit_bytes=(24 if small else 48) * 1024 * 1024)
    anywhere = pl.BlockSpec(memory_space=pl.ANY)
    vmem = pl.BlockSpec(memory_space=pltpu.VMEM)

    sources = [
        alignment, gain.reshape(1, -1), bias.reshape(1, -1), w1.T, b1.reshape(1, -1), w2.T, b2.reshape(1, -1)
    ]
    sources = [pltpu.with_memory_space_constraint(a, pltpu.HBM) for a in sources]
    left, right, final, order = pl.pallas_call(
        _project_kernel,
        in_specs=[anywhere] * 8,
        out_specs=(vmem,) * 4,
        out_shape=(
            jax.ShapeDtypeStruct((half, LANES), jnp.bfloat16),
            jax.ShapeDtypeStruct((n, 8, LANES), jnp.bfloat16),
            jax.ShapeDtypeStruct(final.shape, final.dtype),
            jax.ShapeDtypeStruct((2, 4 * LANES, 8 * CHANS), jnp.bfloat16),
        ),
        scratch_shapes=[pltpu.VMEM(a.shape, a.dtype) for a in sources] + [pltpu.SemaphoreType.DMA((9,))],
        compiler_params=params,
        cost_estimate=pl.CostEstimate(
            flops=4 * seqs * residues * feats * CHANS, bytes_accessed=2 * seqs * residues * feats, transcendentals=0
        ),
    )(*sources, pltpu.with_memory_space_constraint(final, pltpu.HBM))

    right = lax.all_to_all(right, "row", split_axis=0, concat_axis=0, tiled=True)

    part = 32
    parts = n // part
    pieces = [left] + [_xor(left, m, n) for m in range(8, n, 8)]
    pieces = [pieces[k ^ (k // 2 % 2)] for k in range(len(pieces))]
    line = pl.pallas_call(
        _line_kernel,
        in_specs=[vmem] * (len(pieces) + 1),
        out_specs=vmem,
        out_shape=jax.ShapeDtypeStruct((band, parts * 8 * CHANS), jnp.bfloat16),
        compiler_params=params,
        cost_estimate=pl.CostEstimate(flops=2**27, bytes_accessed=2**20, transcendentals=0),
    )(*pieces, order)
    x, y = _xor(line, 2, n), _xor(line, 4, n)

    fold_cost = pl.CostEstimate(
        flops=2 * n * 32 * 256 * CHANS * zdim, bytes_accessed=4 * n * CHANS * cols * zdim, transcendentals=0
    )
    fold_out = jax.ShapeDtypeStruct((8, parts, 8 * CHANS, cols * zdim), jnp.bfloat16)
    if small:
        specs = dict(in_specs=[vmem, vmem], out_specs=vmem)
    else:
        specs = dict(
            grid=(parts,),
            in_specs=[
                pl.BlockSpec((part, 8, LANES), lambda i: (i, 0, 0)),
                pl.BlockSpec(final.shape, lambda i: (0, 0)),
            ],
            out_specs=pl.BlockSpec((8, 1, 8 * CHANS, cols * zdim), lambda i: (0, i, 0, 0)),
        )
    folded = pl.pallas_call(
        _fold_kernel,
        out_shape=fold_out,
        scratch_shapes=[pltpu.VMEM((part * 8, LANES), jnp.float32), pltpu.VMEM((part * 16, LANES), jnp.float32)],
        compiler_params=params,
        cost_estimate=fold_cost,
        **specs,
    )(right, final)

    def add(lines, masks, total, last, scaled=False):
        depth = len(masks) * parts * 8 * CHANS
        scratch = []
        operands = [*lines, folded] + ([] if total is None else [total])
        if scaled and not last:
            operands.append(shift.reshape(1, -1))
        if last:
            operands.append(pair)
            scratch += [
                pltpu.VMEM((band * (cols + 1), zdim), jnp.float32),
                pltpu.VMEM(pair.shape, jnp.bfloat16),
                pltpu.SemaphoreType.DMA((band // 32,)),
            ]
        if not small:
            scratch.append(pltpu.VMEM((depth, 256), jnp.bfloat16))
        in_specs = [vmem] * len(operands)
        if not small:
            in_specs[len(lines)] = anywhere
        return pl.pallas_call(
            functools.partial(_band_kernel, masks, total is None, 1.0 / count if scaled else None, last, small),
            in_specs=in_specs,
            out_specs=anywhere if last else vmem,
            out_shape=jax.ShapeDtypeStruct(pair.shape, jnp.bfloat16)
            if last
            else jax.ShapeDtypeStruct((band, cols * zdim), jnp.float32),
            scratch_shapes=scratch,
            compiler_params=params,
            cost_estimate=pl.CostEstimate(
                flops=band * cols * zdim, bytes_accessed=band * cols, transcendentals=0
            ),
        )(*operands)

    x, y, folded = lax.optimization_barrier((x, y, folded))
    cut = band * 9 // 16
    upper, lower = _xor(x[:cut], 4, n), _xor(y[cut:], 2, n)
    across = _xor(jnp.stack([line, x, y]), 1, n)
    total = add([line, x, y], (0, 2, 4), None, False)
    total = add([across], (1, 3, 5), total, False)
    upper, total = lax.optimization_barrier((upper, total))
    last = [_xor(upper, 1, n)]
    lower, total = lax.optimization_barrier((lower, total))
    last.append(_xor(lower, 1, n))
    total = add([upper, lower], (6,), total, False, True)
    return add(last, (7,), total, True, True)


def solution(mesh):
    placed = (P(("group", "row"), None, None), P("group", "row", None)) + (P(),) * 8
    return jax.shard_map(
        functools.partial(shards, mesh.shape["row"]),
        mesh=mesh,
        in_specs=placed,
        out_specs=P("group", "row", None),
        check_vma=False,
    )
```

```python
import functools

import jax
import jax.numpy as jnp
from jax import lax
from jax.experimental import pallas as pl
from jax.experimental.pallas import tpu as pltpu
from jax.sharding import PartitionSpec as P

LANES = 128
CHANS = 32
NT = (((1,), (1,)), ((), ()))


def _stacked(weights, copies):
    c, q = weights.shape
    rows = []
    for k in range(copies):
        left = [jnp.zeros((c, k * q), weights.dtype)] if k else []
        right = [jnp.zeros((c, (copies - 1 - k) * q), weights.dtype)] if k < copies - 1 else []
        rows.append(jnp.concatenate(left + [weights] + right, axis=1))
    return jnp.concatenate(rows, axis=0)


def _order(me, half):
    row = lax.broadcasted_iota(jnp.int32, (4 * LANES, 8 * CHANS), 0)
    col = lax.broadcasted_iota(jnp.int32, (4 * LANES, 8 * CHANS), 1)
    device = (row // LANES) ^ (me // 8 % 4)
    wanted = (row % CHANS) * 8 + ((row // CHANS) % 2) * 4 + device
    hit = (wanted == col) & ((row // (2 * CHANS)) % 2 == half)
    return jnp.where(hit, 1.0, 0.0).astype(jnp.bfloat16)


def _project_kernel(*refs):
    sources, final_source, outs, held = refs[:7], refs[7], refs[8:12], refs[12:19]
    left_ref, right_ref, final_ref, order_ref = outs
    sems = refs[19]
    pairs = [(sources[0].at[s], held[0].at[s]) for s in range(2)]
    pairs += list(zip(sources[1:], held[1:])) + [(final_source, final_ref)]
    copies = [pltpu.make_async_copy(a, b, sems.at[i]) for i, (a, b) in enumerate(pairs)]
    for copy in copies:
        copy.start()
    me = lax.axis_index("row")
    for h in range(2):
        order_ref[h] = _order(me, h)
    for copy in copies[:1] + copies[2:8]:
        copy.wait()
    x_ref, gain_ref, bias_ref, w1_ref, b1_ref, w2_ref, b2_ref = held
    half = left_ref.shape[0]
    n = right_ref.shape[0]
    feats = x_ref.shape[2]
    split = []
    for s in range(2):
        if s:
            copies[1].wait()
        x = x_ref[s].astype(jnp.float32)
        center = jnp.mean(x, axis=-1, keepdims=True)
        off = x - center
        spread = jnp.mean(off * off, axis=-1, keepdims=True)
        normed = off * lax.rsqrt(spread + 1e-05) * gain_ref[...] + bias_ref[...]
        split.append(normed.reshape(n, 2, 8, feats))
    parts = [split[s][:, jh].reshape(n * 8, feats).astype(jnp.bfloat16) for jh in range(2) for s in range(2)]
    weights = jnp.concatenate([_stacked(w1_ref[...], 4), _stacked(w2_ref[...], 4)], axis=0)
    shifts = jnp.concatenate([b1_ref[...]] * 4 + [b2_ref[...]] * 4, axis=1)
    both = lax.dot_general(jnp.concatenate(parts, axis=1), weights, NT, preferred_element_type=jnp.float32) + shifts
    left_ref[...] = both[:half, :LANES].astype(jnp.bfloat16)
    right_ref[...] = both[:, LANES:].reshape(n, 8, LANES).astype(jnp.bfloat16)
    copies[8].wait()


def _line_kernel(*refs):
    pieces, order_ref, out_ref = refs[:-2], refs[-2], refs[-1]
    half = pieces[0].shape[0]
    wide = order_ref.shape[2]
    for q in range(len(pieces) // 4):
        lhs = jnp.concatenate([pieces[q * 4 + k][...] for k in (0, 1, 3, 2)], axis=1)
        for h in range(2):
            moved = jnp.dot(lhs, order_ref[h], preferred_element_type=jnp.float32)
            out_ref[pl.ds(h * half, half), pl.ds(q * wide, wide)] = moved.astype(jnp.bfloat16)


def _fold_kernel(right_ref, final_ref, out_ref, block_ref, pairs_ref):
    devices = right_ref.shape[0]
    groups = devices // 4
    block_ref[...] = right_ref[...].astype(jnp.float32).reshape(devices * 8, LANES)
    for jr in range(8):
        for g in range(groups):
            four = block_ref[pl.ds(g * 8 + jr, 4, stride=groups * 8), :]
            for s in range(2):
                pairs_ref[pl.ds((jr * groups + g) * 8 + s * 4, 4), :] = four
    block = pairs_ref[...]
    lane = lax.broadcasted_iota(jnp.int32, block.shape, 1) // CHANS
    s = lax.broadcasted_iota(jnp.int32, block.shape, 0) // 4 % 2
    lhs = [jnp.where(lane == jh * 2 + s, block, 0.0).astype(jnp.bfloat16) for jh in range(2)]
    lhs = jnp.concatenate(lhs, axis=0)

    for pair in range(CHANS // 2):
        rhs = []
        for k in range(2):
            at = pair * 2 * CHANS + k * CHANS
            rhs.append(jnp.concatenate([final_ref[pl.ds(at, CHANS), :]] * 4, axis=0))
        res = jnp.dot(lhs, jnp.concatenate(rhs, axis=1), preferred_element_type=jnp.float32)
        for j in range(16):
            for g in range(groups):
                r = (j * groups + g) * 8
                tile = jnp.concatenate([res[r : r + 8, :LANES], res[r : r + 8, LANES:]], axis=0)
                out_ref[g, 0, pl.ds(pair * 16, 16), pl.ds(j * LANES, LANES)] = tile.astype(jnp.bfloat16)


def _band_kernel(masks, begins, scale, last, held, *refs):
    refs = list(refs)
    take = lambda k: [refs.pop(0) for _ in range(k)]
    if masks == (1, 3, 5):
        (block,) = take(1)
        lines = [[block.at[k]] for k in range(3)]
    else:
        lines = [take(2 if mask in (6, 7) else 1) for mask in masks]
    (t_ref,) = take(1)
    (sum_ref,) = (None,) if begins else take(1)
    shift_ref = None if scale is None or last else take(1)[0]
    pair_ref = take(1)[0] if last else None
    (out_ref,) = take(1)
    me = lax.axis_index("row")
    wide = t_ref.shape[2]
    chunks = [((me % 8) ^ mask, q ^ (me // 32)) for mask in masks for q in range(t_ref.shape[1])]

    tile = 256 if last or not held else 512
    band = sum(part.shape[0] for part in lines[0])

    def column(begin):
        at = pl.ds(begin, tile)
        if held:
            rhs = jnp.concatenate([t_ref[g, q, :, at] for g, q in chunks], axis=0)
        else:
            for i, (g, q) in enumerate(chunks):
                pltpu.sync_copy(t_ref.at[g, q, :, at], refs[0].at[pl.ds(i * wide, wide)])
            rhs = refs[0][...]
        lhs = jnp.concatenate([jnp.concatenate([part[...] for part in line], axis=0) for line in lines], axis=1)
        res = jnp.dot(lhs, rhs, preferred_element_type=jnp.float32)
        if last:
            return res * scale + sum_ref[:, at]
        if sum_ref is not None:
            res = res + sum_ref[:, at]
        if shift_ref is not None:
            res = res * scale + jnp.concatenate([shift_ref[...]] * (tile // LANES), axis=1)
        return res

    if not last:
        for begin in range(0, t_ref.shape[3], tile):
            out_ref[:, pl.ds(begin, tile)] = column(begin)
        return

    acc_ref, done_ref, sems, fetched_sem = take(4)
    cols = pair_ref.shape[1]
    pitch = cols + 1
    fetch = pltpu.make_async_copy(pair_ref, done_ref, fetched_sem)
    fetch.start()
    for begin in range(0, t_ref.shape[3], tile):
        res = column(begin)
        for k in range(tile // LANES):
            j = begin // LANES + k
            acc_ref[pl.ds(j, band, stride=pitch), :] = res[:, k * LANES : (k + 1) * LANES]
    fetch.wait()

    chunk = 32

    def finish(r, _):
        for k in range(chunk):
            i = r * chunk + k
            row = k // 8 % 2 * (band // 2) + (r * (chunk // 16) + k // 16) * 8 + k % 8
            total = acc_ref[pl.ds(row * pitch, cols), :]
            done_ref[i] = (done_ref[i].astype(jnp.float32) + total).astype(jnp.bfloat16)
        at = pl.ds(pl.multiple_of(r * chunk, chunk), chunk)
        pltpu.make_async_copy(done_ref.at[at], out_ref.at[at], sems.at[r]).start()
        return 0

    lax.fori_loop(0, band // chunk, finish, 0)

    def drain(r, _):
        at = pl.ds(pl.multiple_of(r * chunk, chunk), chunk)
        pltpu.make_async_copy(done_ref.at[at], out_ref.at[at], sems.at[r]).wait()
        return 0

    lax.fori_loop(0, band // chunk, drain, 0)


def _xor(x, mask, n):
    return lax.ppermute(x, "row", [(i, i ^ mask) for i in range(n)])


def shards(n, alignment, pair, gain, bias, w1, b1, w2, b2, final, shift):
    seqs, residues, feats = alignment.shape
    band, cols, zdim = pair.shape
    half = band // 2
    count = float(seqs * n)
    small = n <= 32
    params = pltpu.CompilerParams(vmem_limit_bytes=(24 if small else 48) * 1024 * 1024)
    anywhere = pl.BlockSpec(memory_space=pl.ANY)
    vmem = pl.BlockSpec(memory_space=pltpu.VMEM)

    sources = [
        alignment, gain.reshape(1, -1), bias.reshape(1, -1), w1.T, b1.reshape(1, -1), w2.T, b2.reshape(1, -1)
    ]
    sources = [pltpu.with_memory_space_constraint(a, pltpu.HBM) for a in sources]
    left, right, final, order = pl.pallas_call(
        _project_kernel,
        in_specs=[anywhere] * 8,
        out_specs=(vmem,) * 4,
        out_shape=(
            jax.ShapeDtypeStruct((half, LANES), jnp.bfloat16),
            jax.ShapeDtypeStruct((n, 8, LANES), jnp.bfloat16),
            jax.ShapeDtypeStruct(final.shape, final.dtype),
            jax.ShapeDtypeStruct((2, 4 * LANES, 8 * CHANS), jnp.bfloat16),
        ),
        scratch_shapes=[pltpu.VMEM(a.shape, a.dtype) for a in sources] + [pltpu.SemaphoreType.DMA((9,))],
        compiler_params=params,
        cost_estimate=pl.CostEstimate(
            flops=4 * seqs * residues * feats * CHANS, bytes_accessed=2 * seqs * residues * feats, transcendentals=0
        ),
    )(*sources, pltpu.with_memory_space_constraint(final, pltpu.HBM))

    right = lax.all_to_all(right, "row", split_axis=0, concat_axis=0, tiled=True)

    part = 32
    parts = n // part
    pieces = [left] + [_xor(left, m, n) for m in range(8, n, 8)]
    pieces = [pieces[k ^ (k // 2 % 2)] for k in range(len(pieces))]
    line = pl.pallas_call(
        _line_kernel,
        in_specs=[vmem] * (len(pieces) + 1),
        out_specs=vmem,
        out_shape=jax.ShapeDtypeStruct((band, parts * 8 * CHANS), jnp.bfloat16),
        compiler_params=params,
        cost_estimate=pl.CostEstimate(flops=2**27, bytes_accessed=2**20, transcendentals=0),
    )(*pieces, order)
    x, y = _xor(line, 2, n), _xor(line, 4, n)

    fold_cost = pl.CostEstimate(
        flops=2 * n * 32 * 256 * CHANS * zdim, bytes_accessed=4 * n * CHANS * cols * zdim, transcendentals=0
    )
    fold_out = jax.ShapeDtypeStruct((8, parts, 8 * CHANS, cols * zdim), jnp.bfloat16)
    if small:
        specs = dict(in_specs=[vmem, vmem], out_specs=vmem)
    else:
        specs = dict(
            grid=(parts,),
            in_specs=[
                pl.BlockSpec((part, 8, LANES), lambda i: (i, 0, 0)),
                pl.BlockSpec(final.shape, lambda i: (0, 0)),
            ],
            out_specs=pl.BlockSpec((8, 1, 8 * CHANS, cols * zdim), lambda i: (0, i, 0, 0)),
        )
    folded = pl.pallas_call(
        _fold_kernel,
        out_shape=fold_out,
        scratch_shapes=[pltpu.VMEM((part * 8, LANES), jnp.float32), pltpu.VMEM((part * 16, LANES), jnp.float32)],
        compiler_params=params,
        cost_estimate=fold_cost,
        **specs,
    )(right, final)

    def add(lines, masks, total, last, scaled=False):
        depth = len(masks) * parts * 8 * CHANS
        scratch = []
        operands = [*lines, folded] + ([] if total is None else [total])
        if scaled and not last:
            operands.append(shift.reshape(1, -1))
        if last:
            operands.append(pltpu.with_memory_space_constraint(pair, pltpu.HBM))
            scratch += [
                pltpu.VMEM((band * (cols + 1), zdim), jnp.float32),
                pltpu.VMEM(pair.shape, jnp.bfloat16),
                pltpu.SemaphoreType.DMA((band // 32,)),
                pltpu.SemaphoreType.DMA(()),
            ]
        if not small:
            scratch.append(pltpu.VMEM((depth, 256), jnp.bfloat16))
        in_specs = [vmem] * (len(operands) - last) + [anywhere] * last
        if not small:
            in_specs[len(lines)] = anywhere
        return pl.pallas_call(
            functools.partial(_band_kernel, masks, total is None, 1.0 / count if scaled else None, last, small),
            in_specs=in_specs,
            out_specs=anywhere if last else vmem,
            out_shape=jax.ShapeDtypeStruct(pair.shape, jnp.bfloat16)
            if last
            else jax.ShapeDtypeStruct((band, cols * zdim), jnp.float32),
            scratch_shapes=scratch,
            compiler_params=params,
            cost_estimate=pl.CostEstimate(
                flops=band * cols * zdim, bytes_accessed=band * cols, transcendentals=0
            ),
        )(*operands)

    x, y, folded = lax.optimization_barrier((x, y, folded))
    cut = band * 9 // 16
    upper, lower = _xor(x[:cut], 4, n), _xor(y[cut:], 2, n)
    across = _xor(jnp.stack([line, x, y]), 1, n)
    total = add([line, x, y], (0, 2, 4), None, False)
    total = add([across], (1, 3, 5), total, False)
    upper, total = lax.optimization_barrier((upper, total))
    last = [_xor(upper, 1, n)]
    lower, total = lax.optimization_barrier((lower, total))
    last.append(_xor(lower, 1, n))
    total = add([upper, lower], (6,), total, False, True)
    return add(last, (7,), total, True, True)


def solution(mesh):
    placed = (P(("group", "row"), None, None), P("group", "row", None)) + (P(),) * 8
    return jax.shard_map(
        functools.partial(shards, mesh.shape["row"]),
        mesh=mesh,
        in_specs=placed,
        out_specs=P("group", "row", None),
        check_vma=False,
    )
```

```python
import functools

import jax
import jax.numpy as jnp
from jax import lax
from jax.experimental import pallas as pl
from jax.experimental.pallas import tpu as pltpu
from jax.sharding import PartitionSpec as P

LANES = 128
CHANS = 32
NT = (((1,), (1,)), ((), ()))


def _stacked(weights, copies):
    c, q = weights.shape
    rows = []
    for k in range(copies):
        left = [jnp.zeros((c, k * q), weights.dtype)] if k else []
        right = [jnp.zeros((c, (copies - 1 - k) * q), weights.dtype)] if k < copies - 1 else []
        rows.append(jnp.concatenate(left + [weights] + right, axis=1))
    return jnp.concatenate(rows, axis=0)


def _order(me, half):
    row = lax.broadcasted_iota(jnp.int32, (4 * LANES, 8 * CHANS), 0)
    col = lax.broadcasted_iota(jnp.int32, (4 * LANES, 8 * CHANS), 1)
    device = (row // LANES) ^ (me // 8 % 4)
    wanted = (row % CHANS) * 8 + ((row // CHANS) % 2) * 4 + device
    hit = (wanted == col) & ((row // (2 * CHANS)) % 2 == half)
    return jnp.where(hit, 1.0, 0.0).astype(jnp.bfloat16)


def _project_kernel(*refs):
    sources, final_source, outs, held = refs[:7], refs[7], refs[8:12], refs[12:19]
    left_ref, right_ref, final_ref, order_ref = outs
    sems = refs[19]
    pairs = [(sources[0].at[s], held[0].at[s]) for s in range(2)]
    pairs += list(zip(sources[1:], held[1:])) + [(final_source, final_ref)]
    copies = [pltpu.make_async_copy(a, b, sems.at[i]) for i, (a, b) in enumerate(pairs)]
    for copy in copies:
        copy.start()
    me = lax.axis_index("row")
    for h in range(2):
        order_ref[h] = _order(me, h)
    for copy in copies[:1] + copies[2:8]:
        copy.wait()
    x_ref, gain_ref, bias_ref, w1_ref, b1_ref, w2_ref, b2_ref = held
    half = left_ref.shape[0]
    n = right_ref.shape[0]
    feats = x_ref.shape[2]
    split = []
    for s in range(2):
        if s:
            copies[1].wait()
        x = x_ref[s].astype(jnp.float32)
        center = jnp.mean(x, axis=-1, keepdims=True)
        off = x - center
        spread = jnp.mean(off * off, axis=-1, keepdims=True)
        normed = off * lax.rsqrt(spread + 1e-05) * gain_ref[...] + bias_ref[...]
        split.append(normed.reshape(n, 2, 8, feats))
    parts = [split[s][:, jh].reshape(n * 8, feats).astype(jnp.bfloat16) for jh in range(2) for s in range(2)]
    weights = jnp.concatenate([_stacked(w1_ref[...], 4), _stacked(w2_ref[...], 4)], axis=0)
    shifts = jnp.concatenate([b1_ref[...]] * 4 + [b2_ref[...]] * 4, axis=1)
    both = lax.dot_general(jnp.concatenate(parts, axis=1), weights, NT, preferred_element_type=jnp.float32) + shifts
    left_ref[...] = both[:half, :LANES].astype(jnp.bfloat16)
    right_ref[...] = both[:, LANES:].reshape(n, 8, LANES).astype(jnp.bfloat16)
    copies[8].wait()


def _line_kernel(*refs):
    pieces, order_ref, out_ref = refs[:-2], refs[-2], refs[-1]
    half = pieces[0].shape[0]
    wide = order_ref.shape[2]
    for q in range(len(pieces) // 4):
        lhs = jnp.concatenate([pieces[q * 4 + k][...] for k in (0, 1, 3, 2)], axis=1)
        for h in range(2):
            moved = jnp.dot(lhs, order_ref[h], preferred_element_type=jnp.float32)
            out_ref[pl.ds(h * half, half), pl.ds(q * wide, wide)] = moved.astype(jnp.bfloat16)


def _fold_kernel(right_ref, final_ref, out_ref, block_ref, pairs_ref):
    devices = right_ref.shape[0]
    groups = devices // 4
    block_ref[...] = right_ref[...].astype(jnp.float32).reshape(devices * 8, LANES)
    for jr in range(8):
        for g in range(groups):
            four = block_ref[pl.ds(g * 8 + jr, 4, stride=groups * 8), :]
            for s in range(2):
                pairs_ref[pl.ds((jr * groups + g) * 8 + s * 4, 4), :] = four
    block = pairs_ref[...]
    lane = lax.broadcasted_iota(jnp.int32, block.shape, 1) // CHANS
    s = lax.broadcasted_iota(jnp.int32, block.shape, 0) // 4 % 2
    lhs = [jnp.where(lane == jh * 2 + s, block, 0.0).astype(jnp.bfloat16) for jh in range(2)]
    lhs = jnp.concatenate(lhs, axis=0)

    for pair in range(CHANS // 2):
        rhs = []
        for k in range(2):
            at = pair * 2 * CHANS + k * CHANS
            rhs.append(jnp.concatenate([final_ref[pl.ds(at, CHANS), :]] * 4, axis=0))
        res = jnp.dot(lhs, jnp.concatenate(rhs, axis=1), preferred_element_type=jnp.float32)
        for j in range(16):
            for g in range(groups):
                r = (j * groups + g) * 8
                tile = jnp.concatenate([res[r : r + 8, :LANES], res[r : r + 8, LANES:]], axis=0)
                out_ref[g, 0, pl.ds(pair * 16, 16), pl.ds(j * LANES, LANES)] = tile.astype(jnp.bfloat16)


def _band_kernel(masks, begins, scale, last, held, *refs):
    refs = list(refs)
    take = lambda k: [refs.pop(0) for _ in range(k)]
    if masks == (1, 3, 5):
        (block,) = take(1)
        lines = [[block.at[k]] for k in range(3)]
    else:
        lines = [take(2 if mask in (6, 7) else 1) for mask in masks]
    (t_ref,) = take(1)
    (sum_ref,) = (None,) if begins else take(1)
    shift_ref = None if scale is None or last else take(1)[0]
    carries = masks == (1, 3, 5)
    pair_ref = take(1)[0] if last or carries else None
    (out_ref,) = take(1)
    if carries:
        held_pair, pair_sem = take(2)
        fetch = pltpu.make_async_copy(pair_ref, held_pair, pair_sem)
        fetch.start()
    me = lax.axis_index("row")
    wide = t_ref.shape[2]
    chunks = [((me % 8) ^ mask, q ^ (me // 32)) for mask in masks for q in range(t_ref.shape[1])]

    tile = 256 if last or not held else 512
    band = sum(part.shape[0] for part in lines[0])

    def column(begin):
        at = pl.ds(begin, tile)
        if held:
            rhs = jnp.concatenate([t_ref[g, q, :, at] for g, q in chunks], axis=0)
        else:
            for i, (g, q) in enumerate(chunks):
                pltpu.sync_copy(t_ref.at[g, q, :, at], refs[0].at[pl.ds(i * wide, wide)])
            rhs = refs[0][...]
        lhs = jnp.concatenate([jnp.concatenate([part[...] for part in line], axis=0) for line in lines], axis=1)
        res = jnp.dot(lhs, rhs, preferred_element_type=jnp.float32)
        if last:
            return res * scale + sum_ref[:, at]
        if sum_ref is not None:
            res = res + sum_ref[:, at]
        if shift_ref is not None:
            res = res * scale + jnp.concatenate([shift_ref[...]] * (tile // LANES), axis=1)
        return res

    if not last:
        for begin in range(0, t_ref.shape[3], tile):
            out_ref[:, pl.ds(begin, tile)] = column(begin)
        if carries:
            fetch.wait()
        return

    acc_ref, done_ref, sems = take(3)
    cols = pair_ref.shape[1]
    pitch = cols + 1
    for begin in range(0, t_ref.shape[3], tile):
        res = column(begin)
        for k in range(tile // LANES):
            j = begin // LANES + k
            acc_ref[pl.ds(j, band, stride=pitch), :] = res[:, k * LANES : (k + 1) * LANES]

    chunk = 32

    def finish(r, _):
        for k in range(chunk):
            i = r * chunk + k
            row = k // 8 % 2 * (band // 2) + (r * (chunk // 16) + k // 16) * 8 + k % 8
            total = acc_ref[pl.ds(row * pitch, cols), :]
            done_ref[i] = (pair_ref[i].astype(jnp.float32) + total).astype(jnp.bfloat16)
        at = pl.ds(pl.multiple_of(r * chunk, chunk), chunk)
        pltpu.make_async_copy(done_ref.at[at], out_ref.at[at], sems.at[r]).start()
        return 0

    lax.fori_loop(0, band // chunk, finish, 0)

    def drain(r, _):
        at = pl.ds(pl.multiple_of(r * chunk, chunk), chunk)
        pltpu.make_async_copy(done_ref.at[at], out_ref.at[at], sems.at[r]).wait()
        return 0

    lax.fori_loop(0, band // chunk, drain, 0)


def _xor(x, mask, n):
    return lax.ppermute(x, "row", [(i, i ^ mask) for i in range(n)])


def shards(n, alignment, pair, gain, bias, w1, b1, w2, b2, final, shift):
    seqs, residues, feats = alignment.shape
    band, cols, zdim = pair.shape
    half = band // 2
    count = float(seqs * n)
    small = n <= 32
    params = pltpu.CompilerParams(vmem_limit_bytes=(24 if small else 48) * 1024 * 1024)
    anywhere = pl.BlockSpec(memory_space=pl.ANY)
    vmem = pl.BlockSpec(memory_space=pltpu.VMEM)

    sources = [
        alignment, gain.reshape(1, -1), bias.reshape(1, -1), w1.T, b1.reshape(1, -1), w2.T, b2.reshape(1, -1)
    ]
    sources = [pltpu.with_memory_space_constraint(a, pltpu.HBM) for a in sources]
    left, right, final, order = pl.pallas_call(
        _project_kernel,
        in_specs=[anywhere] * 8,
        out_specs=(vmem,) * 4,
        out_shape=(
            jax.ShapeDtypeStruct((half, LANES), jnp.bfloat16),
            jax.ShapeDtypeStruct((n, 8, LANES), jnp.bfloat16),
            jax.ShapeDtypeStruct(final.shape, final.dtype),
            jax.ShapeDtypeStruct((2, 4 * LANES, 8 * CHANS), jnp.bfloat16),
        ),
        scratch_shapes=[pltpu.VMEM(a.shape, a.dtype) for a in sources] + [pltpu.SemaphoreType.DMA((9,))],
        compiler_params=params,
        cost_estimate=pl.CostEstimate(
            flops=4 * seqs * residues * feats * CHANS, bytes_accessed=2 * seqs * residues * feats, transcendentals=0
        ),
    )(*sources, pltpu.with_memory_space_constraint(final, pltpu.HBM))

    right = lax.all_to_all(right, "row", split_axis=0, concat_axis=0, tiled=True)

    part = 32
    parts = n // part
    pieces = [left] + [_xor(left, m, n) for m in range(8, n, 8)]
    pieces = [pieces[k ^ (k // 2 % 2)] for k in range(len(pieces))]
    line = pl.pallas_call(
        _line_kernel,
        in_specs=[vmem] * (len(pieces) + 1),
        out_specs=vmem,
        out_shape=jax.ShapeDtypeStruct((band, parts * 8 * CHANS), jnp.bfloat16),
        compiler_params=params,
        cost_estimate=pl.CostEstimate(flops=2**27, bytes_accessed=2**20, transcendentals=0),
    )(*pieces, order)
    x, y = _xor(line, 2, n), _xor(line, 4, n)

    fold_cost = pl.CostEstimate(
        flops=2 * n * 32 * 256 * CHANS * zdim, bytes_accessed=4 * n * CHANS * cols * zdim, transcendentals=0
    )
    fold_out = jax.ShapeDtypeStruct((8, parts, 8 * CHANS, cols * zdim), jnp.bfloat16)
    if small:
        specs = dict(in_specs=[vmem, vmem], out_specs=vmem)
    else:
        specs = dict(
            grid=(parts,),
            in_specs=[
                pl.BlockSpec((part, 8, LANES), lambda i: (i, 0, 0)),
                pl.BlockSpec(final.shape, lambda i: (0, 0)),
            ],
            out_specs=pl.BlockSpec((8, 1, 8 * CHANS, cols * zdim), lambda i: (0, i, 0, 0)),
        )
    folded = pl.pallas_call(
        _fold_kernel,
        out_shape=fold_out,
        scratch_shapes=[pltpu.VMEM((part * 8, LANES), jnp.float32), pltpu.VMEM((part * 16, LANES), jnp.float32)],
        compiler_params=params,
        cost_estimate=fold_cost,
        **specs,
    )(right, final)

    pinned = pltpu.with_memory_space_constraint(pair, pltpu.HBM)

    def add(lines, masks, total, last=False, scaled=False, carried=None):
        depth = len(masks) * parts * 8 * CHANS
        carries = masks == (1, 3, 5)
        operands = [*lines, folded] + ([] if total is None else [total])
        in_specs = [vmem] * len(operands)
        if not small:
            in_specs[len(lines)] = anywhere
        if scaled and not last:
            operands.append(shift.reshape(1, -1))
            in_specs.append(vmem)
        out_shape, out_specs, scratch = jax.ShapeDtypeStruct((band, cols * zdim), jnp.float32), vmem, []
        if carries:
            operands.append(pinned)
            in_specs.append(anywhere)
            out_shape, out_specs = (out_shape, jax.ShapeDtypeStruct(pair.shape, pair.dtype)), (vmem, vmem)
            scratch = [pltpu.SemaphoreType.DMA(())]
        if last:
            operands.append(carried)
            in_specs.append(vmem)
            out_shape, out_specs = jax.ShapeDtypeStruct(pair.shape, jnp.bfloat16), anywhere
            scratch = [
                pltpu.VMEM((band * (cols + 1), zdim), jnp.float32),
                pltpu.VMEM(pair.shape, jnp.bfloat16),
                pltpu.SemaphoreType.DMA((band // 32,)),
            ]
        if not small:
            scratch.append(pltpu.VMEM((depth, 256), jnp.bfloat16))
        return pl.pallas_call(
            functools.partial(_band_kernel, masks, total is None, 1.0 / count if scaled else None, last, small),
            in_specs=in_specs,
            out_specs=out_specs,
            out_shape=out_shape,
            scratch_shapes=scratch,
            compiler_params=params,
            cost_estimate=pl.CostEstimate(
                flops=band * cols * zdim, bytes_accessed=band * cols, transcendentals=0
            ),
        )(*operands)

    x, y, folded = lax.optimization_barrier((x, y, folded))
    cut = band * 9 // 16
    upper, lower = _xor(x[:cut], 4, n), _xor(y[cut:], 2, n)
    across = _xor(jnp.stack([line, x, y]), 1, n)
    total = add([line, x, y], (0, 2, 4), None)
    total, carried = add([across], (1, 3, 5), total)
    upper, total = lax.optimization_barrier((upper, total))
    last = [_xor(upper, 1, n)]
    lower, total = lax.optimization_barrier((lower, total))
    last.append(_xor(lower, 1, n))
    total = add([upper, lower], (6,), total, scaled=True)
    return add(last, (7,), total, last=True, scaled=True, carried=carried)


def solution(mesh):
    placed = (P(("group", "row"), None, None), P("group", "row", None)) + (P(),) * 8
    return jax.shard_map(
        functools.partial(shards, mesh.shape["row"]),
        mesh=mesh,
        in_specs=placed,
        out_specs=P("group", "row", None),
        check_vma=False,
    )
```

```python
import functools

import jax
import jax.numpy as jnp
from jax import lax
from jax.experimental import pallas as pl
from jax.experimental.pallas import tpu as pltpu
from jax.sharding import PartitionSpec as P

LANES = 128
CHANS = 32
NT = (((1,), (1,)), ((), ()))


def _stacked(weights, copies):
    c, q = weights.shape
    rows = []
    for k in range(copies):
        left = [jnp.zeros((c, k * q), weights.dtype)] if k else []
        right = [jnp.zeros((c, (copies - 1 - k) * q), weights.dtype)] if k < copies - 1 else []
        rows.append(jnp.concatenate(left + [weights] + right, axis=1))
    return jnp.concatenate(rows, axis=0)


def _order(me, half):
    row = lax.broadcasted_iota(jnp.int32, (4 * LANES, 8 * CHANS), 0)
    col = lax.broadcasted_iota(jnp.int32, (4 * LANES, 8 * CHANS), 1)
    device = (row // LANES) ^ (me // 8 % 4)
    wanted = (row % CHANS) * 8 + ((row // CHANS) % 2) * 4 + device
    hit = (wanted == col) & ((row // (2 * CHANS)) % 2 == half)
    return jnp.where(hit, 1.0, 0.0).astype(jnp.bfloat16)


def _project_kernel(*refs):
    sources, final_source, outs, held = refs[:7], refs[7], refs[8:12], refs[12:19]
    left_ref, right_ref, final_ref, order_ref = outs
    sems = refs[19]
    pairs = [(sources[0].at[s], held[0].at[s]) for s in range(2)]
    pairs += list(zip(sources[1:], held[1:])) + [(final_source, final_ref)]
    copies = [pltpu.make_async_copy(a, b, sems.at[i]) for i, (a, b) in enumerate(pairs)]
    for copy in copies:
        copy.start()
    me = lax.axis_index("row")
    for h in range(2):
        order_ref[h] = _order(me, h)
    for copy in copies[:1] + copies[2:8]:
        copy.wait()
    x_ref, gain_ref, bias_ref, w1_ref, b1_ref, w2_ref, b2_ref = held
    half = left_ref.shape[0]
    n = right_ref.shape[0]
    feats = x_ref.shape[2]
    share = jnp.full((feats, LANES), 1.0 / feats, jnp.bfloat16)
    widen = lambda mean: jnp.concatenate([mean] * (feats // LANES), axis=1)
    split = []
    for s in range(2):
        if s:
            copies[1].wait()
        x = x_ref[s]
        off = x.astype(jnp.float32) - widen(jnp.dot(x, share, preferred_element_type=jnp.float32))
        square = off * off
        high = square.astype(jnp.bfloat16)
        low = (square - high.astype(jnp.float32)).astype(jnp.bfloat16)
        spread = jnp.dot(
            jnp.concatenate([high, low], axis=1),
            jnp.concatenate([share, share], axis=0),
            preferred_element_type=jnp.float32,
        )
        normed = off * widen(lax.rsqrt(spread + 1e-05)) * gain_ref[...] + bias_ref[...]
        split.append(normed.reshape(n, 2, 8, feats))
    parts = [split[s][:, jh].reshape(n * 8, feats).astype(jnp.bfloat16) for jh in range(2) for s in range(2)]
    weights = jnp.concatenate([_stacked(w1_ref[...], 4), _stacked(w2_ref[...], 4)], axis=0)
    shifts = jnp.concatenate([b1_ref[...]] * 4 + [b2_ref[...]] * 4, axis=1)
    both = lax.dot_general(jnp.concatenate(parts, axis=1), weights, NT, preferred_element_type=jnp.float32) + shifts
    left_ref[...] = both[:half, :LANES].astype(jnp.bfloat16)
    right_ref[...] = both[:, LANES:].reshape(n, 8, LANES).astype(jnp.bfloat16)
    copies[8].wait()


def _line_kernel(*refs):
    pieces, order_ref, out_ref = refs[:-2], refs[-2], refs[-1]
    half = pieces[0].shape[0]
    wide = order_ref.shape[2]
    for q in range(len(pieces) // 4):
        lhs = jnp.concatenate([pieces[q * 4 + k][...] for k in (0, 1, 3, 2)], axis=1)
        for h in range(2):
            moved = jnp.dot(lhs, order_ref[h], preferred_element_type=jnp.float32)
            out_ref[pl.ds(h * half, half), pl.ds(q * wide, wide)] = moved.astype(jnp.bfloat16)


def _fold_kernel(right_ref, final_ref, out_ref, block_ref, pairs_ref):
    devices = right_ref.shape[0]
    groups = devices // 4
    block_ref[...] = right_ref[...].astype(jnp.float32).reshape(devices * 8, LANES)
    for jr in range(8):
        for g in range(groups):
            four = block_ref[pl.ds(g * 8 + jr, 4, stride=groups * 8), :]
            for s in range(2):
                pairs_ref[pl.ds((jr * groups + g) * 8 + s * 4, 4), :] = four
    block = pairs_ref[...]
    lane = lax.broadcasted_iota(jnp.int32, block.shape, 1) // CHANS
    s = lax.broadcasted_iota(jnp.int32, block.shape, 0) // 4 % 2
    lhs = [jnp.where(lane == jh * 2 + s, block, 0.0).astype(jnp.bfloat16) for jh in range(2)]
    lhs = jnp.concatenate(lhs, axis=0)

    for pair in range(CHANS // 2):
        rhs = []
        for k in range(2):
            at = pair * 2 * CHANS + k * CHANS
            rhs.append(jnp.concatenate([final_ref[pl.ds(at, CHANS), :]] * 4, axis=0))
        res = jnp.dot(lhs, jnp.concatenate(rhs, axis=1), preferred_element_type=jnp.float32)
        for j in range(16):
            for g in range(groups):
                r = (j * groups + g) * 8
                tile = jnp.concatenate([res[r : r + 8, :LANES], res[r : r + 8, LANES:]], axis=0)
                out_ref[g, 0, pl.ds(pair * 16, 16), pl.ds(j * LANES, LANES)] = tile.astype(jnp.bfloat16)


def _band_kernel(masks, begins, scale, last, held, *refs):
    refs = list(refs)
    take = lambda k: [refs.pop(0) for _ in range(k)]
    if masks == (1, 3, 5):
        (block,) = take(1)
        lines = [[block.at[k]] for k in range(3)]
    else:
        lines = [take(2 if mask in (6, 7) else 1) for mask in masks]
    (t_ref,) = take(1)
    (sum_ref,) = (None,) if begins else take(1)
    shift_ref = None if scale is None or last else take(1)[0]
    carries = masks == (1, 3, 5)
    pair_ref = take(1)[0] if last or carries else None
    (out_ref,) = take(1)
    if carries:
        held_pair, pair_sem = take(2)
        fetch = pltpu.make_async_copy(pair_ref, held_pair, pair_sem)
        fetch.start()
    me = lax.axis_index("row")
    wide = t_ref.shape[2]
    chunks = [((me % 8) ^ mask, q ^ (me // 32)) for mask in masks for q in range(t_ref.shape[1])]

    tile = 256 if last or not held else 512
    band = sum(part.shape[0] for part in lines[0])

    def column(begin):
        at = pl.ds(begin, tile)
        if held:
            rhs = jnp.concatenate([t_ref[g, q, :, at] for g, q in chunks], axis=0)
        else:
            for i, (g, q) in enumerate(chunks):
                pltpu.sync_copy(t_ref.at[g, q, :, at], refs[0].at[pl.ds(i * wide, wide)])
            rhs = refs[0][...]
        lhs = jnp.concatenate([jnp.concatenate([part[...] for part in line], axis=0) for line in lines], axis=1)
        res = jnp.dot(lhs, rhs, preferred_element_type=jnp.float32)
        if last:
            return res * scale + sum_ref[:, at]
        if sum_ref is not None:
            res = res + sum_ref[:, at]
        if shift_ref is not None:
            res = res * scale + jnp.concatenate([shift_ref[...]] * (tile // LANES), axis=1)
        return res

    if not last:
        for begin in range(0, t_ref.shape[3], tile):
            out_ref[:, pl.ds(begin, tile)] = column(begin)
        if carries:
            fetch.wait()
        return

    acc_ref, done_ref, sems = take(3)
    cols = pair_ref.shape[1]
    gap = 3
    pitch = gap * cols + 1
    for begin in range(0, t_ref.shape[3], tile):
        res = column(begin)
        for k in range(tile // LANES):
            j = begin // LANES + k
            acc_ref[pl.ds(gap * j, band, stride=pitch), :] = res[:, k * LANES : (k + 1) * LANES]

    chunk = 32

    def finish(r, _):
        for k in range(chunk):
            i = r * chunk + k
            row = k // 8 % 2 * (band // 2) + (r * (chunk // 16) + k // 16) * 8 + k % 8
            total = acc_ref[pl.ds(row * pitch, cols, stride=gap), :]
            done_ref[i] = (pair_ref[i].astype(jnp.float32) + total).astype(jnp.bfloat16)
        at = pl.ds(pl.multiple_of(r * chunk, chunk), chunk)
        pltpu.make_async_copy(done_ref.at[at], out_ref.at[at], sems.at[r]).start()
        return 0

    lax.fori_loop(0, band // chunk, finish, 0)

    def drain(r, _):
        at = pl.ds(pl.multiple_of(r * chunk, chunk), chunk)
        pltpu.make_async_copy(done_ref.at[at], out_ref.at[at], sems.at[r]).wait()
        return 0

    lax.fori_loop(0, band // chunk, drain, 0)


def _xor(x, mask, n):
    return lax.ppermute(x, "row", [(i, i ^ mask) for i in range(n)])


def shards(n, alignment, pair, gain, bias, w1, b1, w2, b2, final, shift):
    seqs, residues, feats = alignment.shape
    band, cols, zdim = pair.shape
    half = band // 2
    count = float(seqs * n)
    small = n <= 32
    params = pltpu.CompilerParams(vmem_limit_bytes=(24 if small else 48) * 1024 * 1024)
    anywhere = pl.BlockSpec(memory_space=pl.ANY)
    vmem = pl.BlockSpec(memory_space=pltpu.VMEM)

    sources = [
        alignment, gain.reshape(1, -1), bias.reshape(1, -1), w1.T, b1.reshape(1, -1), w2.T, b2.reshape(1, -1)
    ]
    sources = [pltpu.with_memory_space_constraint(a, pltpu.HBM) for a in sources]
    left, right, final, order = pl.pallas_call(
        _project_kernel,
        in_specs=[anywhere] * 8,
        out_specs=(vmem,) * 4,
        out_shape=(
            jax.ShapeDtypeStruct((half, LANES), jnp.bfloat16),
            jax.ShapeDtypeStruct((n, 8, LANES), jnp.bfloat16),
            jax.ShapeDtypeStruct(final.shape, final.dtype),
            jax.ShapeDtypeStruct((2, 4 * LANES, 8 * CHANS), jnp.bfloat16),
        ),
        scratch_shapes=[pltpu.VMEM(a.shape, a.dtype) for a in sources] + [pltpu.SemaphoreType.DMA((9,))],
        compiler_params=params,
        cost_estimate=pl.CostEstimate(
            flops=4 * seqs * residues * feats * CHANS, bytes_accessed=2 * seqs * residues * feats, transcendentals=0
        ),
    )(*sources, pltpu.with_memory_space_constraint(final, pltpu.HBM))

    right = lax.all_to_all(right, "row", split_axis=0, concat_axis=0, tiled=True)

    part = 32
    parts = n // part
    pieces = [left] + [_xor(left, m, n) for m in range(8, n, 8)]
    pieces = [pieces[k ^ (k // 2 % 2)] for k in range(len(pieces))]
    line = pl.pallas_call(
        _line_kernel,
        in_specs=[vmem] * (len(pieces) + 1),
        out_specs=vmem,
        out_shape=jax.ShapeDtypeStruct((band, parts * 8 * CHANS), jnp.bfloat16),
        compiler_params=params,
        cost_estimate=pl.CostEstimate(flops=2**27, bytes_accessed=2**20, transcendentals=0),
    )(*pieces, order)
    x, y = _xor(line, 2, n), _xor(line, 4, n)

    fold_cost = pl.CostEstimate(
        flops=2 * n * 32 * 256 * CHANS * zdim, bytes_accessed=4 * n * CHANS * cols * zdim, transcendentals=0
    )
    fold_out = jax.ShapeDtypeStruct((8, parts, 8 * CHANS, cols * zdim), jnp.bfloat16)
    if small:
        specs = dict(in_specs=[vmem, vmem], out_specs=vmem)
    else:
        specs = dict(
            grid=(parts,),
            in_specs=[
                pl.BlockSpec((part, 8, LANES), lambda i: (i, 0, 0)),
                pl.BlockSpec(final.shape, lambda i: (0, 0)),
            ],
            out_specs=pl.BlockSpec((8, 1, 8 * CHANS, cols * zdim), lambda i: (0, i, 0, 0)),
        )
    folded = pl.pallas_call(
        _fold_kernel,
        out_shape=fold_out,
        scratch_shapes=[pltpu.VMEM((part * 8, LANES), jnp.float32), pltpu.VMEM((part * 16, LANES), jnp.float32)],
        compiler_params=params,
        cost_estimate=fold_cost,
        **specs,
    )(right, final)

    pinned = pltpu.with_memory_space_constraint(pair, pltpu.HBM)

    def add(lines, masks, total, last=False, scaled=False, carried=None):
        depth = len(masks) * parts * 8 * CHANS
        carries = masks == (1, 3, 5)
        operands = [*lines, folded] + ([] if total is None else [total])
        in_specs = [vmem] * len(operands)
        if not small:
            in_specs[len(lines)] = anywhere
        if scaled and not last:
            operands.append(shift.reshape(1, -1))
            in_specs.append(vmem)
        out_shape, out_specs, scratch = jax.ShapeDtypeStruct((band, cols * zdim), jnp.float32), vmem, []
        if carries:
            operands.append(pinned)
            in_specs.append(anywhere)
            out_shape, out_specs = (out_shape, jax.ShapeDtypeStruct(pair.shape, pair.dtype)), (vmem, vmem)
            scratch = [pltpu.SemaphoreType.DMA(())]
        if last:
            operands.append(carried)
            in_specs.append(vmem)
            out_shape, out_specs = jax.ShapeDtypeStruct(pair.shape, jnp.bfloat16), anywhere
            scratch = [
                pltpu.VMEM((band * (3 * cols + 1), zdim), jnp.float32),
                pltpu.VMEM(pair.shape, jnp.bfloat16),
                pltpu.SemaphoreType.DMA((band // 32,)),
            ]
        if not small:
            scratch.append(pltpu.VMEM((depth, 256), jnp.bfloat16))
        return pl.pallas_call(
            functools.partial(_band_kernel, masks, total is None, 1.0 / count if scaled else None, last, small),
            in_specs=in_specs,
            out_specs=out_specs,
            out_shape=out_shape,
            scratch_shapes=scratch,
            compiler_params=params,
            cost_estimate=pl.CostEstimate(
                flops=band * cols * zdim, bytes_accessed=band * cols, transcendentals=0
            ),
        )(*operands)

    x, y, folded = lax.optimization_barrier((x, y, folded))
    cut = band * 9 // 16
    upper, lower = _xor(x[:cut], 4, n), _xor(y[cut:], 2, n)
    across = _xor(jnp.stack([line, x, y]), 1, n)
    total = add([line, x, y], (0, 2, 4), None)
    total, carried = add([across], (1, 3, 5), total)
    upper, total = lax.optimization_barrier((upper, total))
    last = [_xor(upper, 1, n)]
    lower, total = lax.optimization_barrier((lower, total))
    last.append(_xor(lower, 1, n))
    total = add([upper, lower], (6,), total, scaled=True)
    return add(last, (7,), total, last=True, scaled=True, carried=carried)


def solution(mesh):
    placed = (P(("group", "row"), None, None), P("group", "row", None)) + (P(),) * 8
    return jax.shard_map(
        functools.partial(shards, mesh.shape["row"]),
        mesh=mesh,
        in_specs=placed,
        out_specs=P("group", "row", None),
        check_vma=False,
    )
```

```python
import functools

import jax
import jax.numpy as jnp
from jax import lax
from jax.experimental import pallas as pl
from jax.experimental.pallas import tpu as pltpu
from jax.sharding import PartitionSpec as P

LANES = 128
CHANS = 32
NT = (((1,), (1,)), ((), ()))


def _stacked(weights, copies):
    c, q = weights.shape
    rows = []
    for k in range(copies):
        left = [jnp.zeros((c, k * q), weights.dtype)] if k else []
        right = [jnp.zeros((c, (copies - 1 - k) * q), weights.dtype)] if k < copies - 1 else []
        rows.append(jnp.concatenate(left + [weights] + right, axis=1))
    return jnp.concatenate(rows, axis=0)


def _order(me, half):
    row = lax.broadcasted_iota(jnp.int32, (4 * LANES, 8 * CHANS), 0)
    col = lax.broadcasted_iota(jnp.int32, (4 * LANES, 8 * CHANS), 1)
    device = (row // LANES) ^ (me // 8 % 4)
    wanted = (row % CHANS) * 8 + ((row // CHANS) % 2) * 4 + device
    hit = (wanted == col) & ((row // (2 * CHANS)) % 2 == half)
    return jnp.where(hit, 1.0, 0.0).astype(jnp.bfloat16)


def _project_kernel(*refs):
    sources, final_source, outs, held = refs[:7], refs[7], refs[8:12], refs[12:19]
    left_ref, right_ref, final_ref, order_ref = outs
    sems = refs[19]
    pieces = 4
    size = held[0].shape[1] // pieces
    at = [(s, pl.ds(k * size, size)) for s in range(2) for k in range(pieces)]
    pairs = [(sources[0].at[i], held[0].at[i]) for i in at]
    pairs += list(zip(sources[1:], held[1:])) + [(final_source, final_ref)]
    copies = [pltpu.make_async_copy(a, b, sems.at[i]) for i, (a, b) in enumerate(pairs)]
    for copy in copies:
        copy.start()
    me = lax.axis_index("row")
    for h in range(2):
        order_ref[h] = _order(me, h)
    for copy in copies[:pieces] + copies[2 * pieces : -1]:
        copy.wait()
    x_ref, gain_ref, bias_ref, w1_ref, b1_ref, w2_ref, b2_ref = held
    half = left_ref.shape[0]
    n = right_ref.shape[0]
    feats = x_ref.shape[2]
    split = []
    for s in range(2):
        if s:
            for copy in copies[pieces : 2 * pieces]:
                copy.wait()
        x = x_ref[s].astype(jnp.float32)
        center = jnp.mean(x, axis=-1, keepdims=True)
        off = x - center
        spread = jnp.mean(off * off, axis=-1, keepdims=True)
        normed = off * lax.rsqrt(spread + 1e-05) * gain_ref[...] + bias_ref[...]
        split.append(normed.reshape(n, 2, 8, feats))
    parts = [split[s][:, jh].reshape(n * 8, feats).astype(jnp.bfloat16) for jh in range(2) for s in range(2)]
    weights = jnp.concatenate([_stacked(w1_ref[...], 4), _stacked(w2_ref[...], 4)], axis=0)
    shifts = jnp.concatenate([b1_ref[...]] * 4 + [b2_ref[...]] * 4, axis=1)
    both = lax.dot_general(jnp.concatenate(parts, axis=1), weights, NT, preferred_element_type=jnp.float32) + shifts
    left_ref[...] = both[:half, :LANES].astype(jnp.bfloat16)
    right_ref[...] = both[:, LANES:].reshape(n, 8, LANES).astype(jnp.bfloat16)
    copies[-1].wait()


def _line_kernel(*refs):
    pieces, order_ref, out_ref = refs[:-2], refs[-2], refs[-1]
    half = pieces[0].shape[0]
    wide = order_ref.shape[2]
    for q in range(len(pieces) // 4):
        lhs = jnp.concatenate([pieces[q * 4 + k][...] for k in (0, 1, 3, 2)], axis=1)
        for h in range(2):
            moved = jnp.dot(lhs, order_ref[h], preferred_element_type=jnp.float32)
            out_ref[pl.ds(h * half, half), pl.ds(q * wide, wide)] = moved.astype(jnp.bfloat16)


def _fold_kernel(right_ref, final_ref, out_ref, block_ref, pairs_ref):
    devices = right_ref.shape[0]
    groups = devices // 4
    block_ref[...] = right_ref[...].astype(jnp.float32).reshape(devices * 8, LANES)
    for jr in range(8):
        for g in range(groups):
            four = block_ref[pl.ds(g * 8 + jr, 4, stride=groups * 8), :]
            for s in range(2):
                pairs_ref[pl.ds((jr * groups + g) * 8 + s * 4, 4), :] = four
    block = pairs_ref[...]
    lane = lax.broadcasted_iota(jnp.int32, block.shape, 1) // CHANS
    s = lax.broadcasted_iota(jnp.int32, block.shape, 0) // 4 % 2
    lhs = [jnp.where(lane == jh * 2 + s, block, 0.0).astype(jnp.bfloat16) for jh in range(2)]
    lhs = jnp.concatenate(lhs, axis=0)

    for pair in range(CHANS // 2):
        rhs = []
        for k in range(2):
            at = pair * 2 * CHANS + k * CHANS
            rhs.append(jnp.concatenate([final_ref[pl.ds(at, CHANS), :]] * 4, axis=0))
        res = jnp.dot(lhs, jnp.concatenate(rhs, axis=1), preferred_element_type=jnp.float32)
        for j in range(16):
            for g in range(groups):
                r = (j * groups + g) * 8
                tile = jnp.concatenate([res[r : r + 8, :LANES], res[r : r + 8, LANES:]], axis=0)
                out_ref[g, 0, pl.ds(pair * 16, 16), pl.ds(j * LANES, LANES)] = tile.astype(jnp.bfloat16)


def _band_kernel(masks, begins, scale, last, held, *refs):
    refs = list(refs)
    take = lambda k: [refs.pop(0) for _ in range(k)]
    if masks == (1, 3, 5):
        (block,) = take(1)
        lines = [[block.at[k]] for k in range(3)]
    else:
        lines = [take(2 if mask in (6, 7) else 1) for mask in masks]
    (t_ref,) = take(1)
    (sum_ref,) = (None,) if begins else take(1)
    shift_ref = None if scale is None or last else take(1)[0]
    carries = masks == (1, 3, 5)
    pair_ref = take(1)[0] if last or carries else None
    (out_ref,) = take(1)
    if carries:
        held_pair, pair_sem = take(2)
        fetch = pltpu.make_async_copy(pair_ref, held_pair, pair_sem)
        fetch.start()
    me = lax.axis_index("row")
    wide = t_ref.shape[2]
    chunks = [((me % 8) ^ mask, q ^ (me // 32)) for mask in masks for q in range(t_ref.shape[1])]

    tile = 256 if last or not held else 512
    band = sum(part.shape[0] for part in lines[0])

    def column(begin):
        at = pl.ds(begin, tile)
        if held:
            rhs = jnp.concatenate([t_ref[g, q, :, at] for g, q in chunks], axis=0)
        else:
            for i, (g, q) in enumerate(chunks):
                pltpu.sync_copy(t_ref.at[g, q, :, at], refs[0].at[pl.ds(i * wide, wide)])
            rhs = refs[0][...]
        lhs = jnp.concatenate([jnp.concatenate([part[...] for part in line], axis=0) for line in lines], axis=1)
        res = jnp.dot(lhs, rhs, preferred_element_type=jnp.float32)
        if last:
            return res * scale + sum_ref[:, at]
        if sum_ref is not None:
            res = res + sum_ref[:, at]
        if shift_ref is not None:
            res = res * scale + jnp.concatenate([shift_ref[...]] * (tile // LANES), axis=1)
        return res

    if not last:
        for begin in range(0, t_ref.shape[3], tile):
            out_ref[:, pl.ds(begin, tile)] = column(begin)
        if carries:
            fetch.wait()
        return

    acc_ref, done_ref, sems = take(3)
    cols = pair_ref.shape[1]
    gap = 3
    pitch = gap * cols + 1
    for begin in range(0, t_ref.shape[3], tile):
        res = column(begin)
        for k in range(tile // LANES):
            j = begin // LANES + k
            acc_ref[pl.ds(gap * j, band, stride=pitch), :] = res[:, k * LANES : (k + 1) * LANES]

    chunk = 32

    def finish(r, _):
        for k in range(chunk):
            i = r * chunk + k
            row = k // 8 % 2 * (band // 2) + (r * (chunk // 16) + k // 16) * 8 + k % 8
            total = acc_ref[pl.ds(row * pitch, cols, stride=gap), :]
            done_ref[i] = (pair_ref[i].astype(jnp.float32) + total).astype(jnp.bfloat16)
        at = pl.ds(pl.multiple_of(r * chunk, chunk), chunk)
        pltpu.make_async_copy(done_ref.at[at], out_ref.at[at], sems.at[r]).start()
        return 0

    lax.fori_loop(0, band // chunk, finish, 0)

    def drain(r, _):
        at = pl.ds(pl.multiple_of(r * chunk, chunk), chunk)
        pltpu.make_async_copy(done_ref.at[at], out_ref.at[at], sems.at[r]).wait()
        return 0

    lax.fori_loop(0, band // chunk, drain, 0)


def _xor(x, mask, n):
    return lax.ppermute(x, "row", [(i, i ^ mask) for i in range(n)])


def shards(n, alignment, pair, gain, bias, w1, b1, w2, b2, final, shift):
    seqs, residues, feats = alignment.shape
    band, cols, zdim = pair.shape
    half = band // 2
    count = float(seqs * n)
    small = n <= 32
    params = pltpu.CompilerParams(vmem_limit_bytes=(24 if small else 48) * 1024 * 1024)
    anywhere = pl.BlockSpec(memory_space=pl.ANY)
    vmem = pl.BlockSpec(memory_space=pltpu.VMEM)

    sources = [
        alignment, gain.reshape(1, -1), bias.reshape(1, -1), w1.T, b1.reshape(1, -1), w2.T, b2.reshape(1, -1)
    ]
    sources = [pltpu.with_memory_space_constraint(a, pltpu.HBM) for a in sources]
    left, right, final, order = pl.pallas_call(
        _project_kernel,
        in_specs=[anywhere] * 8,
        out_specs=(vmem,) * 4,
        out_shape=(
            jax.ShapeDtypeStruct((half, LANES), jnp.bfloat16),
            jax.ShapeDtypeStruct((n, 8, LANES), jnp.bfloat16),
            jax.ShapeDtypeStruct(final.shape, final.dtype),
            jax.ShapeDtypeStruct((2, 4 * LANES, 8 * CHANS), jnp.bfloat16),
        ),
        scratch_shapes=[pltpu.VMEM(a.shape, a.dtype) for a in sources] + [pltpu.SemaphoreType.DMA((15,))],
        compiler_params=params,
        cost_estimate=pl.CostEstimate(
            flops=4 * seqs * residues * feats * CHANS, bytes_accessed=2 * seqs * residues * feats, transcendentals=0
        ),
    )(*sources, pltpu.with_memory_space_constraint(final, pltpu.HBM))

    right = lax.all_to_all(right, "row", split_axis=0, concat_axis=0, tiled=True)

    part = 32
    parts = n // part
    pieces = [left] + [_xor(left, m, n) for m in range(8, n, 8)]
    pieces = [pieces[k ^ (k // 2 % 2)] for k in range(len(pieces))]
    line = pl.pallas_call(
        _line_kernel,
        in_specs=[vmem] * (len(pieces) + 1),
        out_specs=vmem,
        out_shape=jax.ShapeDtypeStruct((band, parts * 8 * CHANS), jnp.bfloat16),
        compiler_params=params,
        cost_estimate=pl.CostEstimate(flops=2**27, bytes_accessed=2**20, transcendentals=0),
    )(*pieces, order)
    x, y = _xor(line, 2, n), _xor(line, 4, n)

    fold_cost = pl.CostEstimate(
        flops=2 * n * 32 * 256 * CHANS * zdim, bytes_accessed=4 * n * CHANS * cols * zdim, transcendentals=0
    )
    fold_out = jax.ShapeDtypeStruct((8, parts, 8 * CHANS, cols * zdim), jnp.bfloat16)
    if small:
        specs = dict(in_specs=[vmem, vmem], out_specs=vmem)
    else:
        specs = dict(
            grid=(parts,),
            in_specs=[
                pl.BlockSpec((part, 8, LANES), lambda i: (i, 0, 0)),
                pl.BlockSpec(final.shape, lambda i: (0, 0)),
            ],
            out_specs=pl.BlockSpec((8, 1, 8 * CHANS, cols * zdim), lambda i: (0, i, 0, 0)),
        )
    folded = pl.pallas_call(
        _fold_kernel,
        out_shape=fold_out,
        scratch_shapes=[pltpu.VMEM((part * 8, LANES), jnp.float32), pltpu.VMEM((part * 16, LANES), jnp.float32)],
        compiler_params=params,
        cost_estimate=fold_cost,
        **specs,
    )(right, final)

    pinned = pltpu.with_memory_space_constraint(pair, pltpu.HBM)

    def add(lines, masks, total, last=False, scaled=False, carried=None):
        depth = len(masks) * parts * 8 * CHANS
        carries = masks == (1, 3, 5)
        operands = [*lines, folded] + ([] if total is None else [total])
        in_specs = [vmem] * len(operands)
        if not small:
            in_specs[len(lines)] = anywhere
        if scaled and not last:
            operands.append(shift.reshape(1, -1))
            in_specs.append(vmem)
        out_shape, out_specs, scratch = jax.ShapeDtypeStruct((band, cols * zdim), jnp.float32), vmem, []
        if carries:
            operands.append(pinned)
            in_specs.append(anywhere)
            out_shape, out_specs = (out_shape, jax.ShapeDtypeStruct(pair.shape, pair.dtype)), (vmem, vmem)
            scratch = [pltpu.SemaphoreType.DMA(())]
        if last:
            operands.append(carried)
            in_specs.append(vmem)
            out_shape, out_specs = jax.ShapeDtypeStruct(pair.shape, jnp.bfloat16), anywhere
            scratch = [
                pltpu.VMEM((band * (3 * cols + 1), zdim), jnp.float32),
                pltpu.VMEM(pair.shape, jnp.bfloat16),
                pltpu.SemaphoreType.DMA((band // 32,)),
            ]
        if not small:
            scratch.append(pltpu.VMEM((depth, 256), jnp.bfloat16))
        return pl.pallas_call(
            functools.partial(_band_kernel, masks, total is None, 1.0 / count if scaled else None, last, small),
            in_specs=in_specs,
            out_specs=out_specs,
            out_shape=out_shape,
            scratch_shapes=scratch,
            compiler_params=params,
            cost_estimate=pl.CostEstimate(
                flops=band * cols * zdim, bytes_accessed=band * cols, transcendentals=0
            ),
        )(*operands)

    x, y, folded = lax.optimization_barrier((x, y, folded))
    cut = band * 9 // 16
    upper, lower = _xor(x[:cut], 4, n), _xor(y[cut:], 2, n)
    across = _xor(jnp.stack([line, x, y]), 1, n)
    total = add([line, x, y], (0, 2, 4), None)
    total, carried = add([across], (1, 3, 5), total)
    upper, total = lax.optimization_barrier((upper, total))
    last = [_xor(upper, 1, n)]
    lower, total = lax.optimization_barrier((lower, total))
    last.append(_xor(lower, 1, n))
    total = add([upper, lower], (6,), total, scaled=True)
    return add(last, (7,), total, last=True, scaled=True, carried=carried)


def solution(mesh):
    placed = (P(("group", "row"), None, None), P("group", "row", None)) + (P(),) * 8
    return jax.shard_map(
        functools.partial(shards, mesh.shape["row"]),
        mesh=mesh,
        in_specs=placed,
        out_specs=P("group", "row", None),
        check_vma=False,
    )
```

```python
import functools

import jax
import jax.numpy as jnp
from jax import lax
from jax.experimental import pallas as pl
from jax.experimental.pallas import tpu as pltpu
from jax.sharding import PartitionSpec as P

LANES = 128
CHANS = 32
NT = (((1,), (1,)), ((), ()))


def _stacked(weights, copies):
    c, q = weights.shape
    rows = []
    for k in range(copies):
        left = [jnp.zeros((c, k * q), weights.dtype)] if k else []
        right = [jnp.zeros((c, (copies - 1 - k) * q), weights.dtype)] if k < copies - 1 else []
        rows.append(jnp.concatenate(left + [weights] + right, axis=1))
    return jnp.concatenate(rows, axis=0)


def _order(me, half):
    row = lax.broadcasted_iota(jnp.int32, (4 * LANES, 8 * CHANS), 0)
    col = lax.broadcasted_iota(jnp.int32, (4 * LANES, 8 * CHANS), 1)
    device = (row // LANES) ^ (me // 8 % 4)
    wanted = (row % CHANS) * 8 + ((row // CHANS) % 2) * 4 + device
    hit = (wanted == col) & ((row // (2 * CHANS)) % 2 == half)
    return jnp.where(hit, 1.0, 0.0).astype(jnp.bfloat16)


def _project_kernel(*refs):
    sources, final_source, outs, held = refs[:7], refs[7], refs[8:12], refs[12:19]
    left_ref, right_ref, final_ref, order_ref = outs
    sems = refs[19]
    pieces = 1
    size = held[0].shape[1] // pieces
    at = [(s, pl.ds(k * size, size)) for s in range(2) for k in range(pieces)]
    pairs = [(sources[0].at[i], held[0].at[i]) for i in at]
    pairs += list(zip(sources[1:], held[1:])) + [(final_source, final_ref)]
    copies = [pltpu.make_async_copy(a, b, sems.at[i]) for i, (a, b) in enumerate(pairs)]
    for copy in copies:
        copy.start()
    me = lax.axis_index("row")
    for h in range(2):
        order_ref[h] = _order(me, h)
    for copy in copies[:pieces] + copies[2 * pieces : -1]:
        copy.wait()
    x_ref, gain_ref, bias_ref, w1_ref, b1_ref, w2_ref, b2_ref = held
    half = left_ref.shape[0]
    n = right_ref.shape[0]
    feats = x_ref.shape[2]
    split = []
    for s in range(2):
        if s:
            for copy in copies[pieces : 2 * pieces]:
                copy.wait()
        x = x_ref[s].astype(jnp.float32)
        center = jnp.mean(x, axis=-1, keepdims=True)
        off = x - center
        spread = jnp.mean(off * off, axis=-1, keepdims=True)
        normed = off * lax.rsqrt(spread + 1e-05) * gain_ref[...] + bias_ref[...]
        split.append(normed.reshape(n, 2, 8, feats))
    parts = [split[s][:, jh].reshape(n * 8, feats).astype(jnp.bfloat16) for jh in range(2) for s in range(2)]
    weights = jnp.concatenate([_stacked(w1_ref[...], 4), _stacked(w2_ref[...], 4)], axis=0)
    shifts = jnp.concatenate([b1_ref[...]] * 4 + [b2_ref[...]] * 4, axis=1)
    both = lax.dot_general(jnp.concatenate(parts, axis=1), weights, NT, preferred_element_type=jnp.float32) + shifts
    left_ref[...] = both[:half, :LANES].astype(jnp.bfloat16)
    right_ref[...] = both[:, LANES:].reshape(n, 8, LANES).astype(jnp.bfloat16)
    copies[-1].wait()


def _line_kernel(*refs):
    pieces, order_ref, out_ref = refs[:-2], refs[-2], refs[-1]
    half = pieces[0].shape[0]
    wide = order_ref.shape[2]
    for q in range(len(pieces) // 4):
        lhs = jnp.concatenate([pieces[q * 4 + k][...] for k in (0, 1, 3, 2)], axis=1)
        for h in range(2):
            moved = jnp.dot(lhs, order_ref[h], preferred_element_type=jnp.float32)
            out_ref[pl.ds(h * half, half), pl.ds(q * wide, wide)] = moved.astype(jnp.bfloat16)


def _fold_kernel(right_ref, final_ref, out_ref, block_ref, pairs_ref):
    devices = right_ref.shape[0]
    groups = devices // 4
    block_ref[...] = right_ref[...].astype(jnp.float32).reshape(devices * 8, LANES)
    for jr in range(8):
        for g in range(groups):
            four = block_ref[pl.ds(g * 8 + jr, 4, stride=groups * 8), :]
            for s in range(2):
                pairs_ref[pl.ds((jr * groups + g) * 8 + s * 4, 4), :] = four
    block = pairs_ref[...]
    lane = lax.broadcasted_iota(jnp.int32, block.shape, 1) // CHANS
    s = lax.broadcasted_iota(jnp.int32, block.shape, 0) // 4 % 2
    lhs = [jnp.where(lane == jh * 2 + s, block, 0.0).astype(jnp.bfloat16) for jh in range(2)]
    lhs = jnp.concatenate(lhs, axis=0)

    for pair in range(CHANS // 2):
        rhs = []
        for k in range(2):
            at = pair * 2 * CHANS + k * CHANS
            rhs.append(jnp.concatenate([final_ref[pl.ds(at, CHANS), :]] * 4, axis=0))
        res = jnp.dot(lhs, jnp.concatenate(rhs, axis=1), preferred_element_type=jnp.float32)
        for j in range(16):
            for g in range(groups):
                r = (j * groups + g) * 8
                tile = jnp.concatenate([res[r : r + 8, :LANES], res[r : r + 8, LANES:]], axis=0)
                out_ref[g, 0, pl.ds(pair * 16, 16), pl.ds(j * LANES, LANES)] = tile.astype(jnp.bfloat16)


def _band_kernel(masks, begins, scale, last, carries, held, *refs):
    refs = list(refs)
    take = lambda k: [refs.pop(0) for _ in range(k)]
    lines = take(len(masks))
    (t_ref,) = take(1)
    (sum_ref,) = (None,) if begins else take(1)
    shift_ref = None if scale is None or last else take(1)[0]
    pair_ref = take(1)[0] if last or carries else None
    (out_ref,) = take(1)
    if carries:
        held_pair, pair_sem = take(2)
        fetch = pltpu.make_async_copy(pair_ref, held_pair, pair_sem)
        fetch.start()
    me = lax.axis_index("row")
    wide = t_ref.shape[2]
    first = 2 + me % 2 * 2
    offset = lambda mask: mask if mask < 8 else (first if mask < 10 else 6 - first) ^ (mask % 2)
    chunks = [((me % 8) ^ offset(mask), q ^ (me // 32)) for mask in masks for q in range(t_ref.shape[1])]

    tile = 256 if last or not held else 512
    band = lines[0].shape[0]

    def column(begin):
        at = pl.ds(begin, tile)
        if held:
            rhs = jnp.concatenate([t_ref[g, q, :, at] for g, q in chunks], axis=0)
        else:
            for i, (g, q) in enumerate(chunks):
                pltpu.sync_copy(t_ref.at[g, q, :, at], refs[0].at[pl.ds(i * wide, wide)])
            rhs = refs[0][...]
        lhs = jnp.concatenate([line[...] for line in lines], axis=1)
        res = jnp.dot(lhs, rhs, preferred_element_type=jnp.float32)
        if last:
            return res * scale + sum_ref[:, at]
        if sum_ref is not None:
            res = res + sum_ref[:, at]
        if shift_ref is not None:
            res = res * scale + jnp.concatenate([shift_ref[...]] * (tile // LANES), axis=1)
        return res

    if not last:
        for begin in range(0, t_ref.shape[3], tile):
            out_ref[:, pl.ds(begin, tile)] = column(begin)
        if carries:
            fetch.wait()
        return

    acc_ref, done_ref, sems = take(3)
    cols = pair_ref.shape[1]
    gap = 3
    pitch = gap * cols + 1
    for begin in range(0, t_ref.shape[3], tile):
        res = column(begin)
        for k in range(tile // LANES):
            j = begin // LANES + k
            acc_ref[pl.ds(gap * j, band, stride=pitch), :] = res[:, k * LANES : (k + 1) * LANES]

    chunk = 32

    def finish(r, _):
        for k in range(chunk):
            i = r * chunk + k
            row = k // 8 % 2 * (band // 2) + (r * (chunk // 16) + k // 16) * 8 + k % 8
            total = acc_ref[pl.ds(row * pitch, cols, stride=gap), :]
            done_ref[i] = (pair_ref[i].astype(jnp.float32) + total).astype(jnp.bfloat16)
        at = pl.ds(pl.multiple_of(r * chunk, chunk), chunk)
        pltpu.make_async_copy(done_ref.at[at], out_ref.at[at], sems.at[r]).start()
        return 0

    lax.fori_loop(0, band // chunk, finish, 0)

    def drain(r, _):
        at = pl.ds(pl.multiple_of(r * chunk, chunk), chunk)
        pltpu.make_async_copy(done_ref.at[at], out_ref.at[at], sems.at[r]).wait()
        return 0

    lax.fori_loop(0, band // chunk, drain, 0)


def _xor(x, mask, n):
    return lax.ppermute(x, "row", [(i, i ^ mask) for i in range(n)])


def shards(n, alignment, pair, gain, bias, w1, b1, w2, b2, final, shift):
    seqs, residues, feats = alignment.shape
    band, cols, zdim = pair.shape
    half = band // 2
    count = float(seqs * n)
    small = n <= 32
    params = pltpu.CompilerParams(vmem_limit_bytes=(24 if small else 48) * 1024 * 1024)
    anywhere = pl.BlockSpec(memory_space=pl.ANY)
    vmem = pl.BlockSpec(memory_space=pltpu.VMEM)

    sources = [
        alignment, gain.reshape(1, -1), bias.reshape(1, -1), w1.T, b1.reshape(1, -1), w2.T, b2.reshape(1, -1)
    ]
    sources = [pltpu.with_memory_space_constraint(a, pltpu.HBM) for a in sources]
    left, right, final, order = pl.pallas_call(
        _project_kernel,
        in_specs=[anywhere] * 8,
        out_specs=(vmem,) * 4,
        out_shape=(
            jax.ShapeDtypeStruct((half, LANES), jnp.bfloat16),
            jax.ShapeDtypeStruct((n, 8, LANES), jnp.bfloat16),
            jax.ShapeDtypeStruct(final.shape, final.dtype),
            jax.ShapeDtypeStruct((2, 4 * LANES, 8 * CHANS), jnp.bfloat16),
        ),
        scratch_shapes=[pltpu.VMEM(a.shape, a.dtype) for a in sources] + [pltpu.SemaphoreType.DMA((9,))],
        compiler_params=params,
        cost_estimate=pl.CostEstimate(
            flops=4 * seqs * residues * feats * CHANS, bytes_accessed=2 * seqs * residues * feats, transcendentals=0
        ),
    )(*sources, pltpu.with_memory_space_constraint(final, pltpu.HBM))

    right = lax.all_to_all(right, "row", split_axis=0, concat_axis=0, tiled=True)

    part = 32
    parts = n // part
    pieces = [left] + [_xor(left, m, n) for m in range(8, n, 8)]
    pieces = [pieces[k ^ (k // 2 % 2)] for k in range(len(pieces))]
    line = pl.pallas_call(
        _line_kernel,
        in_specs=[vmem] * (len(pieces) + 1),
        out_specs=vmem,
        out_shape=jax.ShapeDtypeStruct((band, parts * 8 * CHANS), jnp.bfloat16),
        compiler_params=params,
        cost_estimate=pl.CostEstimate(flops=2**27, bytes_accessed=2**20, transcendentals=0),
    )(*pieces, order)
    turn = lambda a, masks: lax.ppermute(a, "row", [(i, i ^ masks[i % 2]) for i in range(n)])
    partner = _xor(line, 1, n)
    near = turn(line, (2, 4))
    near_other = turn(partner, (2, 4))
    diagonal = turn(near, (4, 2))

    fold_cost = pl.CostEstimate(
        flops=2 * n * 32 * 256 * CHANS * zdim, bytes_accessed=4 * n * CHANS * cols * zdim, transcendentals=0
    )
    fold_out = jax.ShapeDtypeStruct((8, parts, 8 * CHANS, cols * zdim), jnp.bfloat16)
    if small:
        specs = dict(in_specs=[vmem, vmem], out_specs=vmem)
    else:
        specs = dict(
            grid=(parts,),
            in_specs=[
                pl.BlockSpec((part, 8, LANES), lambda i: (i, 0, 0)),
                pl.BlockSpec(final.shape, lambda i: (0, 0)),
            ],
            out_specs=pl.BlockSpec((8, 1, 8 * CHANS, cols * zdim), lambda i: (0, i, 0, 0)),
        )
    folded = pl.pallas_call(
        _fold_kernel,
        out_shape=fold_out,
        scratch_shapes=[pltpu.VMEM((part * 8, LANES), jnp.float32), pltpu.VMEM((part * 16, LANES), jnp.float32)],
        compiler_params=params,
        cost_estimate=fold_cost,
        **specs,
    )(right, final)

    pinned = pltpu.with_memory_space_constraint(pair, pltpu.HBM)

    def add(lines, masks, total, last=False, scaled=False, carries=False, carried=None):
        depth = len(masks) * parts * 8 * CHANS
        operands = [*lines, folded] + ([] if total is None else [total])
        in_specs = [vmem] * len(operands)
        if not small:
            in_specs[len(lines)] = anywhere
        if scaled and not last:
            operands.append(shift.reshape(1, -1))
            in_specs.append(vmem)
        out_shape, out_specs, scratch = jax.ShapeDtypeStruct((band, cols * zdim), jnp.float32), vmem, []
        if carries:
            operands.append(pinned)
            in_specs.append(anywhere)
            out_shape, out_specs = (out_shape, jax.ShapeDtypeStruct(pair.shape, pair.dtype)), (vmem, vmem)
            scratch = [pltpu.SemaphoreType.DMA(())]
        if last:
            operands.append(carried)
            in_specs.append(vmem)
            out_shape, out_specs = jax.ShapeDtypeStruct(pair.shape, jnp.bfloat16), anywhere
            scratch = [
                pltpu.VMEM((band * (3 * cols + 1), zdim), jnp.float32),
                pltpu.VMEM(pair.shape, jnp.bfloat16),
                pltpu.SemaphoreType.DMA((band // 32,)),
            ]
        if not small:
            scratch.append(pltpu.VMEM((depth, 256), jnp.bfloat16))
        return pl.pallas_call(
            functools.partial(_band_kernel, masks, total is None, 1.0 / count if scaled else None, last, carries, small),
            in_specs=in_specs,
            out_specs=out_specs,
            out_shape=out_shape,
            scratch_shapes=scratch,
            compiler_params=params,
            cost_estimate=pl.CostEstimate(
                flops=band * cols * zdim, bytes_accessed=band * cols, transcendentals=0
            ),
        )(*operands)

    far_other = _xor(near, 1, n)
    near_other, folded = lax.optimization_barrier((near_other, folded))
    far = _xor(near_other, 1, n)
    total, carried = add([line, partner, near, near_other], (0, 1, 8, 9), None, carries=True)
    diagonal, total = lax.optimization_barrier((diagonal, total))
    last = _xor(diagonal, 1, n)
    total = add([diagonal], (6,), total)
    total = add([far, far_other], (10, 11), total, scaled=True)
    return add([last], (7,), total, last=True, scaled=True, carried=carried)


def solution(mesh):
    placed = (P(("group", "row"), None, None), P("group", "row", None)) + (P(),) * 8
    return jax.shard_map(
        functools.partial(shards, mesh.shape["row"]),
        mesh=mesh,
        in_specs=placed,
        out_specs=P("group", "row", None),
        check_vma=False,
    )
```

```python
import functools

import jax
import jax.numpy as jnp
from jax import lax
from jax.experimental import pallas as pl
from jax.experimental.pallas import tpu as pltpu
from jax.sharding import PartitionSpec as P

LANES = 128
CHANS = 32
NT = (((1,), (1,)), ((), ()))


def _stacked(weights, copies):
    c, q = weights.shape
    rows = []
    for k in range(copies):
        left = [jnp.zeros((c, k * q), weights.dtype)] if k else []
        right = [jnp.zeros((c, (copies - 1 - k) * q), weights.dtype)] if k < copies - 1 else []
        rows.append(jnp.concatenate(left + [weights] + right, axis=1))
    return jnp.concatenate(rows, axis=0)


def _order(me, half):
    row = lax.broadcasted_iota(jnp.int32, (4 * LANES, 8 * CHANS), 0)
    col = lax.broadcasted_iota(jnp.int32, (4 * LANES, 8 * CHANS), 1)
    device = (row // LANES) ^ (me // 8 % 4)
    wanted = (row % CHANS) * 8 + ((row // CHANS) % 2) * 4 + device
    hit = (wanted == col) & ((row // (2 * CHANS)) % 2 == half)
    return jnp.where(hit, 1.0, 0.0).astype(jnp.bfloat16)


def _project_kernel(*refs):
    sources, final_source, outs, held = refs[:7], refs[7], refs[8:12], refs[12:19]
    left_ref, right_ref, final_ref, order_ref = outs
    sems = refs[19]
    pieces = 1
    size = held[0].shape[1] // pieces
    at = [(s, pl.ds(k * size, size)) for s in range(2) for k in range(pieces)]
    pairs = [(sources[0].at[i], held[0].at[i]) for i in at]
    pairs += list(zip(sources[1:], held[1:])) + [(final_source, final_ref)]
    copies = [pltpu.make_async_copy(a, b, sems.at[i]) for i, (a, b) in enumerate(pairs)]
    for copy in copies:
        copy.start()
    me = lax.axis_index("row")
    for h in range(2):
        order_ref[h] = _order(me, h)
    for copy in copies[:pieces] + copies[2 * pieces : -1]:
        copy.wait()
    x_ref, gain_ref, bias_ref, w1_ref, b1_ref, w2_ref, b2_ref = held
    half = left_ref.shape[0]
    n = right_ref.shape[0]
    feats = x_ref.shape[2]
    split = []
    for s in range(2):
        if s:
            for copy in copies[pieces : 2 * pieces]:
                copy.wait()
        x = x_ref[s].astype(jnp.float32)
        center = jnp.mean(x, axis=-1, keepdims=True)
        off = x - center
        spread = jnp.mean(off * off, axis=-1, keepdims=True)
        normed = off * lax.rsqrt(spread + 1e-05) * gain_ref[...] + bias_ref[...]
        split.append(normed.reshape(n, 2, 8, feats))
    parts = [split[s][:, jh].reshape(n * 8, feats).astype(jnp.bfloat16) for jh in range(2) for s in range(2)]
    weights = jnp.concatenate([_stacked(w1_ref[...], 4), _stacked(w2_ref[...], 4)], axis=0)
    shifts = jnp.concatenate([b1_ref[...]] * 4 + [b2_ref[...]] * 4, axis=1)
    both = lax.dot_general(jnp.concatenate(parts, axis=1), weights, NT, preferred_element_type=jnp.float32) + shifts
    left_ref[...] = both[:half, :LANES].astype(jnp.bfloat16)
    right_ref[...] = both[:, LANES:].reshape(n, 8, LANES).astype(jnp.bfloat16)
    copies[-1].wait()


def _line_kernel(*refs):
    pieces, order_ref, out_ref = refs[:-2], refs[-2], refs[-1]
    half = pieces[0].shape[0]
    wide = order_ref.shape[2]
    for q in range(len(pieces) // 4):
        lhs = jnp.concatenate([pieces[q * 4 + k][...] for k in (0, 1, 3, 2)], axis=1)
        for h in range(2):
            moved = jnp.dot(lhs, order_ref[h], preferred_element_type=jnp.float32)
            out_ref[pl.ds(h * half, half), pl.ds(q * wide, wide)] = moved.astype(jnp.bfloat16)


def _fold_kernel(right_ref, final_ref, out_ref, block_ref, pairs_ref):
    devices = right_ref.shape[0]
    groups = devices // 4
    block_ref[...] = right_ref[...].astype(jnp.float32).reshape(devices * 8, LANES)
    for jr in range(8):
        for g in range(groups):
            four = block_ref[pl.ds(g * 8 + jr, 4, stride=groups * 8), :]
            for s in range(2):
                pairs_ref[pl.ds((jr * groups + g) * 8 + s * 4, 4), :] = four
    block = pairs_ref[...]
    lane = lax.broadcasted_iota(jnp.int32, block.shape, 1) // CHANS
    s = lax.broadcasted_iota(jnp.int32, block.shape, 0) // 4 % 2
    lhs = [jnp.where(lane == jh * 2 + s, block, 0.0).astype(jnp.bfloat16) for jh in range(2)]
    lhs = jnp.concatenate(lhs, axis=0)

    for pair in range(CHANS // 2):
        rhs = []
        for k in range(2):
            at = pair * 2 * CHANS + k * CHANS
            rhs.append(jnp.concatenate([final_ref[pl.ds(at, CHANS), :]] * 4, axis=0))
        res = jnp.dot(lhs, jnp.concatenate(rhs, axis=1), preferred_element_type=jnp.float32)
        for j in range(16):
            for g in range(groups):
                r = (j * groups + g) * 8
                tile = jnp.concatenate([res[r : r + 8, :LANES], res[r : r + 8, LANES:]], axis=0)
                out_ref[g, 0, pl.ds(pair * 16, 16), pl.ds(j * LANES, LANES)] = tile.astype(jnp.bfloat16)


def _band_kernel(masks, begins, scale, last, carries, held, *refs):
    refs = list(refs)
    take = lambda k: [refs.pop(0) for _ in range(k)]
    lines = take(len(masks))
    (t_ref,) = take(1)
    (sum_ref,) = (None,) if begins else take(1)
    shift_ref = None if scale is None or last else take(1)[0]
    pair_ref = take(1)[0] if last or carries else None
    (out_ref,) = take(1)
    if carries:
        held_pair, pair_sem = take(2)
        fetch = pltpu.make_async_copy(pair_ref, held_pair, pair_sem)
        fetch.start()
    me = lax.axis_index("row")
    wide = t_ref.shape[2]
    first = 2 + me % 2 * 2
    offset = lambda mask: mask if mask < 8 else (first if mask < 10 else 6 - first) ^ (mask % 2)
    chunks = [((me % 8) ^ offset(mask), q ^ (me // 32)) for mask in masks for q in range(t_ref.shape[1])]

    tile = 256 if last or not held else 512
    band = lines[0].shape[0]

    def column(begin):
        at = pl.ds(begin, tile)
        if held:
            rhs = jnp.concatenate([t_ref[g, q, :, at] for g, q in chunks], axis=0)
        else:
            for i, (g, q) in enumerate(chunks):
                pltpu.sync_copy(t_ref.at[g, q, :, at], refs[0].at[pl.ds(i * wide, wide)])
            rhs = refs[0][...]
        lhs = jnp.concatenate([line[...] for line in lines], axis=1)
        res = jnp.dot(lhs, rhs, preferred_element_type=jnp.float32)
        if last:
            return res * scale + sum_ref[:, at]
        if sum_ref is not None:
            res = res + sum_ref[:, at]
        if shift_ref is not None:
            res = res * scale + jnp.concatenate([shift_ref[...]] * (tile // LANES), axis=1)
        return res

    if not last:
        for begin in range(0, t_ref.shape[3], tile):
            out_ref[:, pl.ds(begin, tile)] = column(begin)
        if carries:
            fetch.wait()
        return

    acc_ref, done_ref, sems = take(3)
    cols = pair_ref.shape[1]
    gap = 3
    pitch = gap * cols + 1
    for begin in range(0, t_ref.shape[3], tile):
        res = column(begin)
        for k in range(tile // LANES):
            j = begin // LANES + k
            acc_ref[pl.ds(gap * j, band, stride=pitch), :] = res[:, k * LANES : (k + 1) * LANES]

    chunk = 32

    def finish(r, _):
        for k in range(chunk):
            i = r * chunk + k
            row = k // 8 % 2 * (band // 2) + (r * (chunk // 16) + k // 16) * 8 + k % 8
            total = acc_ref[pl.ds(row * pitch, cols, stride=gap), :]
            done_ref[i] = (pair_ref[i].astype(jnp.float32) + total).astype(jnp.bfloat16)
        at = pl.ds(pl.multiple_of(r * chunk, chunk), chunk)
        pltpu.make_async_copy(done_ref.at[at], out_ref.at[at], sems.at[r]).start()
        return 0

    lax.fori_loop(0, band // chunk, finish, 0)

    def drain(r, _):
        at = pl.ds(pl.multiple_of(r * chunk, chunk), chunk)
        pltpu.make_async_copy(done_ref.at[at], out_ref.at[at], sems.at[r]).wait()
        return 0

    lax.fori_loop(0, band // chunk, drain, 0)


def _xor(x, mask, n):
    return lax.ppermute(x, "row", [(i, i ^ mask) for i in range(n)])


def shards(n, alignment, pair, gain, bias, w1, b1, w2, b2, final, shift):
    seqs, residues, feats = alignment.shape
    band, cols, zdim = pair.shape
    half = band // 2
    count = float(seqs * n)
    small = n <= 32
    params = pltpu.CompilerParams(vmem_limit_bytes=(24 if small else 48) * 1024 * 1024)
    anywhere = pl.BlockSpec(memory_space=pl.ANY)
    vmem = pl.BlockSpec(memory_space=pltpu.VMEM)

    sources = [
        alignment, gain.reshape(1, -1), bias.reshape(1, -1), w1.T, b1.reshape(1, -1), w2.T, b2.reshape(1, -1)
    ]
    sources = [pltpu.with_memory_space_constraint(a, pltpu.HBM) for a in sources]
    left, right, final, order = pl.pallas_call(
        _project_kernel,
        in_specs=[anywhere] * 8,
        out_specs=(vmem,) * 4,
        out_shape=(
            jax.ShapeDtypeStruct((half, LANES), jnp.bfloat16),
            jax.ShapeDtypeStruct((n, 8, LANES), jnp.bfloat16),
            jax.ShapeDtypeStruct(final.shape, final.dtype),
            jax.ShapeDtypeStruct((2, 4 * LANES, 8 * CHANS), jnp.bfloat16),
        ),
        scratch_shapes=[pltpu.VMEM(a.shape, a.dtype) for a in sources] + [pltpu.SemaphoreType.DMA((9,))],
        compiler_params=params,
        cost_estimate=pl.CostEstimate(
            flops=4 * seqs * residues * feats * CHANS, bytes_accessed=2 * seqs * residues * feats, transcendentals=0
        ),
    )(*sources, pltpu.with_memory_space_constraint(final, pltpu.HBM))

    right = lax.all_to_all(right, "row", split_axis=0, concat_axis=0, tiled=True)

    part = 32
    parts = n // part
    pieces = [left] + [_xor(left, m, n) for m in range(8, n, 8)]
    pieces = [pieces[k ^ (k // 2 % 2)] for k in range(len(pieces))]
    line = pl.pallas_call(
        _line_kernel,
        in_specs=[vmem] * (len(pieces) + 1),
        out_specs=vmem,
        out_shape=jax.ShapeDtypeStruct((band, parts * 8 * CHANS), jnp.bfloat16),
        compiler_params=params,
        cost_estimate=pl.CostEstimate(flops=2**27, bytes_accessed=2**20, transcendentals=0),
    )(*pieces, order)
    turn = lambda a, masks: lax.ppermute(a, "row", [(i, i ^ masks[i % 2]) for i in range(n)])
    partner = _xor(line, 1, n)
    near = turn(line, (2, 4))
    near_other = turn(partner, (2, 4))

    fold_cost = pl.CostEstimate(
        flops=2 * n * 32 * 256 * CHANS * zdim, bytes_accessed=4 * n * CHANS * cols * zdim, transcendentals=0
    )
    fold_out = jax.ShapeDtypeStruct((8, parts, 8 * CHANS, cols * zdim), jnp.bfloat16)
    if small:
        specs = dict(in_specs=[vmem, vmem], out_specs=vmem)
    else:
        specs = dict(
            grid=(parts,),
            in_specs=[
                pl.BlockSpec((part, 8, LANES), lambda i: (i, 0, 0)),
                pl.BlockSpec(final.shape, lambda i: (0, 0)),
            ],
            out_specs=pl.BlockSpec((8, 1, 8 * CHANS, cols * zdim), lambda i: (0, i, 0, 0)),
        )
    folded = pl.pallas_call(
        _fold_kernel,
        out_shape=fold_out,
        scratch_shapes=[pltpu.VMEM((part * 8, LANES), jnp.float32), pltpu.VMEM((part * 16, LANES), jnp.float32)],
        compiler_params=params,
        cost_estimate=fold_cost,
        **specs,
    )(right, final)

    pinned = pltpu.with_memory_space_constraint(pair, pltpu.HBM)

    def add(lines, masks, total, last=False, scaled=False, carries=False, carried=None):
        depth = len(masks) * parts * 8 * CHANS
        operands = [*lines, folded] + ([] if total is None else [total])
        in_specs = [vmem] * len(operands)
        if not small:
            in_specs[len(lines)] = anywhere
        if scaled and not last:
            operands.append(shift.reshape(1, -1))
            in_specs.append(vmem)
        out_shape, out_specs, scratch = jax.ShapeDtypeStruct((band, cols * zdim), jnp.float32), vmem, []
        if carries:
            operands.append(pinned)
            in_specs.append(anywhere)
            out_shape, out_specs = (out_shape, jax.ShapeDtypeStruct(pair.shape, pair.dtype)), (vmem, vmem)
            scratch = [pltpu.SemaphoreType.DMA(())]
        if last:
            operands.append(carried)
            in_specs.append(vmem)
            out_shape, out_specs = jax.ShapeDtypeStruct(pair.shape, jnp.bfloat16), anywhere
            scratch = [
                pltpu.VMEM((band * (3 * cols + 1), zdim), jnp.float32),
                pltpu.VMEM(pair.shape, jnp.bfloat16),
                pltpu.SemaphoreType.DMA((band // 32,)),
            ]
        if not small:
            scratch.append(pltpu.VMEM((depth, 256), jnp.bfloat16))
        return pl.pallas_call(
            functools.partial(_band_kernel, masks, total is None, 1.0 / count if scaled else None, last, carries, small),
            in_specs=in_specs,
            out_specs=out_specs,
            out_shape=out_shape,
            scratch_shapes=scratch,
            compiler_params=params,
            cost_estimate=pl.CostEstimate(
                flops=band * cols * zdim, bytes_accessed=band * cols, transcendentals=0
            ),
        )(*operands)

    total = add([line, partner], (0, 1), None)
    near, near_other, _ = lax.optimization_barrier((near, near_other, folded))
    diagonal = turn(near, (4, 2))
    far_other, far = _xor(near, 1, n), _xor(near_other, 1, n)
    total, carried = add([near, near_other], (8, 9), total, carries=True)
    diagonal, total = lax.optimization_barrier((diagonal, total))
    last = _xor(diagonal, 1, n)
    total = add([diagonal], (6,), total)
    total = add([far, far_other], (10, 11), total, scaled=True)
    return add([last], (7,), total, last=True, scaled=True, carried=carried)


def solution(mesh):
    placed = (P(("group", "row"), None, None), P("group", "row", None)) + (P(),) * 8
    return jax.shard_map(
        functools.partial(shards, mesh.shape["row"]),
        mesh=mesh,
        in_specs=placed,
        out_specs=P("group", "row", None),
        check_vma=False,
    )
```

```python
import functools

import jax
import jax.numpy as jnp
from jax import lax
from jax.experimental import pallas as pl
from jax.experimental.pallas import tpu as pltpu
from jax.sharding import PartitionSpec as P

LANES = 128
CHANS = 32
NT = (((1,), (1,)), ((), ()))


def _stacked(weights, copies):
    c, q = weights.shape
    rows = []
    for k in range(copies):
        left = [jnp.zeros((c, k * q), weights.dtype)] if k else []
        right = [jnp.zeros((c, (copies - 1 - k) * q), weights.dtype)] if k < copies - 1 else []
        rows.append(jnp.concatenate(left + [weights] + right, axis=1))
    return jnp.concatenate(rows, axis=0)


def _order(me, half):
    row = lax.broadcasted_iota(jnp.int32, (4 * LANES, 8 * CHANS), 0)
    col = lax.broadcasted_iota(jnp.int32, (4 * LANES, 8 * CHANS), 1)
    device = (row // LANES) ^ (me // 8 % 4)
    wanted = (row % CHANS) * 8 + ((row // CHANS) % 2) * 4 + device
    hit = (wanted == col) & ((row // (2 * CHANS)) % 2 == half)
    return jnp.where(hit, 1.0, 0.0).astype(jnp.bfloat16)


def _project_kernel(*refs):
    sources, final_source, outs, held = refs[:7], refs[7], refs[8:12], refs[12:19]
    left_ref, right_ref, final_ref, order_ref = outs
    sems = refs[19]
    pieces = 1
    size = held[0].shape[1] // pieces
    at = [(s, pl.ds(k * size, size)) for s in range(2) for k in range(pieces)]
    pairs = [(sources[0].at[i], held[0].at[i]) for i in at]
    pairs += list(zip(sources[1:], held[1:])) + [(final_source, final_ref)]
    copies = [pltpu.make_async_copy(a, b, sems.at[i]) for i, (a, b) in enumerate(pairs)]
    for copy in copies:
        copy.start()
    me = lax.axis_index("row")
    for h in range(2):
        order_ref[h] = _order(me, h)
    for copy in copies[:pieces] + copies[2 * pieces : -1]:
        copy.wait()
    x_ref, gain_ref, bias_ref, w1_ref, b1_ref, w2_ref, b2_ref = held
    half = left_ref.shape[0]
    n = right_ref.shape[0]
    feats = x_ref.shape[2]
    split = []
    for s in range(2):
        if s:
            for copy in copies[pieces : 2 * pieces]:
                copy.wait()
        x = x_ref[s].astype(jnp.float32)
        center = jnp.mean(x, axis=-1, keepdims=True)
        off = x - center
        spread = jnp.mean(off * off, axis=-1, keepdims=True)
        normed = off * lax.rsqrt(spread + 1e-05) * gain_ref[...] + bias_ref[...]
        split.append(normed.reshape(n, 2, 8, feats))
    parts = [split[s][:, jh].reshape(n * 8, feats).astype(jnp.bfloat16) for jh in range(2) for s in range(2)]
    weights = jnp.concatenate([_stacked(w1_ref[...], 4), _stacked(w2_ref[...], 4)], axis=0)
    shifts = jnp.concatenate([b1_ref[...]] * 4 + [b2_ref[...]] * 4, axis=1)
    both = lax.dot_general(jnp.concatenate(parts, axis=1), weights, NT, preferred_element_type=jnp.float32) + shifts
    left_ref[...] = both[:half, :LANES].astype(jnp.bfloat16)
    right_ref[...] = both[:, LANES:].reshape(n, 8, LANES).astype(jnp.bfloat16)
    copies[-1].wait()


def _line_kernel(*refs):
    pieces, order_ref, out_ref = refs[:-2], refs[-2], refs[-1]
    half = pieces[0].shape[0]
    wide = order_ref.shape[2]
    for q in range(len(pieces) // 4):
        lhs = jnp.concatenate([pieces[q * 4 + k][...] for k in (0, 1, 3, 2)], axis=1)
        for h in range(2):
            moved = jnp.dot(lhs, order_ref[h], preferred_element_type=jnp.float32)
            out_ref[pl.ds(h * half, half), pl.ds(q * wide, wide)] = moved.astype(jnp.bfloat16)


def _fold_kernel(right_ref, final_ref, out_ref, block_ref, pairs_ref):
    devices = right_ref.shape[0]
    groups = devices // 4
    block_ref[...] = right_ref[...].astype(jnp.float32).reshape(devices * 8, LANES)
    for jr in range(8):
        for g in range(groups):
            four = block_ref[pl.ds(g * 8 + jr, 4, stride=groups * 8), :]
            for s in range(2):
                pairs_ref[pl.ds((jr * groups + g) * 8 + s * 4, 4), :] = four
    block = pairs_ref[...]
    lane = lax.broadcasted_iota(jnp.int32, block.shape, 1) // CHANS
    s = lax.broadcasted_iota(jnp.int32, block.shape, 0) // 4 % 2
    lhs = [jnp.where(lane == jh * 2 + s, block, 0.0).astype(jnp.bfloat16) for jh in range(2)]
    lhs = jnp.concatenate(lhs, axis=0)

    for pair in range(CHANS // 2):
        rhs = []
        for k in range(2):
            at = pair * 2 * CHANS + k * CHANS
            rhs.append(jnp.concatenate([final_ref[pl.ds(at, CHANS), :]] * 4, axis=0))
        res = jnp.dot(lhs, jnp.concatenate(rhs, axis=1), preferred_element_type=jnp.float32)
        for j in range(16):
            for g in range(groups):
                r = (j * groups + g) * 8
                tile = jnp.concatenate([res[r : r + 8, :LANES], res[r : r + 8, LANES:]], axis=0)
                out_ref[g, 0, pl.ds(pair * 16, 16), pl.ds(j * LANES, LANES)] = tile.astype(jnp.bfloat16)


def _band_kernel(masks, begins, scale, last, carries, held, *refs):
    refs = list(refs)
    take = lambda k: [refs.pop(0) for _ in range(k)]
    lines = take(len(masks))
    (t_ref,) = take(1)
    (sum_ref,) = (None,) if begins else take(1)
    shift_ref = None if scale is None or last else take(1)[0]
    pair_ref = take(1)[0] if last or carries else None
    (out_ref,) = take(1)
    if carries:
        held_pair, pair_sem = take(2)
        fetch = pltpu.make_async_copy(pair_ref, held_pair, pair_sem)
        fetch.start()
    me = lax.axis_index("row")
    wide = t_ref.shape[2]
    first = 2 + me % 2 * 2
    offset = lambda mask: mask if mask < 8 else (first if mask < 10 else 6 - first) ^ (mask % 2)
    chunks = [((me % 8) ^ offset(mask), q ^ (me // 32)) for mask in masks for q in range(t_ref.shape[1])]

    tile = 256 if last or not held else 512
    band = lines[0].shape[0]

    def column(begin):
        at = pl.ds(begin, tile)
        if held:
            rhs = jnp.concatenate([t_ref[g, q, :, at] for g, q in chunks], axis=0)
        else:
            for i, (g, q) in enumerate(chunks):
                pltpu.sync_copy(t_ref.at[g, q, :, at], refs[0].at[pl.ds(i * wide, wide)])
            rhs = refs[0][...]
        lhs = jnp.concatenate([line[...] for line in lines], axis=1)
        res = jnp.dot(lhs, rhs, preferred_element_type=jnp.float32)
        if last:
            return res * scale + sum_ref[:, at]
        if sum_ref is not None:
            res = res + sum_ref[:, at]
        if shift_ref is not None:
            res = res * scale + jnp.concatenate([shift_ref[...]] * (tile // LANES), axis=1)
        return res

    if not last:
        for begin in range(0, t_ref.shape[3], tile):
            out_ref[:, pl.ds(begin, tile)] = column(begin)
        if carries:
            fetch.wait()
        return

    acc_ref, done_ref, sems = take(3)
    cols = pair_ref.shape[1]
    gap = 3
    pitch = gap * cols + 1
    for begin in range(0, t_ref.shape[3], tile):
        res = column(begin)
        for k in range(tile // LANES):
            j = begin // LANES + k
            acc_ref[pl.ds(gap * j, band, stride=pitch), :] = res[:, k * LANES : (k + 1) * LANES]

    chunk = 32

    def finish(r, _):
        for k in range(chunk):
            i = r * chunk + k
            row = k // 8 % 2 * (band // 2) + (r * (chunk // 16) + k // 16) * 8 + k % 8
            total = acc_ref[pl.ds(row * pitch, cols, stride=gap), :]
            done_ref[i] = (pair_ref[i].astype(jnp.float32) + total).astype(jnp.bfloat16)
        at = pl.ds(pl.multiple_of(r * chunk, chunk), chunk)
        pltpu.make_async_copy(done_ref.at[at], out_ref.at[at], sems.at[r]).start()
        return 0

    lax.fori_loop(0, band // chunk, finish, 0)

    def drain(r, _):
        at = pl.ds(pl.multiple_of(r * chunk, chunk), chunk)
        pltpu.make_async_copy(done_ref.at[at], out_ref.at[at], sems.at[r]).wait()
        return 0

    lax.fori_loop(0, band // chunk, drain, 0)


def _xor(x, mask, n):
    return lax.ppermute(x, "row", [(i, i ^ mask) for i in range(n)])


def shards(n, alignment, pair, gain, bias, w1, b1, w2, b2, final, shift):
    seqs, residues, feats = alignment.shape
    band, cols, zdim = pair.shape
    half = band // 2
    count = float(seqs * n)
    small = n <= 32
    params = pltpu.CompilerParams(vmem_limit_bytes=(24 if small else 48) * 1024 * 1024)
    anywhere = pl.BlockSpec(memory_space=pl.ANY)
    vmem = pl.BlockSpec(memory_space=pltpu.VMEM)

    sources = [
        alignment, gain.reshape(1, -1), bias.reshape(1, -1), w1.T, b1.reshape(1, -1), w2.T, b2.reshape(1, -1)
    ]
    sources = [pltpu.with_memory_space_constraint(a, pltpu.HBM) for a in sources]
    left, right, final, order = pl.pallas_call(
        _project_kernel,
        in_specs=[anywhere] * 8,
        out_specs=(vmem,) * 4,
        out_shape=(
            jax.ShapeDtypeStruct((half, LANES), jnp.bfloat16),
            jax.ShapeDtypeStruct((n, 8, LANES), jnp.bfloat16),
            jax.ShapeDtypeStruct(final.shape, final.dtype),
            jax.ShapeDtypeStruct((2, 4 * LANES, 8 * CHANS), jnp.bfloat16),
        ),
        scratch_shapes=[pltpu.VMEM(a.shape, a.dtype) for a in sources] + [pltpu.SemaphoreType.DMA((9,))],
        compiler_params=params,
        cost_estimate=pl.CostEstimate(
            flops=4 * seqs * residues * feats * CHANS, bytes_accessed=2 * seqs * residues * feats, transcendentals=0
        ),
    )(*sources, pltpu.with_memory_space_constraint(final, pltpu.HBM))

    right = lax.all_to_all(right, "row", split_axis=0, concat_axis=0, tiled=True)

    part = 32
    parts = n // part
    pieces = [left] + [_xor(left, m, n) for m in range(8, n, 8)]
    pieces = [pieces[k ^ (k // 2 % 2)] for k in range(len(pieces))]
    line = pl.pallas_call(
        _line_kernel,
        in_specs=[vmem] * (len(pieces) + 1),
        out_specs=vmem,
        out_shape=jax.ShapeDtypeStruct((band, parts * 8 * CHANS), jnp.bfloat16),
        compiler_params=params,
        cost_estimate=pl.CostEstimate(flops=2**27, bytes_accessed=2**20, transcendentals=0),
    )(*pieces, order)
    turn = lambda a, masks: lax.ppermute(a, "row", [(i, i ^ masks[i % 2]) for i in range(n)])
    partner = _xor(line, 1, n)
    near = turn(line, (2, 4))
    near_other = turn(line, (5, 3))

    fold_cost = pl.CostEstimate(
        flops=2 * n * 32 * 256 * CHANS * zdim, bytes_accessed=4 * n * CHANS * cols * zdim, transcendentals=0
    )
    fold_out = jax.ShapeDtypeStruct((8, parts, 8 * CHANS, cols * zdim), jnp.bfloat16)
    if small:
        specs = dict(in_specs=[vmem, vmem], out_specs=vmem)
    else:
        specs = dict(
            grid=(parts,),
            in_specs=[
                pl.BlockSpec((part, 8, LANES), lambda i: (i, 0, 0)),
                pl.BlockSpec(final.shape, lambda i: (0, 0)),
            ],
            out_specs=pl.BlockSpec((8, 1, 8 * CHANS, cols * zdim), lambda i: (0, i, 0, 0)),
        )
    folded = pl.pallas_call(
        _fold_kernel,
        out_shape=fold_out,
        scratch_shapes=[pltpu.VMEM((part * 8, LANES), jnp.float32), pltpu.VMEM((part * 16, LANES), jnp.float32)],
        compiler_params=params,
        cost_estimate=fold_cost,
        **specs,
    )(right, final)

    pinned = pltpu.with_memory_space_constraint(pair, pltpu.HBM)

    def add(lines, masks, total, last=False, scaled=False, carries=False, carried=None):
        depth = len(masks) * parts * 8 * CHANS
        operands = [*lines, folded] + ([] if total is None else [total])
        in_specs = [vmem] * len(operands)
        if not small:
            in_specs[len(lines)] = anywhere
        if scaled and not last:
            operands.append(shift.reshape(1, -1))
            in_specs.append(vmem)
        out_shape, out_specs, scratch = jax.ShapeDtypeStruct((band, cols * zdim), jnp.float32), vmem, []
        if carries:
            operands.append(pinned)
            in_specs.append(anywhere)
            out_shape, out_specs = (out_shape, jax.ShapeDtypeStruct(pair.shape, pair.dtype)), (vmem, vmem)
            scratch = [pltpu.SemaphoreType.DMA(())]
        if last:
            operands.append(carried)
            in_specs.append(vmem)
            out_shape, out_specs = jax.ShapeDtypeStruct(pair.shape, jnp.bfloat16), anywhere
            scratch = [
                pltpu.VMEM((band * (3 * cols + 1), zdim), jnp.float32),
                pltpu.VMEM(pair.shape, jnp.bfloat16),
                pltpu.SemaphoreType.DMA((band // 32,)),
            ]
        if not small:
            scratch.append(pltpu.VMEM((depth, 256), jnp.bfloat16))
        return pl.pallas_call(
            functools.partial(_band_kernel, masks, total is None, 1.0 / count if scaled else None, last, carries, small),
            in_specs=in_specs,
            out_specs=out_specs,
            out_shape=out_shape,
            scratch_shapes=scratch,
            compiler_params=params,
            cost_estimate=pl.CostEstimate(
                flops=band * cols * zdim, bytes_accessed=band * cols, transcendentals=0
            ),
        )(*operands)

    total = add([line, partner], (0, 1), None)
    near, near_other, _ = lax.optimization_barrier((near, near_other, folded))
    diagonal = turn(near, (4, 2))
    far_other, far = _xor(near, 1, n), _xor(near_other, 1, n)
    total, carried = add([near, near_other], (8, 9), total, carries=True)
    diagonal, total = lax.optimization_barrier((diagonal, total))
    last = _xor(diagonal, 1, n)
    total = add([diagonal], (6,), total)
    total = add([far, far_other], (10, 11), total, scaled=True)
    return add([last], (7,), total, last=True, scaled=True, carried=carried)


def solution(mesh):
    placed = (P(("group", "row"), None, None), P("group", "row", None)) + (P(),) * 8
    return jax.shard_map(
        functools.partial(shards, mesh.shape["row"]),
        mesh=mesh,
        in_specs=placed,
        out_specs=P("group", "row", None),
        check_vma=False,
    )
```

```python
import functools

import jax
import jax.numpy as jnp
from jax import lax
from jax.experimental import pallas as pl
from jax.experimental.pallas import tpu as pltpu
from jax.sharding import PartitionSpec as P

LANES = 128
CHANS = 32
NT = (((1,), (1,)), ((), ()))


def _stacked(weights, copies):
    c, q = weights.shape
    rows = []
    for k in range(copies):
        left = [jnp.zeros((c, k * q), weights.dtype)] if k else []
        right = [jnp.zeros((c, (copies - 1 - k) * q), weights.dtype)] if k < copies - 1 else []
        rows.append(jnp.concatenate(left + [weights] + right, axis=1))
    return jnp.concatenate(rows, axis=0)


def _order(me, half):
    row = lax.broadcasted_iota(jnp.int32, (4 * LANES, 8 * CHANS), 0)
    col = lax.broadcasted_iota(jnp.int32, (4 * LANES, 8 * CHANS), 1)
    device = (row // LANES) ^ (me // 8 % 4)
    wanted = (row % CHANS) * 8 + ((row // CHANS) % 2) * 4 + device
    hit = (wanted == col) & ((row // (2 * CHANS)) % 2 == half)
    return jnp.where(hit, 1.0, 0.0).astype(jnp.bfloat16)


def _project_kernel(*refs):
    sources, final_source, outs, held = refs[:7], refs[7], refs[8:12], refs[12:19]
    left_ref, right_ref, final_ref, order_ref = outs
    sems = refs[19]
    pieces = 1
    size = held[0].shape[1] // pieces
    at = [(s, pl.ds(k * size, size)) for s in range(2) for k in range(pieces)]
    pairs = [(sources[0].at[i], held[0].at[i]) for i in at]
    pairs += list(zip(sources[1:], held[1:])) + [(final_source, final_ref)]
    copies = [pltpu.make_async_copy(a, b, sems.at[i]) for i, (a, b) in enumerate(pairs)]
    for copy in copies:
        copy.start()
    me = lax.axis_index("row")
    for h in range(2):
        order_ref[h] = _order(me, h)
    for copy in copies[:pieces] + copies[2 * pieces : -1]:
        copy.wait()
    x_ref, gain_ref, bias_ref, w1_ref, b1_ref, w2_ref, b2_ref = held
    half = left_ref.shape[0]
    n = right_ref.shape[0]
    feats = x_ref.shape[2]
    split = []
    for s in range(2):
        if s:
            for copy in copies[pieces : 2 * pieces]:
                copy.wait()
        x = x_ref[s].astype(jnp.float32)
        center = jnp.mean(x, axis=-1, keepdims=True)
        off = x - center
        spread = jnp.mean(off * off, axis=-1, keepdims=True)
        normed = off * lax.rsqrt(spread + 1e-05) * gain_ref[...] + bias_ref[...]
        split.append(normed.reshape(n, 2, 8, feats))
    parts = [split[s][:, jh].reshape(n * 8, feats).astype(jnp.bfloat16) for jh in range(2) for s in range(2)]
    weights = jnp.concatenate([_stacked(w1_ref[...], 4), _stacked(w2_ref[...], 4)], axis=0)
    shifts = jnp.concatenate([b1_ref[...]] * 4 + [b2_ref[...]] * 4, axis=1)
    both = lax.dot_general(jnp.concatenate(parts, axis=1), weights, NT, preferred_element_type=jnp.float32) + shifts
    left_ref[...] = both[:half, :LANES].astype(jnp.bfloat16)
    right_ref[...] = both[:, LANES:].reshape(n, 8, LANES).astype(jnp.bfloat16)
    copies[-1].wait()


def _line_kernel(*refs):
    pieces, order_ref, out_ref = refs[:-2], refs[-2], refs[-1]
    half = pieces[0].shape[0]
    wide = order_ref.shape[2]
    for q in range(len(pieces) // 4):
        lhs = jnp.concatenate([pieces[q * 4 + k][...] for k in (0, 1, 3, 2)], axis=1)
        for h in range(2):
            moved = jnp.dot(lhs, order_ref[h], preferred_element_type=jnp.float32)
            out_ref[pl.ds(h * half, half), pl.ds(q * wide, wide)] = moved.astype(jnp.bfloat16)


def _fold_kernel(right_ref, final_ref, out_ref, block_ref, pairs_ref):
    devices = right_ref.shape[0]
    groups = devices // 4
    block_ref[...] = right_ref[...].astype(jnp.float32).reshape(devices * 8, LANES)
    for jr in range(8):
        for g in range(groups):
            four = block_ref[pl.ds(g * 8 + jr, 4, stride=groups * 8), :]
            for s in range(2):
                pairs_ref[pl.ds((jr * groups + g) * 8 + s * 4, 4), :] = four
    block = pairs_ref[...]
    lane = lax.broadcasted_iota(jnp.int32, block.shape, 1) // CHANS
    s = lax.broadcasted_iota(jnp.int32, block.shape, 0) // 4 % 2
    lhs = [jnp.where(lane == jh * 2 + s, block, 0.0).astype(jnp.bfloat16) for jh in range(2)]
    lhs = jnp.concatenate(lhs, axis=0)

    for pair in range(CHANS // 2):
        rhs = []
        for k in range(2):
            at = pair * 2 * CHANS + k * CHANS
            rhs.append(jnp.concatenate([final_ref[pl.ds(at, CHANS), :]] * 4, axis=0))
        res = jnp.dot(lhs, jnp.concatenate(rhs, axis=1), preferred_element_type=jnp.float32)
        for j in range(16):
            for g in range(groups):
                r = (j * groups + g) * 8
                tile = jnp.concatenate([res[r : r + 8, :LANES], res[r : r + 8, LANES:]], axis=0)
                out_ref[g, 0, pl.ds(pair * 16, 16), pl.ds(j * LANES, LANES)] = tile.astype(jnp.bfloat16)


def _band_kernel(masks, begins, scale, last, carries, held, *refs):
    refs = list(refs)
    take = lambda k: [refs.pop(0) for _ in range(k)]
    lines = take(len(masks))
    (t_ref,) = take(1)
    (sum_ref,) = (None,) if begins else take(1)
    shift_ref = None if scale is None or last else take(1)[0]
    pair_ref = take(1)[0] if last or carries else None
    (out_ref,) = take(1)
    if carries:
        held_pair, pair_sem = take(2)
        fetch = pltpu.make_async_copy(pair_ref, held_pair, pair_sem)
        fetch.start()
    me = lax.axis_index("row")
    wide = t_ref.shape[2]
    first = 2 + me % 2 * 2
    offset = lambda mask: mask if mask < 8 else (first if mask < 10 else 6 - first) ^ (mask % 2)
    chunks = [((me % 8) ^ offset(mask), q ^ (me // 32)) for mask in masks for q in range(t_ref.shape[1])]

    tile = 256 if last or not held else 512
    band = lines[0].shape[0]

    def column(begin):
        at = pl.ds(begin, tile)
        if held:
            rhs = jnp.concatenate([t_ref[g, q, :, at] for g, q in chunks], axis=0)
        else:
            for i, (g, q) in enumerate(chunks):
                pltpu.sync_copy(t_ref.at[g, q, :, at], refs[0].at[pl.ds(i * wide, wide)])
            rhs = refs[0][...]
        lhs = jnp.concatenate([line[...] for line in lines], axis=1)
        res = jnp.dot(lhs, rhs, preferred_element_type=jnp.float32)
        if last:
            return res * scale + sum_ref[:, at]
        if sum_ref is not None:
            res = res + sum_ref[:, at]
        if shift_ref is not None:
            res = res * scale + jnp.concatenate([shift_ref[...]] * (tile // LANES), axis=1)
        return res

    if not last:
        for begin in range(0, t_ref.shape[3], tile):
            out_ref[:, pl.ds(begin, tile)] = column(begin)
        if carries:
            fetch.wait()
        return

    acc_ref, done_ref, sems = take(3)
    cols = pair_ref.shape[1]
    gap = 3
    pitch = gap * cols + 1
    for begin in range(0, t_ref.shape[3], tile):
        res = column(begin)
        for k in range(tile // LANES):
            j = begin // LANES + k
            acc_ref[pl.ds(gap * j, band, stride=pitch), :] = res[:, k * LANES : (k + 1) * LANES]

    chunk = 32

    def finish(r, _):
        for k in range(chunk):
            i = r * chunk + k
            row = k // 8 % 2 * (band // 2) + (r * (chunk // 16) + k // 16) * 8 + k % 8
            total = acc_ref[pl.ds(row * pitch, cols, stride=gap), :]
            done_ref[i] = (pair_ref[i].astype(jnp.float32) + total).astype(jnp.bfloat16)
        at = pl.ds(pl.multiple_of(r * chunk, chunk), chunk)
        pltpu.make_async_copy(done_ref.at[at], out_ref.at[at], sems.at[r]).start()
        return 0

    lax.fori_loop(0, band // chunk, finish, 0)

    def drain(r, _):
        at = pl.ds(pl.multiple_of(r * chunk, chunk), chunk)
        pltpu.make_async_copy(done_ref.at[at], out_ref.at[at], sems.at[r]).wait()
        return 0

    lax.fori_loop(0, band // chunk, drain, 0)


def _xor(x, mask, n):
    return lax.ppermute(x, "row", [(i, i ^ mask) for i in range(n)])


def shards(n, alignment, pair, gain, bias, w1, b1, w2, b2, final, shift):
    seqs, residues, feats = alignment.shape
    band, cols, zdim = pair.shape
    half = band // 2
    count = float(seqs * n)
    small = n <= 32
    params = pltpu.CompilerParams(vmem_limit_bytes=(24 if small else 48) * 1024 * 1024)
    anywhere = pl.BlockSpec(memory_space=pl.ANY)
    vmem = pl.BlockSpec(memory_space=pltpu.VMEM)

    sources = [
        alignment, gain.reshape(1, -1), bias.reshape(1, -1), w1.T, b1.reshape(1, -1), w2.T, b2.reshape(1, -1)
    ]
    sources = [pltpu.with_memory_space_constraint(a, pltpu.HBM) for a in sources]
    left, right, final, order = pl.pallas_call(
        _project_kernel,
        in_specs=[anywhere] * 8,
        out_specs=(vmem,) * 4,
        out_shape=(
            jax.ShapeDtypeStruct((half, LANES), jnp.bfloat16),
            jax.ShapeDtypeStruct((n, 8, LANES), jnp.bfloat16),
            jax.ShapeDtypeStruct(final.shape, final.dtype),
            jax.ShapeDtypeStruct((2, 4 * LANES, 8 * CHANS), jnp.bfloat16),
        ),
        scratch_shapes=[pltpu.VMEM(a.shape, a.dtype) for a in sources] + [pltpu.SemaphoreType.DMA((9,))],
        compiler_params=params,
        cost_estimate=pl.CostEstimate(
            flops=4 * seqs * residues * feats * CHANS, bytes_accessed=2 * seqs * residues * feats, transcendentals=0
        ),
    )(*sources, pltpu.with_memory_space_constraint(final, pltpu.HBM))

    right = lax.all_to_all(right, "row", split_axis=0, concat_axis=0, tiled=True)

    part = 32
    parts = n // part
    pieces = [left] + [_xor(left, m, n) for m in range(8, n, 8)]
    pieces = [pieces[k ^ (k // 2 % 2)] for k in range(len(pieces))]
    line = pl.pallas_call(
        _line_kernel,
        in_specs=[vmem] * (len(pieces) + 1),
        out_specs=vmem,
        out_shape=jax.ShapeDtypeStruct((band, parts * 8 * CHANS), jnp.bfloat16),
        compiler_params=params,
        cost_estimate=pl.CostEstimate(flops=2**27, bytes_accessed=2**20, transcendentals=0),
    )(*pieces, order)
    turn = lambda a, masks: lax.ppermute(a, "row", [(i, i ^ masks[i % 2]) for i in range(n)])
    partner = _xor(line, 1, n)
    near = turn(line, (2, 4))
    near_other = turn(line, (5, 3))
    near, right = lax.optimization_barrier((near, right))
    diagonal = turn(near, (4, 2))

    fold_cost = pl.CostEstimate(
        flops=2 * n * 32 * 256 * CHANS * zdim, bytes_accessed=4 * n * CHANS * cols * zdim, transcendentals=0
    )
    fold_out = jax.ShapeDtypeStruct((8, parts, 8 * CHANS, cols * zdim), jnp.bfloat16)
    if small:
        specs = dict(in_specs=[vmem, vmem], out_specs=vmem)
    else:
        specs = dict(
            grid=(parts,),
            in_specs=[
                pl.BlockSpec((part, 8, LANES), lambda i: (i, 0, 0)),
                pl.BlockSpec(final.shape, lambda i: (0, 0)),
            ],
            out_specs=pl.BlockSpec((8, 1, 8 * CHANS, cols * zdim), lambda i: (0, i, 0, 0)),
        )
    folded = pl.pallas_call(
        _fold_kernel,
        out_shape=fold_out,
        scratch_shapes=[pltpu.VMEM((part * 8, LANES), jnp.float32), pltpu.VMEM((part * 16, LANES), jnp.float32)],
        compiler_params=params,
        cost_estimate=fold_cost,
        **specs,
    )(right, final)

    pinned = pltpu.with_memory_space_constraint(pair, pltpu.HBM)

    def add(lines, masks, total, last=False, scaled=False, carries=False, carried=None):
        depth = len(masks) * parts * 8 * CHANS
        operands = [*lines, folded] + ([] if total is None else [total])
        in_specs = [vmem] * len(operands)
        if not small:
            in_specs[len(lines)] = anywhere
        if scaled and not last:
            operands.append(shift.reshape(1, -1))
            in_specs.append(vmem)
        out_shape, out_specs, scratch = jax.ShapeDtypeStruct((band, cols * zdim), jnp.float32), vmem, []
        if carries:
            operands.append(pinned)
            in_specs.append(anywhere)
            out_shape, out_specs = (out_shape, jax.ShapeDtypeStruct(pair.shape, pair.dtype)), (vmem, vmem)
            scratch = [pltpu.SemaphoreType.DMA(())]
        if last:
            operands.append(carried)
            in_specs.append(vmem)
            out_shape, out_specs = jax.ShapeDtypeStruct(pair.shape, jnp.bfloat16), anywhere
            scratch = [
                pltpu.VMEM((band * (3 * cols + 1), zdim), jnp.float32),
                pltpu.VMEM(pair.shape, jnp.bfloat16),
                pltpu.SemaphoreType.DMA((band // 32,)),
            ]
        if not small:
            scratch.append(pltpu.VMEM((depth, 256), jnp.bfloat16))
        return pl.pallas_call(
            functools.partial(_band_kernel, masks, total is None, 1.0 / count if scaled else None, last, carries, small),
            in_specs=in_specs,
            out_specs=out_specs,
            out_shape=out_shape,
            scratch_shapes=scratch,
            compiler_params=params,
            cost_estimate=pl.CostEstimate(
                flops=band * cols * zdim, bytes_accessed=band * cols, transcendentals=0
            ),
        )(*operands)

    far_other = _xor(near, 1, n)
    near_other, folded = lax.optimization_barrier((near_other, folded))
    far = _xor(near_other, 1, n)
    total = add([line, partner], (0, 1), None)
    total, carried = add([near, near_other], (8, 9), total, carries=True)
    diagonal, total = lax.optimization_barrier((diagonal, total))
    last = _xor(diagonal, 1, n)
    total = add([diagonal], (6,), total)
    total = add([far, far_other], (10, 11), total, scaled=True)
    return add([last], (7,), total, last=True, scaled=True, carried=carried)


def solution(mesh):
    placed = (P(("group", "row"), None, None), P("group", "row", None)) + (P(),) * 8
    return jax.shard_map(
        functools.partial(shards, mesh.shape["row"]),
        mesh=mesh,
        in_specs=placed,
        out_specs=P("group", "row", None),
        check_vma=False,
    )
```

```python
import functools

import jax
import jax.numpy as jnp
from jax import lax
from jax.experimental import pallas as pl
from jax.experimental.pallas import tpu as pltpu
from jax.sharding import PartitionSpec as P

LANES = 128
CHANS = 32
NT = (((1,), (1,)), ((), ()))


def _stacked(weights, copies):
    c, q = weights.shape
    rows = []
    for k in range(copies):
        left = [jnp.zeros((c, k * q), weights.dtype)] if k else []
        right = [jnp.zeros((c, (copies - 1 - k) * q), weights.dtype)] if k < copies - 1 else []
        rows.append(jnp.concatenate(left + [weights] + right, axis=1))
    return jnp.concatenate(rows, axis=0)


def _order(me, half):
    row = lax.broadcasted_iota(jnp.int32, (4 * LANES, 8 * CHANS), 0)
    col = lax.broadcasted_iota(jnp.int32, (4 * LANES, 8 * CHANS), 1)
    device = (row // LANES) ^ (me // 8 % 4)
    wanted = (row % CHANS) * 8 + ((row // CHANS) % 2) * 4 + device
    hit = (wanted == col) & ((row // (2 * CHANS)) % 2 == half)
    return jnp.where(hit, 1.0, 0.0).astype(jnp.bfloat16)


def _project_kernel(*refs):
    sources, final_source, outs, held = refs[:7], refs[7], refs[8:12], refs[12:19]
    left_ref, right_ref, final_ref, order_ref = outs
    sems = refs[19]
    pieces = 1
    size = held[0].shape[1] // pieces
    at = [(s, pl.ds(k * size, size)) for s in range(2) for k in range(pieces)]
    pairs = [(sources[0].at[i], held[0].at[i]) for i in at]
    pairs += list(zip(sources[1:], held[1:])) + [(final_source, final_ref)]
    copies = [pltpu.make_async_copy(a, b, sems.at[i]) for i, (a, b) in enumerate(pairs)]
    for copy in copies:
        copy.start()
    me = lax.axis_index("row")
    for h in range(2):
        order_ref[h] = _order(me, h)
    for copy in copies[:pieces] + copies[2 * pieces : -1]:
        copy.wait()
    x_ref, gain_ref, bias_ref, w1_ref, b1_ref, w2_ref, b2_ref = held
    half = left_ref.shape[0]
    n = right_ref.shape[0]
    feats = x_ref.shape[2]
    split = []
    for s in range(2):
        if s:
            for copy in copies[pieces : 2 * pieces]:
                copy.wait()
        x = x_ref[s].astype(jnp.float32)
        center = jnp.mean(x, axis=-1, keepdims=True)
        off = x - center
        spread = jnp.mean(off * off, axis=-1, keepdims=True)
        normed = off * lax.rsqrt(spread + 1e-05) * gain_ref[...] + bias_ref[...]
        split.append(normed.reshape(n, 2, 8, feats))
    parts = [split[s][:, jh].reshape(n * 8, feats).astype(jnp.bfloat16) for jh in range(2) for s in range(2)]
    weights = jnp.concatenate([_stacked(w1_ref[...], 4), _stacked(w2_ref[...], 4)], axis=0)
    shifts = jnp.concatenate([b1_ref[...]] * 4 + [b2_ref[...]] * 4, axis=1)
    both = lax.dot_general(jnp.concatenate(parts, axis=1), weights, NT, preferred_element_type=jnp.float32) + shifts
    left_ref[...] = both[:half, :LANES].astype(jnp.bfloat16)
    right_ref[...] = both[:, LANES:].reshape(n, 8, LANES).astype(jnp.bfloat16)
    copies[-1].wait()


def _line_kernel(*refs):
    pieces, order_ref, out_ref = refs[:-2], refs[-2], refs[-1]
    half = pieces[0].shape[0]
    wide = order_ref.shape[2]
    for q in range(len(pieces) // 4):
        lhs = jnp.concatenate([pieces[q * 4 + k][...] for k in (0, 1, 3, 2)], axis=1)
        for h in range(2):
            moved = jnp.dot(lhs, order_ref[h], preferred_element_type=jnp.float32)
            out_ref[pl.ds(h * half, half), pl.ds(q * wide, wide)] = moved.astype(jnp.bfloat16)


def _fold_kernel(right_ref, final_ref, out_ref, block_ref, pairs_ref):
    devices = right_ref.shape[0]
    groups = devices // 4
    block_ref[...] = right_ref[...].astype(jnp.float32).reshape(devices * 8, LANES)
    for jr in range(8):
        for g in range(groups):
            four = block_ref[pl.ds(g * 8 + jr, 4, stride=groups * 8), :]
            for s in range(2):
                pairs_ref[pl.ds((jr * groups + g) * 8 + s * 4, 4), :] = four
    block = pairs_ref[...]
    lane = lax.broadcasted_iota(jnp.int32, block.shape, 1) // CHANS
    s = lax.broadcasted_iota(jnp.int32, block.shape, 0) // 4 % 2
    lhs = [jnp.where(lane == jh * 2 + s, block, 0.0).astype(jnp.bfloat16) for jh in range(2)]
    lhs = jnp.concatenate(lhs, axis=0)

    for pair in range(CHANS // 2):
        rhs = []
        for k in range(2):
            at = pair * 2 * CHANS + k * CHANS
            rhs.append(jnp.concatenate([final_ref[pl.ds(at, CHANS), :]] * 4, axis=0))
        res = jnp.dot(lhs, jnp.concatenate(rhs, axis=1), preferred_element_type=jnp.float32)
        for j in range(16):
            for g in range(groups):
                r = (j * groups + g) * 8
                tile = jnp.concatenate([res[r : r + 8, :LANES], res[r : r + 8, LANES:]], axis=0)
                out_ref[g, 0, pl.ds(pair * 16, 16), pl.ds(j * LANES, LANES)] = tile.astype(jnp.bfloat16)


def _band_kernel(masks, begins, scale, last, carries, held, *refs):
    refs = list(refs)
    take = lambda k: [refs.pop(0) for _ in range(k)]
    lines = take(len(masks))
    (t_ref,) = take(1)
    (sum_ref,) = (None,) if begins else take(1)
    shift_ref = None if scale is None or last else take(1)[0]
    pair_ref = take(1)[0] if last or carries else None
    (out_ref,) = take(1)
    if carries:
        held_pair, pair_sem = take(2)
        fetch = pltpu.make_async_copy(pair_ref, held_pair, pair_sem)
        fetch.start()
    me = lax.axis_index("row")
    wide = t_ref.shape[2]
    first = 2 + me % 2 * 2
    offset = lambda mask: mask if mask < 8 else (first if mask < 10 else 6 - first) ^ (mask % 2)
    chunks = [((me % 8) ^ offset(mask), q ^ (me // 32)) for mask in masks for q in range(t_ref.shape[1])]

    tile = 256 if last or not held else 512
    band = lines[0].shape[0]

    def column(begin):
        at = pl.ds(begin, tile)
        if held:
            rhs = jnp.concatenate([t_ref[g, q, :, at] for g, q in chunks], axis=0)
        else:
            for i, (g, q) in enumerate(chunks):
                pltpu.sync_copy(t_ref.at[g, q, :, at], refs[0].at[pl.ds(i * wide, wide)])
            rhs = refs[0][...]
        lhs = jnp.concatenate([line[...] for line in lines], axis=1)
        res = jnp.dot(lhs, rhs, preferred_element_type=jnp.float32)
        if last:
            return res * scale + sum_ref[:, at]
        if sum_ref is not None:
            res = res + sum_ref[:, at]
        if shift_ref is not None:
            res = res * scale + jnp.concatenate([shift_ref[...]] * (tile // LANES), axis=1)
        return res

    if not last:
        for begin in range(0, t_ref.shape[3], tile):
            out_ref[:, pl.ds(begin, tile)] = column(begin)
        if carries:
            fetch.wait()
        return

    acc_ref, done_ref, sems = take(3)
    cols = pair_ref.shape[1]
    gap = 3
    pitch = gap * cols + 1
    for begin in range(0, t_ref.shape[3], tile):
        res = column(begin)
        for k in range(tile // LANES):
            j = begin // LANES + k
            acc_ref[pl.ds(gap * j, band, stride=pitch), :] = res[:, k * LANES : (k + 1) * LANES]

    chunk = 32

    def finish(r, _):
        for k in range(chunk):
            i = r * chunk + k
            row = k // 8 % 2 * (band // 2) + (r * (chunk // 16) + k // 16) * 8 + k % 8
            total = acc_ref[pl.ds(row * pitch, cols, stride=gap), :]
            done_ref[i] = (pair_ref[i].astype(jnp.float32) + total).astype(jnp.bfloat16)
        at = pl.ds(pl.multiple_of(r * chunk, chunk), chunk)
        pltpu.make_async_copy(done_ref.at[at], out_ref.at[at], sems.at[r]).start()
        return 0

    lax.fori_loop(0, band // chunk, finish, 0)

    def drain(r, _):
        at = pl.ds(pl.multiple_of(r * chunk, chunk), chunk)
        pltpu.make_async_copy(done_ref.at[at], out_ref.at[at], sems.at[r]).wait()
        return 0

    lax.fori_loop(0, band // chunk, drain, 0)


def _xor(x, mask, n):
    return lax.ppermute(x, "row", [(i, i ^ mask) for i in range(n)])


def shards(n, alignment, pair, gain, bias, w1, b1, w2, b2, final, shift):
    seqs, residues, feats = alignment.shape
    band, cols, zdim = pair.shape
    half = band // 2
    count = float(seqs * n)
    small = n <= 32
    params = pltpu.CompilerParams(vmem_limit_bytes=(24 if small else 48) * 1024 * 1024)
    anywhere = pl.BlockSpec(memory_space=pl.ANY)
    vmem = pl.BlockSpec(memory_space=pltpu.VMEM)

    sources = [
        alignment, gain.reshape(1, -1), bias.reshape(1, -1), w1.T, b1.reshape(1, -1), w2.T, b2.reshape(1, -1)
    ]
    sources = [pltpu.with_memory_space_constraint(a, pltpu.HBM) for a in sources]
    left, right, final, order = pl.pallas_call(
        _project_kernel,
        in_specs=[anywhere] * 8,
        out_specs=(vmem,) * 4,
        out_shape=(
            jax.ShapeDtypeStruct((half, LANES), jnp.bfloat16),
            jax.ShapeDtypeStruct((n, 8, LANES), jnp.bfloat16),
            jax.ShapeDtypeStruct(final.shape, final.dtype),
            jax.ShapeDtypeStruct((2, 4 * LANES, 8 * CHANS), jnp.bfloat16),
        ),
        scratch_shapes=[pltpu.VMEM(a.shape, a.dtype) for a in sources] + [pltpu.SemaphoreType.DMA((9,))],
        compiler_params=params,
        cost_estimate=pl.CostEstimate(
            flops=4 * seqs * residues * feats * CHANS, bytes_accessed=2 * seqs * residues * feats, transcendentals=0
        ),
    )(*sources, pltpu.with_memory_space_constraint(final, pltpu.HBM))

    right = lax.all_to_all(right, "row", split_axis=0, concat_axis=0, tiled=True)

    part = 32
    parts = n // part
    pieces = [left] + [_xor(left, m, n) for m in range(8, n, 8)]
    pieces = [pieces[k ^ (k // 2 % 2)] for k in range(len(pieces))]
    line = pl.pallas_call(
        _line_kernel,
        in_specs=[vmem] * (len(pieces) + 1),
        out_specs=vmem,
        out_shape=jax.ShapeDtypeStruct((band, parts * 8 * CHANS), jnp.bfloat16),
        compiler_params=params,
        cost_estimate=pl.CostEstimate(flops=2**27, bytes_accessed=2**20, transcendentals=0),
    )(*pieces, order)
    turn = lambda a, masks: lax.ppermute(a, "row", [(i, i ^ masks[i % 2]) for i in range(n)])
    partner = _xor(line, 1, n)
    near = turn(line, (2, 4))
    near_other = turn(line, (5, 3))

    fold_cost = pl.CostEstimate(
        flops=2 * n * 32 * 256 * CHANS * zdim, bytes_accessed=4 * n * CHANS * cols * zdim, transcendentals=0
    )
    fold_out = jax.ShapeDtypeStruct((8, parts, 8 * CHANS, cols * zdim), jnp.bfloat16)
    if small:
        specs = dict(in_specs=[vmem, vmem], out_specs=vmem)
    else:
        specs = dict(
            grid=(parts,),
            in_specs=[
                pl.BlockSpec((part, 8, LANES), lambda i: (i, 0, 0)),
                pl.BlockSpec(final.shape, lambda i: (0, 0)),
            ],
            out_specs=pl.BlockSpec((8, 1, 8 * CHANS, cols * zdim), lambda i: (0, i, 0, 0)),
        )
    folded = pl.pallas_call(
        _fold_kernel,
        out_shape=fold_out,
        scratch_shapes=[pltpu.VMEM((part * 8, LANES), jnp.float32), pltpu.VMEM((part * 16, LANES), jnp.float32)],
        compiler_params=params,
        cost_estimate=fold_cost,
        **specs,
    )(right, final)

    pinned = pltpu.with_memory_space_constraint(pair, pltpu.HBM)

    def add(lines, masks, total, last=False, scaled=False, carries=False, carried=None):
        depth = len(masks) * parts * 8 * CHANS
        operands = [*lines, folded] + ([] if total is None else [total])
        in_specs = [vmem] * len(operands)
        if not small:
            in_specs[len(lines)] = anywhere
        if scaled and not last:
            operands.append(shift.reshape(1, -1))
            in_specs.append(vmem)
        out_shape, out_specs, scratch = jax.ShapeDtypeStruct((band, cols * zdim), jnp.float32), vmem, []
        if carries:
            operands.append(pinned)
            in_specs.append(anywhere)
            out_shape, out_specs = (out_shape, jax.ShapeDtypeStruct(pair.shape, pair.dtype)), (vmem, vmem)
            scratch = [pltpu.SemaphoreType.DMA(())]
        if last:
            operands.append(carried)
            in_specs.append(vmem)
            out_shape, out_specs = jax.ShapeDtypeStruct(pair.shape, jnp.bfloat16), anywhere
            scratch = [
                pltpu.VMEM((band * (3 * cols + 1), zdim), jnp.float32),
                pltpu.VMEM(pair.shape, jnp.bfloat16),
                pltpu.SemaphoreType.DMA((band // 32,)),
            ]
        if not small:
            scratch.append(pltpu.VMEM((depth, 256), jnp.bfloat16))
        return pl.pallas_call(
            functools.partial(_band_kernel, masks, total is None, 1.0 / count if scaled else None, last, carries, small),
            in_specs=in_specs,
            out_specs=out_specs,
            out_shape=out_shape,
            scratch_shapes=scratch,
            compiler_params=params,
            cost_estimate=pl.CostEstimate(
                flops=band * cols * zdim, bytes_accessed=band * cols, transcendentals=0
            ),
        )(*operands)

    total = add([line, partner], (0, 1), None)
    near, near_other, _ = lax.optimization_barrier((near, near_other, folded))
    diagonal = turn(near, (4, 2))
    far_other, far = _xor(near, 1, n), _xor(near_other, 1, n)
    total, carried = add([near, near_other], (8, 9), total, carries=True)
    total = add([far, far_other], (10, 11), total)
    diagonal, total = lax.optimization_barrier((diagonal, total))
    last = _xor(diagonal, 1, n)
    total = add([diagonal], (6,), total, scaled=True)
    return add([last], (7,), total, last=True, scaled=True, carried=carried)


def solution(mesh):
    placed = (P(("group", "row"), None, None), P("group", "row", None)) + (P(),) * 8
    return jax.shard_map(
        functools.partial(shards, mesh.shape["row"]),
        mesh=mesh,
        in_specs=placed,
        out_specs=P("group", "row", None),
        check_vma=False,
    )
```
